32 devices in a mesh: blk: 32 (over z, y, x, core).
Axes of the slice: x: 2, y: 2, z: 4, core: 2. Of those that a mesh axis runs over, the one named last changes fastest.
Arguments:
- estimate: float32 [32, 110592], P('blk'), may hold values from 0.3 to 1.5
- observed: bfloat16 [32, 6, 110592], P('blk'), may hold values from 0.19921875 to 2
- psf_cells: float32 [32, 6, 4913], P('blk'), may hold values from 0.005 to 1.8, as said below
- tissue: int32 [32], P('blk'), may hold values from 0 to 1, as said below
- neighbours: int32 [32, 6], P('blk'), may hold values from -1 to 31, as said below
- psf_list: int32 [32, 6, 2], P('blk'), may hold values from 0 to 31
- psf_blend: float32 [32, 6, 2], P('blk'), may hold values from 0.1 to 1
- cell_row: int32 [32], replicated, may hold values from 0 to 31, each once
- view_order: int32 [6], replicated, may hold values from 0 to 5, each once
Outputs:
- refined: float32 [32, 110592], P('blk')
The draws below stay inside these ranges and needn't reach their ends.
Inputs may be any that keep to these rules, and one draw needn't show every extreme that they name: Block b sits on device b; blocks 0 to 1 and 16 to 17 are always tissue. With h the top bit of a block's number and r the number without it: bit 3j of r is bit j of the first grid coordinate, bit 3j + 1 of the second, bit 3j + 2 is bit j + 1 of the third, whose lowest bit is h. neighbours[b, f] is the block next to b across face f in that grid if both are tissue, else -1. `cell_row`: each grid cell in exactly one row. `view_order`: each view once; the first 2 entries are used. `psf_cells`: Positive.
All inputs are finite; a program needn't handle non-finite values.
Results may differ from the reference program's by a relative error of at most 0.0003.
Values may be sent and summed in bfloat16 or wider, within the bound.
No kernel may reach another device: no remote copies, remote signals or barrier semaphores. Data moves between devices by JAX's collectives and lax.ppermute only.
A program may use at most 128 MiB of HBM per device.

```python
import jax
import jax.numpy as jnp
from jax import lax

E = 48
MARGIN = 8
VIEWS = 6
BLEND = 2
UPDATES = 2
BLK_DEV = 1
PAD = 64
KS = 17
E3 = 110592
KS3 = 4913
FACE = 18432
NB = 32
PCELLS = 32


def tissue_mask(key):
    numbers = jnp.arange(NB, dtype=jnp.int32)
    coins = jax.random.randint(jax.random.fold_in(key, 11), (NB,), 0, 4)
    alive = (coins > 0).astype(jnp.int32)
    half_count = NB // 2
    keep = (numbers < 2 * BLK_DEV) | (numbers >= half_count) & (numbers < half_count + 2 * BLK_DEV)
    return jnp.where(keep, 1, alive).astype(jnp.int32)


def draw_tissue(key, part):
    return tissue_mask(key)


def draw_neighbours(key, part):
    alive = tissue_mask(key)
    numbers = jnp.arange(NB, dtype=jnp.int32)
    bit_count = NB.bit_length() - 1
    low_count = bit_count - 1
    coords = [jnp.zeros_like(numbers), jnp.zeros_like(numbers), jnp.zeros_like(numbers)]
    extents = [1, 1, 1]
    for bit_place in range(low_count):
        axis_number = bit_place % 3
        coords[axis_number] = coords[axis_number] + numbers // 2 ** bit_place % 2 * 2 ** (bit_place // 3)
        extents[axis_number] = extents[axis_number] * 2
    top_bit = numbers // 2 ** low_count % 2
    coords[2] = 2 * coords[2] + top_bit
    extents[2] = extents[2] * 2
    columns = []
    for face_index in range(6):
        axis_number = face_index // 2
        step_sign = -1 if face_index % 2 == 0 else 1
        moved = list(coords)
        moved[axis_number] = coords[axis_number] + step_sign
        inside = (moved[axis_number] >= 0) & (moved[axis_number] < extents[axis_number])
        safe = [jnp.maximum(moved[0], 0), jnp.maximum(moved[1], 0), jnp.maximum(moved[2], 0)]
        target = safe[2] % 2 * 2 ** low_count
        reduced = [safe[0], safe[1], safe[2] // 2]
        for bit_place in range(low_count):
            axis_other = bit_place % 3
            level = bit_place // 3
            target = target + reduced[axis_other] // 2 ** level % 2 * 2 ** bit_place
        target = jnp.clip(target, 0, NB - 1)
        valid = inside & (alive > 0) & (alive[target] > 0)
        columns.append(jnp.where(valid, target, -1))
    return jnp.stack(columns, axis=1).astype(jnp.int32)


def draw_psf_cells(key, part):
    places = jnp.arange(KS3, dtype=jnp.int32)
    first = (places // (KS * KS) - MARGIN).astype(jnp.float32)
    second = (places // KS % KS - MARGIN).astype(jnp.float32)
    third = (places % KS - MARGIN).astype(jnp.float32)
    radius = first * first + second * second + third * third
    widths = jax.random.uniform(jax.random.fold_in(key, 21), (PCELLS, VIEWS, 1), jnp.float32, 1.0, 0.6 * MARGIN + 1.0)
    rough = jax.random.uniform(jax.random.fold_in(key, 23), (PCELLS, VIEWS, KS3), jnp.float32, 0.6, 1.4)
    shape_part = jnp.exp(-radius[None, None, :] / (2.0 * widths * widths)) + 0.02
    return (shape_part * rough).astype(jnp.float32)


def with_ends(entries, rng, least, top_value):
    longest = entries.shape.index(max(entries.shape))
    spots = []
    for shift in (0, 1):
        where = [jax.random.randint(jax.random.fold_in(rng, axis), (), 0, length) for axis, length in enumerate(entries.shape)]
        where[longest] = (where[longest] + shift) % entries.shape[longest]
        spots.append(tuple(where))
    return entries.at[spots[0]].set(least).at[spots[1]].set(top_value)


def levels(stream_key, dims, shards, least, largest):
    def one(axis_at, blocks):
        draws = jax.random.uniform(jax.random.fold_in(jax.random.fold_in(stream_key, 6), axis_at), (blocks,), jnp.float32, least / len(shards), largest / len(shards))
        return jnp.repeat(jnp.exp(draws), dims[axis_at] // blocks).reshape((-1,) + (1,) * (len(dims) - axis_at - 1))

    level = one(*shards[0])
    for cut in shards[1:]:
        level = level * one(*cut)
    return level


def setup_inputs(seed: int = 0) -> dict:
    splits = jax.random.split(jax.random.key(seed), 10)
    return {
        "estimate": jnp.clip(0.3 + 1.2 * jax.random.uniform(splits[0], (NB, E3), jnp.float32) ** levels(splits[0], (NB, E3), ((0, 32),), -0.2, 0.2), 0.3, 1.5),
        "observed": jnp.clip(0.19921875 + 1.8007812 * jax.random.uniform(splits[1], (NB, VIEWS, E3), jnp.float32) ** levels(splits[1], (NB, VIEWS, E3), ((0, 32),), -0.2, 0.2), 0.19921875, 2.0).astype(jnp.bfloat16),
        "psf_cells": draw_psf_cells(jax.random.fold_in(splits[9], 71), 0),
        "tissue": draw_tissue(jax.random.fold_in(splits[9], 71), 0),
        "neighbours": draw_neighbours(jax.random.fold_in(splits[9], 71), 0),
        "psf_list": with_ends(jax.random.randint(splits[5], (NB, VIEWS, BLEND), 0, PCELLS), jax.random.fold_in(splits[5], 1), 0, PCELLS - 1).astype(jnp.int32),
        "psf_blend": jnp.clip(0.1 + 0.9 * jax.random.uniform(splits[6], (NB, VIEWS, BLEND), jnp.float32) ** levels(splits[6], (NB, VIEWS, BLEND), ((0, 32),), -0.2, 0.2), 0.1, 1.0),
        "cell_row": jax.random.permutation(splits[7], PCELLS).astype(jnp.int32),
        "view_order": jax.random.permutation(splits[8], VIEWS).astype(jnp.int32),
    }


def side_slab(volume, face_index):
    axis_number = volume.ndim - 3 + face_index // 2
    start_now = 0 if face_index % 2 == 0 else E - MARGIN
    return lax.slice_in_dim(volume, start_now, start_now + MARGIN, axis=axis_number)


def assemble(core_block, margin_rows):
    padded = jnp.zeros((PAD, PAD, PAD), jnp.float32)
    padded = padded.at[MARGIN:MARGIN + E, MARGIN:MARGIN + E, MARGIN:MARGIN + E].set(core_block)
    for face_index in range(6):
        axis_number = face_index // 2
        shape_now = [E, E, E]
        shape_now[axis_number] = MARGIN
        slab_now = margin_rows[face_index].astype(jnp.float32).reshape(shape_now)
        start_now = [MARGIN, MARGIN, MARGIN]
        start_now[axis_number] = 0 if face_index % 2 == 0 else MARGIN + E
        padded = lax.dynamic_update_slice(padded, slab_now, start_now)
    return padded


def place_kernel(kernel):
    grid_cube = jnp.zeros((PAD, PAD, PAD), jnp.float32)
    grid_cube = grid_cube.at[0:KS, 0:KS, 0:KS].set(kernel.reshape(KS, KS, KS))
    return jnp.roll(grid_cube, (-MARGIN, -MARGIN, -MARGIN), axis=(0, 1, 2))


def refine(core_block, margin_rows, kernel, observed_block):
    padded = assemble(core_block, margin_rows)
    spectrum = jnp.fft.fftn(place_kernel(kernel))
    blurred = jnp.real(jnp.fft.ifftn(jnp.fft.fftn(padded) * spectrum))
    blurred = blurred[MARGIN:MARGIN + E, MARGIN:MARGIN + E, MARGIN:MARGIN + E]
    quotient = observed_block.astype(jnp.float32) / blurred
    holder = jnp.zeros((PAD, PAD, PAD), jnp.float32)
    holder = holder.at[MARGIN:MARGIN + E, MARGIN:MARGIN + E, MARGIN:MARGIN + E].set(quotient)
    correction = jnp.real(jnp.fft.ifftn(jnp.fft.fftn(holder) * jnp.conj(spectrum)))
    correction = correction[MARGIN:MARGIN + E, MARGIN:MARGIN + E, MARGIN:MARGIN + E]
    return core_block * correction


def reference(estimate, observed, psf_cells, tissue, neighbours, psf_list, psf_blend, cell_row, view_order):
    current = estimate.reshape(NB, E, E, E)
    opposite = jnp.array([1, 0, 3, 2, 5, 4], jnp.int32)
    for update in range(UPDATES):
        view_now = view_order[update]
        cells_now = lax.dynamic_index_in_dim(psf_cells, view_now, 1, keepdims=False)
        scaled = cells_now / jnp.sum(cells_now, axis=1, keepdims=True)
        listed = lax.dynamic_index_in_dim(psf_list, view_now, 1, keepdims=False)
        cell_rows = cell_row[listed]
        weights = lax.dynamic_index_in_dim(psf_blend, view_now, 1, keepdims=False)
        weights = weights / jnp.sum(weights, axis=1, keepdims=True)
        kernels = jnp.sum(weights[:, :, None] * scaled[cell_rows], axis=1)
        side_slabs = jnp.stack([side_slab(current, face_index).reshape(NB, FACE) for face_index in range(6)], axis=1)
        side_slabs = lax.optimization_barrier(side_slabs.astype(jnp.bfloat16))
        margins = side_slabs[jnp.maximum(neighbours, 0), opposite[None, :]]
        margins = jnp.where((neighbours >= 0)[:, :, None], margins, jnp.zeros_like(margins))
        seen_now = lax.dynamic_index_in_dim(observed, view_now, 1, keepdims=False)

        def one_block(items):
            core_block, margin_rows, kernel, observed_row, alive = items
            refined = refine(core_block, margin_rows, kernel, observed_row.reshape(E, E, E))
            return jnp.where(alive > 0, refined, core_block)

        current = lax.map(one_block, (current, margins, kernels, seen_now, tissue))
    return current.reshape(NB, E3)
```

```python
import numpy as np

import jax
import jax.numpy as jnp
import ml_dtypes
from jax import lax
from jax.experimental import pallas as pl
from jax.experimental.pallas import tpu as pltpu
from jax.sharding import PartitionSpec as P

E = 48
MARGIN = 8
UPDATES = 2
PAD = 64
KS = 17
KS2 = KS * KS
KS3 = 4913
SLOTS = 16
LANES = 256
TAPROWS = 32
CELLPAD = 5120
FLAT = 864

F32 = jnp.float32
BF16 = jnp.bfloat16


def two_terms(table):
    high = table.astype(ml_dtypes.bfloat16)
    low = (table - high.astype(np.float64)).astype(ml_dtypes.bfloat16)
    return high, low


def stacked(table, axis):
    high, low = two_terms(table)
    return np.concatenate([high, high, low], axis=axis)


def x_positions():
    x = np.arange(PAD)
    return np.where(x < PAD - MARGIN, x, x - PAD)


def table_space_to_lines():
    z4, k4, kx = np.arange(4), np.arange(4), np.arange(32)
    angle = -2.0 * np.pi * (
        z4[:, None, None, None] * k4[None, None, :, None] / 4.0
        + (kx[None, None, None, :] + 0.5) * x_positions()[None, :, None, None] / PAD
    )
    angle = angle.reshape(LANES, 128)
    return np.concatenate([np.cos(angle), np.sin(angle)], axis=1)


def table_lines_to_space():
    back = table_space_to_lines().T.copy()
    back = back.reshape(LANES, 4, PAD)
    back[:, 3, :] = 0.0
    back[:, :, E:] = 0.0
    return back.reshape(LANES, LANES)


def complex_rows(angle):
    cosine, sine = np.cos(angle), np.sin(angle)
    return np.concatenate(
        [np.concatenate([cosine, -sine], axis=1), np.concatenate([sine, cosine], axis=1)], axis=0
    )


def table_y(count):
    ky, y = np.arange(PAD), np.arange(count)
    return complex_rows(-2.0 * np.pi * (ky[:, None] * y[None, :] % PAD) / PAD)


def table_y_back():
    ky, y = np.arange(PAD), np.arange(E)
    return complex_rows(2.0 * np.pi * (y[:, None] * ky[None, :] % PAD) / PAD)


def table_y_taps():
    ky, tap = np.arange(PAD), np.arange(TAPROWS) - MARGIN
    angle = -2.0 * np.pi * ky[:, None] * tap[None, :] / PAD
    return complex_rows(angle)


def table_taps(z4):
    k4, kx = np.arange(4), np.arange(32)
    tap_x = np.arange(384) % KS - MARGIN
    angle = -2.0 * np.pi * (
        z4 * k4[None, :, None] / 4.0 + (kx[None, None, :] + 0.5) * tap_x[:, None, None] / PAD
    )
    angle = angle.reshape(384, 128)
    table = np.concatenate([np.cos(angle), np.sin(angle)], axis=1)
    table[KS2:] = 0.0
    return table


def table_tap_mask():
    place = np.arange(384)
    return (place[None, :] // KS == np.arange(TAPROWS)[:, None]).astype(np.float32) * (
        place[None, :] < KS2
    )


def table_twiddle():
    k4 = np.repeat(np.arange(4), 32)
    angle = -2.0 * np.pi * np.arange(SLOTS)[:, None] * k4[None, :] / PAD
    both = np.stack([np.cos(angle), np.sin(angle)], axis=0)
    return np.broadcast_to(both[:, :, None, :], (2, SLOTS, 8, 128)).astype(np.float32)


def table_pack_x():
    table = np.zeros((4, 4, PAD, 2, 4, 4, MARGIN), np.float32)
    for group in range(4):
        for z4 in range(3):
            for step in range(MARGIN):
                table[group, z4, step, 0, group, z4, step] = 1.0
                table[group, z4, E - MARGIN + step, 1, group, z4, step] = 1.0
    return table.reshape(4 * LANES, LANES).astype(ml_dtypes.bfloat16)


def table_unpack_x():
    table = np.zeros((2, 4, 4, MARGIN, 4, 4, PAD), np.float32)
    for group in range(4):
        for z4 in range(3):
            for step in range(MARGIN):
                table[0, group, z4, step, group, z4, PAD - MARGIN + step] = 1.0
                table[1, group, z4, step, group, z4, E + step] = 1.0
    return table.reshape(LANES, 4 * LANES).astype(ml_dtypes.bfloat16)


def split(value):
    high = value.astype(BF16)
    low = (value - high.astype(F32)).astype(BF16)
    return high, low


def dot(left, right):
    return jnp.dot(left, right, preferred_element_type=F32)


def both_halves(rows_ref, rows):
    return jnp.concatenate([rows_ref[0, rows, :], rows_ref[1, rows, :]], axis=1)


def lane_iota(shape):
    return lax.broadcasted_iota(jnp.int32, shape, 1)


def cut(pieces, piece, target):
    offset = E * piece
    first, start = offset // 128, offset % 128
    shift = (target - start) % 128
    one = pltpu.roll(pieces[first], shift, 1) if shift else pieces[first]
    if start + E <= 128:
        return one
    two = pltpu.roll(pieces[first + 1], shift, 1) if shift else pieces[first + 1]
    edge = target + 128 - start
    return jnp.where(lane_iota(one.shape) < edge, one, two)


def unflatten(flat_ref, out_ref):
    lane = lane_iota((8, 128))
    zero = jnp.zeros((8, 128), F32)
    for block in range(12):
        parts = []
        for z4 in range(3):
            first = 3 * (96 * z4 + 8 * block)
            parts.append([flat_ref[pl.ds(first + m, 8, stride=3), :] for m in range(3)])
        for piece in range(8):
            low = cut(parts[0], piece, 0)
            mid = cut(parts[1], piece, 64)
            top = cut(parts[2], piece, 0)
            left = jnp.where(lane < E, low, jnp.where(lane < 64, zero, mid))
            left = jnp.where(lane < 64 + E, left, zero)
            rows = pl.ds(64 * block + piece, 8, stride=8)
            out_ref[0, rows, :] = left
            out_ref[1, rows, :] = jnp.where(lane < E, top, zero)


def flatten(rows_ref, flat_ref):
    lane = lane_iota((8, 128))
    for block in range(12):
        found = []
        for piece in range(8):
            rows = pl.ds(64 * block + piece, 8, stride=8)
            found.append((rows_ref[0, rows, :], rows_ref[1, rows, :]))
        for z4 in range(3):
            first = 3 * (96 * z4 + 8 * block)
            out = [None, None, None]
            for piece in range(8):
                value = found[piece][0] if z4 < 2 else found[piece][1]
                source = 64 if z4 == 1 else 0
                offset = E * piece
                spot, start = offset // 128, offset % 128
                shift = (start - source) % 128
                moved = pltpu.roll(value, shift, 1) if shift else value
                if out[spot] is None:
                    out[spot] = moved
                else:
                    out[spot] = jnp.where(lane < start, out[spot], moved)
                if start + E > 128:
                    out[spot + 1] = moved
            for m in range(3):
                flat_ref[pl.ds(first + m, 8, stride=3), :] = out[m]


def pack_slabs(rows_ref, pack_x, x0, x1, y0, y1, z0, z1):
    high = both_halves(rows_ref, slice(None)).astype(BF16)
    wide = jnp.concatenate([high[192 * g : 192 * (g + 1)] for g in range(4)], axis=1)
    both = dot(wide, pack_x[...]).astype(BF16)
    x0[...] = both[:, 0:128]
    x1[...] = both[:, 128:256]
    low_rows, high_rows = [], []
    for slot in range(SLOTS):
        low_rows.append(both_halves(rows_ref, slice(E * slot, E * slot + MARGIN)))
        high_rows.append(both_halves(rows_ref, slice(E * slot + E - MARGIN, E * (slot + 1))))
    y0[...] = jnp.concatenate(low_rows, axis=0).astype(BF16)
    y1[...] = jnp.concatenate(high_rows, axis=0).astype(BF16)
    lane = lane_iota((192, 128))
    first = rows_ref[0, 0:192, :]
    second = pltpu.roll(rows_ref[0, 192:384, :], 64, 1)
    z0[...] = jnp.where(lane < 64, first, second).astype(BF16)
    first = rows_ref[1, 384:576, :]
    second = pltpu.roll(rows_ref[1, 576:768, :], 64, 1)
    z1[...] = jnp.where(lane < 64, first, second).astype(BF16)


def assemble(present, rows_ref, unpack_x, margins, high_ref, low_ref):
    zm, zp, ym, yp, xm, xp = margins
    on = [present[0, face] >= 0 for face in range(6)]
    zero_x = jnp.zeros((192, 128), BF16)
    wide = jnp.concatenate(
        [jnp.where(on[4], xm[...], zero_x), jnp.where(on[5], xp[...], zero_x)], axis=1
    )
    side = dot(wide, unpack_x[...])
    scale = [jnp.where(on[face], 1.0, 0.0).astype(F32) for face in range(6)]
    yp_rows = yp[...].astype(F32) * scale[3]
    ym_rows = ym[...].astype(F32) * scale[2]
    z_sides = []
    for ref, face in ((zp, 1), (zm, 0)):
        value = ref[...].astype(F32) * scale[face]
        z_sides.append(pltpu.roll(value, 64, 1))
        z_sides.append(value)
    lane = lane_iota((E, 128))
    for slot in range(SLOTS):
        group, inner = slot // 4, slot % 4
        core = both_halves(rows_ref, slice(E * slot, E * (slot + 1)))
        high, low = split(core)
        added = side[E * inner : E * (inner + 1), LANES * group : LANES * (group + 1)]
        full = high.astype(F32) + added
        z_side = z_sides[group][E * inner : E * (inner + 1), :]
        right = jnp.where(lane < 64, full[:, 128:256], z_side)
        high_ref[PAD * slot : PAD * slot + E, 0:128] = full[:, 0:128].astype(BF16)
        high_ref[PAD * slot : PAD * slot + E, 128:256] = right.astype(BF16)
        rows = slice(MARGIN * slot, MARGIN * (slot + 1))
        outer = jnp.concatenate([yp_rows[rows], ym_rows[rows]], axis=0)
        high_ref[PAD * slot + E : PAD * (slot + 1), :] = outer.astype(BF16)
        low_ref[PAD * slot : PAD * slot + E, :] = low
        low_ref[PAD * slot + E : PAD * (slot + 1), :] = jnp.zeros((PAD - E, LANES), BF16)


def lines_stage(high, low, table, out_ref, rows, step):
    for start in range(0, rows, step):
        part = slice(start, start + step)
        wide = jnp.concatenate([high[part, :], low[part, :], high[part, :]], axis=1)
        out_ref[part, :] = dot(wide, table[...])


def y_stage(lines_ref, table, count, out_ref):
    for pair in range(SLOTS // 2):
        one = lines_ref[count * 2 * pair : count * (2 * pair + 1), :]
        two = lines_ref[count * (2 * pair + 1) : count * (2 * pair + 2), :]
        real = jnp.concatenate([one[:, 0:128], two[:, 0:128]], axis=1)
        imag = jnp.concatenate([one[:, 128:256], two[:, 128:256]], axis=1)
        high, low = split(jnp.concatenate([real, imag], axis=0))
        out = dot(table[...], jnp.concatenate([high, low, high], axis=0))
        out_ref[2 * pair] = out[:, 0:128]
        out_ref[2 * pair + 1] = out[:, 128:256]


def y_back_stage(planes_ref, table, out_ref):
    for pair in range(SLOTS // 2):
        both = jnp.concatenate([planes_ref[2 * pair], planes_ref[2 * pair + 1]], axis=1)
        high, low = split(both)
        out = dot(table[...], jnp.concatenate([high, low, high], axis=0))
        for which in range(2):
            rows = slice(E * (2 * pair + which), E * (2 * pair + which + 1))
            lanes = slice(128 * which, 128 * (which + 1))
            out_ref[rows, 0:128] = out[0:E, lanes]
            out_ref[rows, 128:256] = out[E : 2 * E, lanes]


def turn(value, cosine, sine):
    real, imag = value
    return real * cosine - imag * sine, real * sine + imag * cosine


def dft4(values, sign):
    (ar, ai), (br, bi), (cr, ci), (dr, di) = values
    sr, si, mr, mi = ar + cr, ai + ci, ar - cr, ai - ci
    pr, pi, qr, qi = br + dr, bi + di, br - dr, bi - di
    if sign > 0:
        first, third = (mr - qi, mi + qr), (mr + qi, mi - qr)
    else:
        first, third = (mr + qi, mi - qr), (mr - qi, mi + qr)
    return [(sr + pr, si + pi), first, (sr - pr, si - pi), third]


def dft16(values, sign):
    inner = []
    for low in range(4):
        line = dft4([values[4 * top + low] for top in range(4)], sign)
        moved = []
        for k in range(4):
            turns = low * k
            real, imag = line[k]
            if turns == 0:
                moved.append((real, imag))
            elif turns == 4:
                moved.append((-imag, real) if sign > 0 else (imag, -real))
            elif turns in (2, 6):
                root = float(np.sqrt(0.5))
                a, b = root * real, root * imag
                if turns == 2:
                    moved.append((a - b, a + b) if sign > 0 else (a + b, b - a))
                else:
                    moved.append((-a - b, a - b) if sign > 0 else (b - a, -a - b))
            else:
                angle = sign * 2.0 * np.pi * turns / SLOTS
                moved.append(turn((real, imag), float(np.cos(angle)), float(np.sin(angle))))
        inner.append(moved)
    out = [None] * SLOTS
    for k in range(4):
        line = dft4([inner[low][k] for low in range(4)], sign)
        for top in range(4):
            out[k + 4 * top] = line[top]
    return out


def z_forward(planes_ref, twiddle, rows, rows_imag):
    values = []
    for slot in range(SLOTS):
        value = (planes_ref[slot, rows, :], planes_ref[slot, rows_imag, :])
        if slot:
            value = turn(value, twiddle[0, slot], twiddle[1, slot])
        values.append(value)
    return dft16(values, -1)


def z_stage(planes_ref, twiddle, out_ref):
    @pl.loop(0, PAD // 8)
    def _(step):
        rows = pl.ds(pl.multiple_of(8 * step, 8), 8)
        rows_imag = pl.ds(pl.multiple_of(8 * step + PAD, 8), 8)
        values = z_forward(planes_ref, twiddle, rows, rows_imag)
        for slot in range(SLOTS):
            out_ref[slot, rows, :] = values[slot][0]
            out_ref[slot, rows_imag, :] = values[slot][1]


def filter_stage(planes_ref, kernel_ref, twiddle, conjugate, out_ref):
    @pl.loop(0, PAD // 8)
    def _(step):
        rows = pl.ds(pl.multiple_of(8 * step, 8), 8)
        rows_imag = pl.ds(pl.multiple_of(8 * step + PAD, 8), 8)
        values = z_forward(planes_ref, twiddle, rows, rows_imag)
        for slot in range(SLOTS):
            cosine, sine = kernel_ref[slot, rows, :], kernel_ref[slot, rows_imag, :]
            if conjugate:
                real, imag = values[slot]
                values[slot] = (real * cosine + imag * sine, imag * cosine - real * sine)
            else:
                values[slot] = turn(values[slot], cosine, sine)
        values = dft16(values, 1)
        for slot in range(SLOTS):
            real, imag = values[slot]
            if slot:
                cosine, sine = twiddle[0, slot], twiddle[1, slot]
                real, imag = real * cosine + imag * sine, imag * cosine - real * sine
            out_ref[slot, rows, :] = real
            out_ref[slot, rows_imag, :] = imag


def tap_stage(flat, mask, table0, table3, table_y_ref, planes_ref):
    lines = []
    for tap in range(KS):
        offset = KS2 * tap
        start = offset // 128 * 128
        shift = offset - start
        window = flat[:, start : start + 512]
        if shift:
            window = pltpu.roll(window, 512 - shift, 1)
        lines.append(window[:, 0:384])
    spread = []
    for line in lines:
        spread.append(jnp.broadcast_to(line, (TAPROWS, 384)) * mask)

    def first_stage(taps, table):
        high, low = split(jnp.concatenate(taps, axis=0))
        return dot(jnp.concatenate([high, low, high], axis=1), table[...])

    ahead = first_stage(spread[MARGIN:], table0)
    behind = first_stage(spread[:MARGIN], table3)
    slots = []
    for slot in range(MARGIN):
        slots.append(ahead[TAPROWS * slot : TAPROWS * (slot + 1)])
    slots.append(ahead[TAPROWS * MARGIN :] + behind[0:TAPROWS])
    for slot in range(MARGIN + 1, SLOTS):
        at = slot - MARGIN
        slots.append(behind[TAPROWS * at : TAPROWS * (at + 1)])
    for pair in range(SLOTS // 2):
        one, two = slots[2 * pair], slots[2 * pair + 1]
        real = jnp.concatenate([one[:, 0:128], two[:, 0:128]], axis=1)
        imag = jnp.concatenate([one[:, 128:256], two[:, 128:256]], axis=1)
        high, low = split(jnp.concatenate([real, imag], axis=0))
        out = dot(table_y_ref[...], jnp.concatenate([high, low, high], axis=0))
        planes_ref[2 * pair] = out[:, 0:128]
        planes_ref[2 * pair + 1] = out[:, 128:256]


def spectrum_body(update, order, lists, blend, cell_row, cells, mask, table0, table3, table_y_ref, twiddle, out_ref, got, planes, sems):
    view = order[update]
    copies = []
    for k in range(2):
        row = cell_row[lists[0, view, k]]
        copy = pltpu.make_async_copy(cells.at[row], got.at[k], sems.at[k])
        copy.start()
        copies.append(copy)
    for copy in copies:
        copy.wait()
    total = blend[0, view, 0] + blend[0, view, 1]
    flat = None
    for k in range(2):
        line = got[k].astype(F32)[update : update + 1, :]
        weight = blend[0, view, k] / total * (2.0 / float(PAD**3))
        part = line * (weight / jnp.sum(line, axis=1, keepdims=True))
        flat = part if flat is None else flat + part
    tap_stage(flat, mask[...], table0, table3, table_y_ref, planes)
    z_stage(planes, twiddle, out_ref)


def prep_kernel(est, obs0, obs1, pack_x, u_out, o0_out, o1_out, z0, z1, y0, y1, x0, x1):
    unflatten(est, u_out)
    pack_slabs(u_out, pack_x, x0, x1, y0, y1, z0, z1)
    unflatten(obs0, o0_out)
    unflatten(obs1, o1_out)


def field_kernel(present, u, zm, zp, ym, yp, xm, xp, unpack_x, ea, gy, out, high, low, lines):
    assemble(present, u, unpack_x, (zm, zp, ym, yp, xm, xp), high, low)
    lines_stage(high, low, ea, lines, SLOTS * PAD, 256)
    y_stage(lines, gy, PAD, out)


def update_body(tissue, planes, kernel, u, o, tables, scratch, new_ref):
    ea, ei, gh, gb, twiddle = tables
    planes2, lines = scratch
    filter_stage(planes, kernel, twiddle, False, planes2)
    y_back_stage(planes2, gb, lines)
    rows = SLOTS * E
    lane = lane_iota((rows, LANES))
    valid = (lane % PAD < E) & (lane < 3 * PAD)
    high, low = split(lines[...])
    blurred = dot(jnp.concatenate([high, low, high], axis=1), ei[...])
    quotient = jnp.where(valid, both_halves(o, slice(None)) / blurred, 0.0)
    high, low = split(quotient)
    lines[...] = dot(jnp.concatenate([high, low, high], axis=1), ea[...])
    y_stage(lines, gh, E, planes2)
    filter_stage(planes2, kernel, twiddle, True, planes2)
    y_back_stage(planes2, gb, lines)
    high, low = split(lines[...])
    correction = dot(jnp.concatenate([high, low, high], axis=1), ei[...])
    alive = tissue[0] > 0
    for half in range(2):
        core = u[half]
        new_ref[half] = jnp.where(alive, core * correction[:, 128 * half : 128 * (half + 1)], core)


def spectrum_kernel(update, *refs):
    spectrum_body(update, *refs)


def first_kernel(tissue, planes, kernel, u, o, ea, ei, gh, gb, twiddle, pack_x, u_out, z0, z1, y0, y1, x0, x1, planes2, lines):
    update_body(tissue, planes, kernel, u, o, (ea, ei, gh, gb, twiddle), (planes2, lines), u_out)
    pack_slabs(u_out, pack_x, x0, x1, y0, y1, z0, z1)


def last_kernel(tissue, planes, kernel, u, o, ea, ei, gh, gb, twiddle, out, planes2, lines, fresh):
    update_body(tissue, planes, kernel, u, o, (ea, ei, gh, gb, twiddle), (planes2, lines), fresh)
    flatten(fresh, out)


VM = pl.BlockSpec(memory_space=pltpu.VMEM)
SM = pl.BlockSpec(memory_space=pltpu.SMEM)
ANY = pl.BlockSpec(memory_space=pl.ANY)
PARAMS = pltpu.CompilerParams(vmem_limit_bytes=48 * 1024 * 1024)


def shape(dims, kind=F32):
    return jax.ShapeDtypeStruct(dims, kind)


SLABS = [shape((192, 128), BF16)] * 2 + [shape((128, 256), BF16)] * 2 + [shape((192, 128), BF16)] * 2
ROWS = shape((2, SLOTS * E, 128))
ROWS_V = pltpu.VMEM((2, SLOTS * E, 128), F32)
PLANES = shape((SLOTS, 128, 128))
PLANES_V = pltpu.VMEM((SLOTS, 128, 128), F32)
LINES_V = pltpu.VMEM((SLOTS * E, LANES), F32)


def call(body, ins, outs, args, scratch=(), name=None):
    many = isinstance(outs, list)
    return pl.pallas_call(
        body,
        in_specs=ins,
        out_specs=[VM] * len(outs) if many else VM,
        out_shape=outs,
        scratch_shapes=list(scratch),
        compiler_params=PARAMS,
        name=name,
    )(*args)


def neighbour_pairs(count):
    low_count = count.bit_length() - 2
    places = []
    for number in range(count):
        at = [0, 0, 0]
        for bit in range(low_count):
            at[bit % 3] += number // 2**bit % 2 * 2 ** (bit // 3)
        at[2] = 2 * at[2] + number // 2**low_count % 2
        places.append(tuple(at))
    number_at = {at: number for number, at in enumerate(places)}
    pairs = []
    for face in range(6):
        axis, step = face // 2, -1 if face % 2 == 0 else 1
        found = []
        for number, at in enumerate(places):
            moved = list(at)
            moved[axis] += step
            if tuple(moved) in number_at:
                found.append((number_at[tuple(moved)], number))
        pairs.append(found)
    return pairs


def exchange(slabs, pairs):
    out = []
    for face in range(6):
        sent = slabs[face ^ 1]
        out.append(lax.ppermute(sent, "blk", pairs[face]) if pairs[face] else jnp.zeros_like(sent))
    return out


def local(estimate, observed, psf_cells, tissue, neighbours, psf_list, psf_blend, cell_row, view_order):
    count = lax.axis_size("blk")
    pairs = neighbour_pairs(count)
    ea = jnp.asarray(stacked(table_space_to_lines(), 0))
    ei = jnp.asarray(stacked(table_lines_to_space(), 0))
    gy = jnp.asarray(stacked(table_y(PAD), 1))
    gh = jnp.asarray(stacked(table_y(E), 1))
    gb = jnp.asarray(stacked(table_y_back(), 1))
    gt = jnp.asarray(stacked(table_y_taps(), 1))
    taps0 = jnp.asarray(stacked(table_taps(0), 0))
    taps3 = jnp.asarray(stacked(table_taps(3), 0))
    mask = jnp.asarray(table_tap_mask().astype(np.float32))
    twiddle = jnp.asarray(table_twiddle())
    pack_x = jnp.asarray(table_pack_x())
    unpack_x = jnp.asarray(table_unpack_x())

    views = jnp.concatenate(
        [lax.dynamic_slice_in_dim(psf_cells[0], view_order[u], 1, 0) for u in range(UPDATES)], axis=0
    )
    views = jnp.pad(views.astype(BF16), ((0, 0), (0, CELLPAD - KS3)))
    cells = lax.all_gather(views, "blk", axis=0, tiled=False)

    seen = [
        lax.dynamic_index_in_dim(observed[0], view_order[u], 0, keepdims=False).astype(F32).reshape(FLAT, 128)
        for u in range(UPDATES)
    ]
    flat = estimate.reshape(FLAT, 128)
    prep = call(
        prep_kernel, [VM] * 4, [ROWS, ROWS, ROWS] + SLABS, (flat, seen[0], seen[1], pack_x), name="prep"
    )
    rows, targets, slabs = prep[0], prep[1:3], prep[3:]

    def spectrum(update):
        return call(
            lambda *refs: spectrum_kernel(update, *refs),
            [SM] * 4 + [ANY] + [VM] * 5,
            PLANES,
            (view_order, psf_list, psf_blend, cell_row, cells, mask, taps0, taps3, gt, twiddle),
            [pltpu.VMEM((2, 2, CELLPAD), BF16), PLANES_V, pltpu.SemaphoreType.DMA((2,))],
            name="spectrum",
        )

    def field(rows, margins):
        return call(
            field_kernel,
            [SM] + [VM] * 10,
            PLANES,
            (neighbours, rows, *margins, unpack_x, ea, gy),
            [pltpu.VMEM((SLOTS * PAD, LANES), BF16)] * 2 + [pltpu.VMEM((SLOTS * PAD, LANES), F32)],
            name="field",
        )

    margins = exchange(slabs, pairs)
    planes = field(rows, margins)
    kernel = spectrum(0)
    first = call(
        first_kernel,
        [SM] + [VM] * 10,
        [ROWS] + SLABS,
        (tissue, planes, kernel, rows, targets[0], ea, ei, gh, gb, twiddle, pack_x),
        [PLANES_V, LINES_V],
        name="first",
    )
    rows, slabs = first[0], first[1:]
    margins = exchange(slabs, pairs)
    kernel = spectrum(1)
    planes = field(rows, margins)
    out = call(
        last_kernel,
        [SM] + [VM] * 9,
        shape((FLAT, 128)),
        (tissue, planes, kernel, rows, targets[1], ea, ei, gh, gb, twiddle),
        [PLANES_V, LINES_V, ROWS_V],
        name="last",
    )
    return out.reshape(1, FLAT * 128)


def solution(mesh):
    return jax.shard_map(
        local,
        mesh=mesh,
        in_specs=(
            P("blk", None),
            P("blk", None, None),
            P("blk", None, None),
            P("blk"),
            P("blk", None),
            P("blk", None, None),
            P("blk", None, None),
            P(),
            P(),
        ),
        out_specs=P("blk", None),
        check_vma=False,
    )
```

```python
import functools

import numpy as np

import jax
import jax.numpy as jnp
import ml_dtypes
from jax import lax
from jax.experimental import pallas as pl
from jax.experimental.pallas import tpu as pltpu
from jax.sharding import PartitionSpec as P

E = 48
MARGIN = 8
UPDATES = 2
VIEWS = 6
PAD = 64
KS = 17
KS2 = KS * KS
KS3 = 4913
SLOTS = 16
LANES = 256
TAPS = 24
CELLROWS = 40
FLAT = 864

F32 = jnp.float32
BF16 = jnp.bfloat16


def two_terms(table):
    high = table.astype(ml_dtypes.bfloat16)
    low = (table - high.astype(np.float64)).astype(ml_dtypes.bfloat16)
    return high, low


def stacked(table, axis):
    high, low = two_terms(table)
    return np.concatenate([high, high, low], axis=axis)


def x_positions():
    x = np.arange(PAD)
    return np.where(x < PAD - MARGIN, x, x - PAD)


def table_space_to_lines():
    z4, k4, kx = np.arange(4), np.arange(4), np.arange(32)
    angle = -2.0 * np.pi * (
        z4[:, None, None, None] * k4[None, None, :, None] / 4.0
        + (kx[None, None, None, :] + 0.5) * x_positions()[None, :, None, None] / PAD
    )
    angle = angle.reshape(LANES, 128)
    return np.concatenate([np.cos(angle), np.sin(angle)], axis=1)


def table_lines_to_space():
    back = table_space_to_lines().T.copy()
    back = back.reshape(LANES, 4, PAD)
    back[:, 3, :] = 0.0
    back[:, :, E:] = 0.0
    return back.reshape(LANES, LANES)


def complex_rows(angle):
    cosine, sine = np.cos(angle), np.sin(angle)
    return np.concatenate(
        [np.concatenate([cosine, -sine], axis=1), np.concatenate([sine, cosine], axis=1)], axis=0
    )


def table_y(count):
    ky, y = np.arange(PAD), np.arange(count)
    return complex_rows(-2.0 * np.pi * (ky[:, None] * y[None, :] % PAD) / PAD)


def table_y_back():
    ky, y = np.arange(PAD), np.arange(E)
    return complex_rows(2.0 * np.pi * (y[:, None] * ky[None, :] % PAD) / PAD)


def table_y_taps():
    ky, tap = np.arange(PAD), np.arange(TAPS) - MARGIN
    angle = -2.0 * np.pi * ky[:, None] * tap[None, :] / PAD
    return complex_rows(angle)


def table_taps():
    kx, tap = np.arange(32), np.arange(KS) - MARGIN
    angle = -2.0 * np.pi * (kx[None, :] + 0.5) * tap[:, None] / PAD
    full = np.concatenate([np.tile(np.cos(angle), (1, 4)), np.tile(np.sin(angle), (1, 4))], axis=1)
    high, low = two_terms(full)
    table = np.zeros((128, LANES), ml_dtypes.bfloat16)
    for start, term in ((0, high), (32, high), (64, low)):
        table[start : start + KS] = term
    return table


def table_tap_turns():
    k4 = np.repeat(np.arange(4), 32)
    tap = np.arange(KS) - MARGIN
    angle = -2.0 * np.pi * tap[:, None] * k4[None, :] / PAD
    both = np.stack([np.cos(angle), np.sin(angle)], axis=0)
    return np.broadcast_to(both[:, :, None, :], (2, KS, 8, 128)).astype(np.float32)


def table_twiddle():
    k4 = np.repeat(np.arange(4), 32)
    angle = -2.0 * np.pi * np.arange(SLOTS)[:, None] * k4[None, :] / PAD
    both = np.stack([np.cos(angle), np.sin(angle)], axis=0)
    return np.broadcast_to(both[:, :, None, :], (2, SLOTS, 8, 128)).astype(np.float32)


def split(value):
    high = value.astype(BF16)
    low = (value - high.astype(F32)).astype(BF16)
    return high, low


def dot(left, right):
    return jnp.dot(left, right, preferred_element_type=F32)


def both_halves(rows_ref, rows):
    return jnp.concatenate([rows_ref[0, rows, :], rows_ref[1, rows, :]], axis=1)


def lane_iota(shape):
    return lax.broadcasted_iota(jnp.int32, shape, 1)


def cut(pieces, piece, target):
    offset = E * piece
    first, start = offset // 128, offset % 128
    shift = (target - start) % 128
    one = pltpu.roll(pieces[first], shift, 1) if shift else pieces[first]
    if start + E <= 128:
        return one
    two = pltpu.roll(pieces[first + 1], shift, 1) if shift else pieces[first + 1]
    edge = target + 128 - start
    return jnp.where(lane_iota(one.shape) < edge, one, two)


def unflatten(load, out_ref):
    lane = lane_iota((8, 128))
    zero = jnp.zeros((8, 128), F32)
    for block in range(12):
        parts = []
        for z4 in range(3):
            first = 3 * (96 * z4 + 8 * block)
            parts.append([load(first + m) for m in range(3)])
        for piece in range(8):
            low = cut(parts[0], piece, 0)
            mid = cut(parts[1], piece, 64)
            top = cut(parts[2], piece, 0)
            left = jnp.where(lane < E, low, jnp.where(lane < 64, zero, mid))
            left = jnp.where(lane < 64 + E, left, zero)
            rows = pl.ds(64 * block + piece, 8, stride=8)
            out_ref[0, rows, :] = left
            out_ref[1, rows, :] = jnp.where(lane < E, top, zero)


def flatten(rows_ref, flat_ref):
    lane = lane_iota((8, 128))
    for block in range(12):
        found = []
        for piece in range(8):
            rows = pl.ds(64 * block + piece, 8, stride=8)
            found.append((rows_ref[0, rows, :], rows_ref[1, rows, :]))
        for z4 in range(3):
            first = 3 * (96 * z4 + 8 * block)
            out = [None, None, None]
            for piece in range(8):
                value = found[piece][0] if z4 < 2 else found[piece][1]
                source = 64 if z4 == 1 else 0
                offset = E * piece
                spot, start = offset // 128, offset % 128
                shift = (start - source) % 128
                moved = pltpu.roll(value, shift, 1) if shift else value
                if out[spot] is None:
                    out[spot] = moved
                else:
                    out[spot] = jnp.where(lane < start, out[spot], moved)
                if start + E > 128:
                    out[spot + 1] = moved
            for m in range(3):
                flat_ref[pl.ds(first + m, 8, stride=3), :] = out[m]


def x_picks(wide, packed, low_start, high_start):
    place = packed % 128
    start = jnp.where(packed >= 128, high_start, low_start)
    here = (wide // PAD == place // MARGIN) & (wide % PAD == start + place % MARGIN) & (place < 3 * MARGIN)
    return jnp.where(here, 1.0, 0.0).astype(BF16)


def both_iotas():
    dims = (LANES, LANES)
    return lax.broadcasted_iota(jnp.int32, dims, 0), lax.broadcasted_iota(jnp.int32, dims, 1)


def pack_slabs(rows_ref):
    high = both_halves(rows_ref, slice(None)).astype(BF16)
    rows, columns = both_iotas()
    found = dot(high, x_picks(rows, columns, 0, E - MARGIN))
    faces = []
    for face in range(2):
        value = found[0:192, 128 * face : 128 * (face + 1)]
        for group in range(1, 4):
            part = found[192 * group : 192 * (group + 1), 128 * face : 128 * (face + 1)]
            value = value + pltpu.roll(part, 32 * group, 1)
        faces.append(value.astype(BF16))
    x0, x1 = faces
    low_rows, high_rows = [], []
    for slot in range(SLOTS):
        low_rows.append(both_halves(rows_ref, slice(E * slot, E * slot + MARGIN)))
        high_rows.append(both_halves(rows_ref, slice(E * slot + E - MARGIN, E * (slot + 1))))
    y0, y1 = jnp.concatenate(low_rows, axis=0), jnp.concatenate(high_rows, axis=0)
    y0, y1 = [jnp.concatenate([v[:, 0:128], v[:, 128:256]], axis=0).astype(BF16) for v in (y0, y1)]
    lane = lane_iota((192, 128))
    first = rows_ref[0, 0:192, :]
    second = pltpu.roll(rows_ref[0, 192:384, :], 64, 1)
    z0 = jnp.where(lane < 64, first, second).astype(BF16)
    first = rows_ref[1, 384:576, :]
    second = pltpu.roll(rows_ref[1, 576:768, :], 64, 1)
    z1 = jnp.where(lane < 64, first, second).astype(BF16)
    return (z0, z1), (y0, y1), (x0, x1)


def sort_margins(present, odd, axis, pair):
    on = [present[0, 2 * axis + side] >= 0 for side in range(2)]
    pair = [value.astype(F32) for value in pair]
    low = jnp.where(odd, pair[0], pair[1])
    high = jnp.where(odd, pair[1], pair[0])
    zero = jnp.zeros_like(low)
    return jnp.where(on[0], low, zero), jnp.where(on[1], high, zero)


def assemble(present, odds, rows_ref, margins, high_ref, low_ref):
    (zm, zp), (ym, yp), (xm, xp) = [
        sort_margins(present, odds[axis], axis, margins[axis]) for axis in range(3)
    ]
    rows, columns = both_iotas()
    picks = x_picks(columns, rows, PAD - MARGIN, E)
    parts = []
    for group in range(4):
        pair = [pltpu.roll(v, 128 - 32 * group, 1) if group else v for v in (xm, xp)]
        parts.append(jnp.concatenate(pair, axis=1))
    side = dot(jnp.concatenate(parts, axis=0).astype(BF16), picks)
    ym_rows, yp_rows = [jnp.concatenate([v[0:128], v[128:256]], axis=1) for v in (ym, yp)]
    z_sides = []
    for value in (zp, zm):
        z_sides.append(pltpu.roll(value, 64, 1))
        z_sides.append(value)
    lane = lane_iota((E, 128))
    for slot in range(SLOTS):
        group, inner = slot // 4, slot % 4
        core = both_halves(rows_ref, slice(E * slot, E * (slot + 1)))
        high, low = split(core)
        added = side[E * slot : E * (slot + 1)]
        full = high.astype(F32) + added
        z_side = z_sides[group][E * inner : E * (inner + 1), :]
        right = jnp.where(lane < 64, full[:, 128:256], z_side)
        high_ref[PAD * slot : PAD * slot + E, 0:128] = full[:, 0:128].astype(BF16)
        high_ref[PAD * slot : PAD * slot + E, 128:256] = right.astype(BF16)
        rows = slice(MARGIN * slot, MARGIN * (slot + 1))
        outer = jnp.concatenate([yp_rows[rows], ym_rows[rows]], axis=0)
        high_ref[PAD * slot + E : PAD * (slot + 1), :] = outer.astype(BF16)
        low_ref[PAD * slot : PAD * slot + E, :] = low
        low_ref[PAD * slot + E : PAD * (slot + 1), :] = jnp.zeros((PAD - E, LANES), BF16)


def lines_stage(high, low, table, out_ref, rows, step):
    for start in range(0, rows, step):
        part = slice(start, start + step)
        wide = jnp.concatenate([high[part, :], low[part, :], high[part, :]], axis=1)
        out_ref[part, :] = dot(wide, table[...])


def y_stage(lines_ref, table, count, out_ref):
    for pair in range(SLOTS // 2):
        one = lines_ref[count * 2 * pair : count * (2 * pair + 1), :]
        two = lines_ref[count * (2 * pair + 1) : count * (2 * pair + 2), :]
        real = jnp.concatenate([one[:, 0:128], two[:, 0:128]], axis=1)
        imag = jnp.concatenate([one[:, 128:256], two[:, 128:256]], axis=1)
        high, low = split(jnp.concatenate([real, imag], axis=0))
        out = dot(table[...], jnp.concatenate([high, low, high], axis=0))
        out_ref[2 * pair] = out[:, 0:128]
        out_ref[2 * pair + 1] = out[:, 128:256]


def y_back_stage(planes_ref, table, out_ref):
    for pair in range(SLOTS // 2):
        both = jnp.concatenate([planes_ref[2 * pair], planes_ref[2 * pair + 1]], axis=1)
        high, low = split(both)
        out = dot(table[...], jnp.concatenate([high, low, high], axis=0))
        for which in range(2):
            rows = slice(E * (2 * pair + which), E * (2 * pair + which + 1))
            lanes = slice(128 * which, 128 * (which + 1))
            out_ref[rows, 0:128] = out[0:E, lanes]
            out_ref[rows, 128:256] = out[E : 2 * E, lanes]


def turn(value, cosine, sine):
    real, imag = value
    return real * cosine - imag * sine, real * sine + imag * cosine


def dft4(values, sign):
    (ar, ai), (br, bi), (cr, ci), (dr, di) = values
    sr, si, mr, mi = ar + cr, ai + ci, ar - cr, ai - ci
    pr, pi, qr, qi = br + dr, bi + di, br - dr, bi - di
    if sign > 0:
        first, third = (mr - qi, mi + qr), (mr + qi, mi - qr)
    else:
        first, third = (mr + qi, mi - qr), (mr - qi, mi + qr)
    return [(sr + pr, si + pi), first, (sr - pr, si - pi), third]


def dft16(values, sign):
    inner = []
    for low in range(4):
        line = dft4([values[4 * top + low] for top in range(4)], sign)
        moved = []
        for k in range(4):
            turns = low * k
            real, imag = line[k]
            if turns == 0:
                moved.append((real, imag))
            elif turns == 4:
                moved.append((-imag, real) if sign > 0 else (imag, -real))
            elif turns in (2, 6):
                root = float(np.sqrt(0.5))
                a, b = root * real, root * imag
                if turns == 2:
                    moved.append((a - b, a + b) if sign > 0 else (a + b, b - a))
                else:
                    moved.append((-a - b, a - b) if sign > 0 else (b - a, -a - b))
            else:
                angle = sign * 2.0 * np.pi * turns / SLOTS
                moved.append(turn((real, imag), float(np.cos(angle)), float(np.sin(angle))))
        inner.append(moved)
    out = [None] * SLOTS
    for k in range(4):
        line = dft4([inner[low][k] for low in range(4)], sign)
        for top in range(4):
            out[k + 4 * top] = line[top]
    return out


def z_forward(planes_ref, twiddle, rows, rows_imag):
    values = []
    for slot in range(SLOTS):
        value = (planes_ref[slot, rows, :], planes_ref[slot, rows_imag, :])
        if slot:
            value = turn(value, twiddle[0, slot], twiddle[1, slot])
        values.append(value)
    return dft16(values, -1)


def z_stage(planes_ref, out_ref):
    @pl.loop(0, PAD // 8)
    def _(step):
        rows = pl.ds(pl.multiple_of(8 * step, 8), 8)
        rows_imag = pl.ds(pl.multiple_of(8 * step + PAD, 8), 8)
        values = [(planes_ref[slot, rows, :], planes_ref[slot, rows_imag, :]) for slot in range(SLOTS)]
        values = dft16(values, -1)
        for slot in range(SLOTS):
            out_ref[slot, rows, :] = values[slot][0]
            out_ref[slot, rows_imag, :] = values[slot][1]


def filter_stage(planes_ref, kernel_ref, twiddle, conjugate, out_ref):
    @pl.loop(0, PAD // 8)
    def _(step):
        rows = pl.ds(pl.multiple_of(8 * step, 8), 8)
        rows_imag = pl.ds(pl.multiple_of(8 * step + PAD, 8), 8)
        values = z_forward(planes_ref, twiddle, rows, rows_imag)
        for slot in range(SLOTS):
            cosine, sine = kernel_ref[slot, rows, :], kernel_ref[slot, rows_imag, :]
            if conjugate:
                real, imag = values[slot]
                values[slot] = (real * cosine + imag * sine, imag * cosine - real * sine)
            else:
                values[slot] = turn(values[slot], cosine, sine)
        values = dft16(values, 1)
        for slot in range(SLOTS):
            real, imag = values[slot]
            if slot:
                cosine, sine = twiddle[0, slot], twiddle[1, slot]
                real, imag = real * cosine + imag * sine, imag * cosine - real * sine
            out_ref[slot, rows, :] = real
            out_ref[slot, rows_imag, :] = imag


def tap_stage(flat_ref, lines, spread, table, turns, table_y_ref, planes_ref):
    lane = lane_iota((3, 128))
    for tap in range(KS):
        row, start = KS2 * tap // 128, KS2 * tap % 128
        value = flat_ref[row : row + 3, :]
        if start:
            value = pltpu.roll(value, 128 - start, 1)
            after = pltpu.roll(flat_ref[row + 1 : row + 4, :], 128 - start, 1)
            value = jnp.where(lane < 128 - start, value, after)
        for part in range(3):
            lines[part, tap : tap + 1, :] = value[part : part + 1]
    lane = lane_iota((TAPS, 128))
    for line in range(KS):
        part, start = KS * line // 128, KS * line % 128
        value = lines[part]
        if start:
            value = pltpu.roll(value, 128 - start, 1)
            if start + KS > 128:
                after = pltpu.roll(lines[part + 1], 128 - start, 1)
                value = jnp.where(lane < 128 - start, value, after)
        spread[TAPS * line : TAPS * (line + 1), :] = jnp.where(lane < KS, value, 0.0)
    for line in range(KS, TAPS):
        spread[TAPS * line : TAPS * (line + 1), :] = jnp.zeros((TAPS, 128), F32)
    rows = jnp.concatenate([spread[pl.ds(tap, TAPS, stride=TAPS), :] for tap in range(KS)], axis=0)
    high = rows.astype(BF16).astype(F32)
    low = rows - high
    wide = high + pltpu.roll(low, 32, 1) + pltpu.roll(high, 64, 1)
    out = dot(wide.astype(BF16), table[...])
    slots = [None] * SLOTS
    for tap in range(KS):
        part = out[TAPS * tap : TAPS * (tap + 1)]
        value = part[:, 0:128], part[:, 128:256]
        if tap != MARGIN:
            cosine, sine = [jnp.concatenate([turns[i, tap]] * 3, axis=0) for i in range(2)]
            value = turn(value, cosine, sine)
        slot = (tap - MARGIN) % SLOTS
        if slots[slot] is not None:
            value = value[0] + slots[slot][0], value[1] + slots[slot][1]
        slots[slot] = value
    for pair in range(SLOTS // 2):
        one, two = slots[2 * pair], slots[2 * pair + 1]
        real = jnp.concatenate([one[0], two[0]], axis=1)
        imag = jnp.concatenate([one[1], two[1]], axis=1)
        high, low = split(jnp.concatenate([real, imag], axis=0))
        out = dot(table_y_ref[...], jnp.concatenate([high, low, high], axis=0))
        planes_ref[2 * pair] = out[:, 0:128]
        planes_ref[2 * pair + 1] = out[:, 128:256]


def gathered_place(count, distance):
    place, size = 0, 1
    for bits in gather_rounds(count):
        for bit in bits:
            place = place + size * ((distance >> bit) & 1)
            size *= 2
    return place


def spectrum_kernel(update, count, order, lists, blend, cell_row, near, far, table, turns, table_y_ref, out_ref, got, flat, lines, spread, planes, sems):
    view = order[update]
    own = lax.axis_index("blk")
    half = count // 2
    for k in range(2):
        place = gathered_place(count, cell_row[lists[0, k, view]] ^ own)

        @pl.when(place < half)
        def _():
            pltpu.make_async_copy(near.at[place], got.at[k], sems.at[k]).start()

        @pl.when(place >= half)
        def _():
            pltpu.make_async_copy(far.at[place - half], got.at[k], sems.at[k]).start()

    for k in range(2):
        pltpu.make_async_copy(near.at[0], got.at[k], sems.at[k]).wait()
    total = blend[0, 0, view] + blend[0, 1, view]
    value = None
    for k in range(2):
        line = got[k].astype(F32)[CELLROWS * update : CELLROWS * (update + 1), :]
        weight = blend[0, k, view] / total * (2.0 / float(PAD**3))
        part = line * (weight / jnp.sum(line))
        value = part if value is None else value + part
    flat[...] = value
    tap_stage(flat, lines, spread, table, turns, table_y_ref, planes)
    z_stage(planes, out_ref)


def grid_bits(count):
    low_count = count.bit_length() - 2
    bits = [[bit for bit in range(low_count) if bit % 3 == axis] for axis in range(3)]
    bits[2] = [low_count] + bits[2]
    return bits


def gather_rounds(count):
    bits = list(range(count.bit_length() - 1))
    rounds = [bits[:1]]
    bits = bits[1:]
    while bits:
        rounds.append(bits[:2])
        bits = bits[2:]
    return rounds[::-1]


def odd_places(count):
    own = lax.axis_index("blk")
    return [((own >> bits[0]) & 1) == 1 if bits else own < 0 for bits in grid_bits(count)]


def store_slabs(count, slabs, outs):
    for odd, pair, refs in zip(odd_places(count), slabs, outs):
        low, high = pair
        refs[0][...] = jnp.where(odd, low, high)
        refs[1][...] = jnp.where(odd, high, low)


def start_kernel(count, order, cells, est, u_out, cells_out, first_out, z0, z1, y0, y1, x1, pad):
    zero = jnp.zeros((2, CELLROWS * 128), F32)
    pad[...] = zero
    for update in range(UPDATES):
        pad[update : update + 1, 0:KS3] = cells[order[update]]
    wide = pad[...].astype(BF16).astype(F32)
    for update in range(UPDATES):
        rows = [wide[update : update + 1, 128 * row : 128 * (row + 1)] for row in range(CELLROWS)]
        block = jnp.concatenate(rows, axis=0).astype(BF16)
        here = slice(CELLROWS * update, CELLROWS * (update + 1))
        cells_out[here, :] = block
        first_out[here, :] = block
    unflatten(lambda row: est[pl.ds(row, 8, stride=3), :], u_out)
    store_slabs(count, pack_slabs(u_out), ((z0, z1), (y0, y1), (first_out.at[2 * CELLROWS :], x1)))


def views_kernel(order, observed, o0, o1, wide):
    step_rows = 32

    @pl.loop(0, FLAT // step_rows)
    def _(step):
        for row in range(step_rows):
            at = step * step_rows + row
            lanes = pl.ds(pl.multiple_of(at * 128, 128), 128)
            wide[pl.ds(pl.multiple_of(at * 8, 8), VIEWS), :] = observed[0, :, lanes].astype(F32)

    for update, out in enumerate((o0, o1)):
        view = order[update]
        unflatten(lambda row: wide[pl.ds(8 * row + view, 8, stride=24), :], out)


def field_kernel(count, present, u, z0, z1, y0, y1, x0, x1, ea, gy, out, high, low, lines):
    margins = ((z0[...], z1[...]), (y0[...], y1[...]), (x0[2 * CELLROWS :, :] if x0.shape[0] > 192 else x0[...], x1[...]))
    assemble(present, odd_places(count), u, margins, high, low)
    lines_stage(high, low, ea, lines, SLOTS * PAD, 256)
    y_stage(lines, gy, PAD, out)


def update_body(tissue, planes, kernel, u, o, tables, scratch, new_ref):
    ea, ei, gh, gb, twiddle = tables
    planes2, lines = scratch
    filter_stage(planes, kernel, twiddle, False, planes2)
    y_back_stage(planes2, gb, lines)
    rows = SLOTS * E
    lane = lane_iota((rows, LANES))
    valid = (lane % PAD < E) & (lane < 3 * PAD)
    high, low = split(lines[...])
    blurred = dot(jnp.concatenate([high, low, high], axis=1), ei[...])
    quotient = jnp.where(valid, both_halves(o, slice(None)) / blurred, 0.0)
    high, low = split(quotient)
    lines[...] = dot(jnp.concatenate([high, low, high], axis=1), ea[...])
    y_stage(lines, gh, E, planes2)
    filter_stage(planes2, kernel, twiddle, True, planes2)
    y_back_stage(planes2, gb, lines)
    high, low = split(lines[...])
    correction = dot(jnp.concatenate([high, low, high], axis=1), ei[...])
    alive = tissue[0] > 0
    for half in range(2):
        core = u[half]
        new_ref[half] = jnp.where(alive, core * correction[:, 128 * half : 128 * (half + 1)], core)


def first_kernel(count, tissue, planes, kernel, u, o, ea, ei, gh, gb, twiddle, u_out, z0, z1, y0, y1, x0, x1, planes2, lines):
    update_body(tissue, planes, kernel, u, o, (ea, ei, gh, gb, twiddle), (planes2, lines), u_out)
    store_slabs(count, pack_slabs(u_out), ((z0, z1), (y0, y1), (x0, x1)))


def last_kernel(tissue, planes, kernel, u, o, ea, ei, gh, gb, twiddle, out, planes2, lines, fresh):
    update_body(tissue, planes, kernel, u, o, (ea, ei, gh, gb, twiddle), (planes2, lines), fresh)
    flatten(fresh, out)


VM = pl.BlockSpec(memory_space=pltpu.VMEM)
SM = pl.BlockSpec(memory_space=pltpu.SMEM)
ANY = pl.BlockSpec(memory_space=pl.ANY)
PARAMS = pltpu.CompilerParams(vmem_limit_bytes=48 * 1024 * 1024)


def shape(dims, kind=F32):
    return jax.ShapeDtypeStruct(dims, kind)


SLAB = shape((192, 128), BF16)
WIDE_SLAB = shape((256, 128), BF16)
CELLS = shape((UPDATES * CELLROWS, 128), BF16)
ROWS = shape((2, SLOTS * E, 128))
ROWS_V = pltpu.VMEM((2, SLOTS * E, 128), F32)
PLANES = shape((SLOTS, 128, 128))
PLANES_V = pltpu.VMEM((SLOTS, 128, 128), F32)
LINES_V = pltpu.VMEM((SLOTS * E, LANES), F32)


def call(body, ins, outs, args, scratch=(), name=None):
    many = isinstance(outs, list)
    return pl.pallas_call(
        body,
        in_specs=ins,
        out_specs=[VM] * len(outs) if many else VM,
        out_shape=outs,
        scratch_shapes=list(scratch),
        compiler_params=PARAMS,
        name=name,
    )(*args)


def far_pairs(count, axis):
    bits = grid_bits(count)[axis]
    extent = 2 ** len(bits)
    pairs = []
    for number in range(count):
        at = sum(((number >> bit) & 1) << level for level, bit in enumerate(bits))
        moved = at + 1 if at % 2 else at - 1
        if 0 <= moved < extent:
            other = number
            for level, bit in enumerate(bits):
                other = other & ~(1 << bit) | ((moved >> level) & 1) << bit
            pairs.append((number, other))
    return pairs


def swap(value, distance, count):
    return lax.ppermute(value, "blk", [(number, number ^ distance) for number in range(count)])


def near_swap(value, axis, count):
    bits = grid_bits(count)[axis]
    return swap(value, 1 << bits[0], count) if bits else jnp.zeros_like(value)


def far_swap(value, axis, count):
    pairs = far_pairs(count, axis)
    return lax.ppermute(value, "blk", pairs) if pairs else jnp.zeros_like(value)


def local(estimate, observed, psf_cells, tissue, neighbours, psf_list, psf_blend, cell_row, view_order):
    count = lax.axis_size("blk")
    ea = jnp.asarray(stacked(table_space_to_lines(), 0))
    ei = jnp.asarray(stacked(table_lines_to_space(), 0))
    gy = jnp.asarray(stacked(table_y(PAD), 1))
    gh = jnp.asarray(stacked(table_y(E), 1))
    gb = jnp.asarray(stacked(table_y_back(), 1))
    gt = jnp.asarray(stacked(table_y_taps(), 1))
    taps = jnp.asarray(table_taps())
    turns = jnp.asarray(table_tap_turns())
    twiddle = jnp.asarray(table_twiddle())
    lists = jnp.swapaxes(psf_list, 1, 2)
    blend = jnp.swapaxes(psf_blend, 1, 2)

    rows, cells, first, z0, z1, y0, y1, x1 = call(
        functools.partial(start_kernel, count),
        [SM, VM, VM],
        [ROWS, CELLS, shape((UPDATES * CELLROWS + 192, 128), BF16), SLAB, SLAB, WIDE_SLAB, WIDE_SLAB, SLAB],
        (view_order, jnp.swapaxes(psf_cells, 0, 1), estimate.reshape(FLAT, 128)),
        [pltpu.VMEM((UPDATES, CELLROWS * 128), F32)],
        name="start",
    )
    targets = call(
        views_kernel, [SM, VM], [ROWS, ROWS], (view_order, observed), [pltpu.VMEM((8 * FLAT, 128), F32)], name="views"
    )
    pair_bits = [bits[0] if bits else None for bits in grid_bits(count)]
    near_x, near_y = None, None
    held = cells
    rounds = gather_rounds(count)
    for bits in rounds[:-1]:
        arrived = [held]
        size = held.shape[0]
        for part in range(1, 2 ** len(bits)):
            distance = sum(((part >> level) & 1) << bit for level, bit in enumerate(bits))
            sent = held
            if distance == 1 << pair_bits[2] and held is cells:
                near_x = swap(first, distance, count)
                arrived.append(near_x[:size])
            elif pair_bits[1] is not None and distance == 1 << pair_bits[1]:
                both = swap(jnp.concatenate([held, y0], axis=0), distance, count)
                near_y = both[size:]
                arrived.append(both[:size])
            else:
                arrived.append(swap(held, distance, count))
        held = jnp.concatenate(arrived, axis=0)
    if near_x is None:
        near_x = near_swap(first, 2, count)
    if near_y is None:
        near_y = near_swap(y0, 1, count)
    far_z, far_y, far_x = far_swap(z1, 0, count), far_swap(y1, 1, count), far_swap(x1, 2, count)
    near_z = near_swap(z0, 0, count)
    other = swap(held, 1, count)
    near_cells, far_cells = [v.reshape(count // 2, UPDATES * CELLROWS, 128) for v in (held, other)]

    def spectrum(update):
        return call(
            functools.partial(spectrum_kernel, update, count),
            [SM] * 4 + [ANY] * 2 + [VM] * 3,
            PLANES,
            (view_order, lists, blend, cell_row, near_cells, far_cells, taps, turns, gt),
            [
                pltpu.VMEM((2, UPDATES * CELLROWS, 128), BF16),
                pltpu.VMEM((CELLROWS, 128), F32),
                pltpu.VMEM((3, TAPS, 128), F32),
                pltpu.VMEM((TAPS * TAPS, 128), F32),
                PLANES_V,
                pltpu.SemaphoreType.DMA((2,)),
            ],
            name="spectrum",
        )

    def field(rows, margins):
        return call(
            functools.partial(field_kernel, count),
            [SM] + [VM] * 9,
            PLANES,
            (neighbours, rows, *margins, ea, gy),
            [pltpu.VMEM((SLOTS * PAD, LANES), BF16)] * 2 + [pltpu.VMEM((SLOTS * PAD, LANES), F32)],
            name="field",
        )

    planes = field(rows, (near_z, far_z, near_y, far_y, near_x, far_x))
    kernel = spectrum(0)
    first = call(
        functools.partial(first_kernel, count),
        [SM] + [VM] * 9,
        [ROWS, SLAB, SLAB, WIDE_SLAB, WIDE_SLAB, SLAB, SLAB],
        (tissue, planes, kernel, rows, targets[0], ea, ei, gh, gb, twiddle),
        [PLANES_V, LINES_V],
        name="first",
    )
    rows, slabs = first[0], first[1:]
    margins = []
    for axis in range(3):
        margins.append(near_swap(slabs[2 * axis], axis, count))
        margins.append(far_swap(slabs[2 * axis + 1], axis, count))
    kernel = spectrum(1)
    planes = field(rows, margins)
    out = call(
        last_kernel,
        [SM] + [VM] * 9,
        shape((FLAT, 128)),
        (tissue, planes, kernel, rows, targets[1], ea, ei, gh, gb, twiddle),
        [PLANES_V, LINES_V, ROWS_V],
        name="last",
    )
    return out.reshape(1, FLAT * 128)


def solution(mesh):
    return jax.shard_map(
        local,
        mesh=mesh,
        in_specs=(
            P("blk", None),
            P("blk", None, None),
            P("blk", None, None),
            P("blk"),
            P("blk", None),
            P("blk", None, None),
            P("blk", None, None),
            P(),
            P(),
        ),
        out_specs=P("blk", None),
        check_vma=False,
    )
```

```python
import functools

import numpy as np

import jax
import jax.numpy as jnp
import ml_dtypes
from jax import lax
from jax.experimental import pallas as pl
from jax.experimental.pallas import tpu as pltpu
from jax.sharding import PartitionSpec as P

E = 48
MARGIN = 8
UPDATES = 2
VIEWS = 6
PAD = 64
KS = 17
KS2 = KS * KS
KS3 = 4913
SLOTS = 16
LANES = 256
TAPS = 24
CELLROWS = 40
FLAT = 864

F32 = jnp.float32
BF16 = jnp.bfloat16


def two_terms(table):
    high = table.astype(ml_dtypes.bfloat16)
    low = (table - high.astype(np.float64)).astype(ml_dtypes.bfloat16)
    return high, low


def stacked(table, axis):
    high, low = two_terms(table)
    return np.concatenate([high, high, low], axis=axis)


def x_positions():
    x = np.arange(PAD)
    return np.where(x < PAD - MARGIN, x, x - PAD)


def table_space_to_lines():
    z4, k4, kx = np.arange(4), np.arange(4), np.arange(32)
    angle = -2.0 * np.pi * (
        z4[:, None, None, None] * k4[None, None, :, None] / 4.0
        + (kx[None, None, None, :] + 0.5) * x_positions()[None, :, None, None] / PAD
    )
    angle = angle.reshape(LANES, 128)
    return np.concatenate([np.cos(angle), np.sin(angle)], axis=1)


def table_lines_to_space():
    back = table_space_to_lines().T.copy()
    back = back.reshape(LANES, 4, PAD)
    back[:, 3, :] = 0.0
    back[:, :, E:] = 0.0
    return back.reshape(LANES, LANES)


def complex_rows(angle):
    cosine, sine = np.cos(angle), np.sin(angle)
    return np.concatenate(
        [np.concatenate([cosine, -sine], axis=1), np.concatenate([sine, cosine], axis=1)], axis=0
    )


def table_y(count):
    ky, y = np.arange(PAD), np.arange(count)
    return complex_rows(-2.0 * np.pi * (ky[:, None] * y[None, :] % PAD) / PAD)


def table_y_back():
    ky, y = np.arange(PAD), np.arange(E)
    return complex_rows(2.0 * np.pi * (y[:, None] * ky[None, :] % PAD) / PAD)


def table_y_taps():
    ky, tap = np.arange(PAD), np.arange(TAPS) - MARGIN
    angle = -2.0 * np.pi * ky[:, None] * tap[None, :] / PAD
    return complex_rows(angle)


def table_taps():
    kx, tap = np.arange(32), np.arange(KS) - MARGIN
    angle = -2.0 * np.pi * (kx[None, :] + 0.5) * tap[:, None] / PAD
    full = np.concatenate([np.tile(np.cos(angle), (1, 4)), np.tile(np.sin(angle), (1, 4))], axis=1)
    high, low = two_terms(full)
    table = np.zeros((128, LANES), ml_dtypes.bfloat16)
    for start, term in ((0, high), (32, high), (64, low)):
        table[start : start + KS] = term
    return table


def table_tap_turns():
    k4 = np.repeat(np.arange(4), 32)
    tap = np.arange(KS) - MARGIN
    angle = -2.0 * np.pi * tap[:, None] * k4[None, :] / PAD
    both = np.stack([np.cos(angle), np.sin(angle)], axis=0)
    return np.broadcast_to(both[:, :, None, :], (2, KS, 8, 128)).astype(np.float32)


def table_twiddle():
    k4 = np.repeat(np.arange(4), 32)
    angle = -2.0 * np.pi * np.arange(SLOTS)[:, None] * k4[None, :] / PAD
    both = np.stack([np.cos(angle), np.sin(angle)], axis=0)
    return np.broadcast_to(both[:, :, None, :], (2, SLOTS, 8, 128)).astype(np.float32)


def split(value):
    high = value.astype(BF16)
    low = (value - high.astype(F32)).astype(BF16)
    return high, low


def dot(left, right):
    return jnp.dot(left, right, preferred_element_type=F32)


def both_halves(rows_ref, rows):
    return jnp.concatenate([rows_ref[0, rows, :], rows_ref[1, rows, :]], axis=1)


def lane_iota(shape):
    return lax.broadcasted_iota(jnp.int32, shape, 1)


def cut(pieces, piece, target):
    offset = E * piece
    first, start = offset // 128, offset % 128
    shift = (target - start) % 128
    one = pltpu.roll(pieces[first], shift, 1) if shift else pieces[first]
    if start + E <= 128:
        return one
    two = pltpu.roll(pieces[first + 1], shift, 1) if shift else pieces[first + 1]
    edge = target + 128 - start
    return jnp.where(lane_iota(one.shape) < edge, one, two)


def unflatten(load, out_ref):
    lane = lane_iota((8, 128))
    zero = jnp.zeros((8, 128), F32)
    for block in range(12):
        parts = []
        for z4 in range(3):
            first = 3 * (96 * z4 + 8 * block)
            parts.append([load(first + m) for m in range(3)])
        for piece in range(8):
            low = cut(parts[0], piece, 0)
            mid = cut(parts[1], piece, 64)
            top = cut(parts[2], piece, 0)
            left = jnp.where(lane < E, low, jnp.where(lane < 64, zero, mid))
            left = jnp.where(lane < 64 + E, left, zero)
            rows = pl.ds(64 * block + piece, 8, stride=8)
            out_ref[0, rows, :] = left
            out_ref[1, rows, :] = jnp.where(lane < E, top, zero)


def flatten(rows_ref, flat_ref):
    lane = lane_iota((8, 128))
    for block in range(12):
        found = []
        for piece in range(8):
            rows = pl.ds(64 * block + piece, 8, stride=8)
            found.append((rows_ref[0, rows, :], rows_ref[1, rows, :]))
        for z4 in range(3):
            first = 3 * (96 * z4 + 8 * block)
            out = [None, None, None]
            for piece in range(8):
                value = found[piece][0] if z4 < 2 else found[piece][1]
                source = 64 if z4 == 1 else 0
                offset = E * piece
                spot, start = offset // 128, offset % 128
                shift = (start - source) % 128
                moved = pltpu.roll(value, shift, 1) if shift else value
                if out[spot] is None:
                    out[spot] = moved
                else:
                    out[spot] = jnp.where(lane < start, out[spot], moved)
                if start + E > 128:
                    out[spot + 1] = moved
            for m in range(3):
                flat_ref[pl.ds(first + m, 8, stride=3), :] = out[m]


def x_picks(wide, packed, low_start, high_start):
    place = packed % 128
    start = jnp.where(packed >= 128, high_start, low_start)
    here = (wide // PAD == place // MARGIN) & (wide % PAD == start + place % MARGIN) & (place < 3 * MARGIN)
    return jnp.where(here, 1.0, 0.0).astype(BF16)


def both_iotas():
    dims = (LANES, LANES)
    return lax.broadcasted_iota(jnp.int32, dims, 0), lax.broadcasted_iota(jnp.int32, dims, 1)


def pack_slabs(rows_ref):
    high = both_halves(rows_ref, slice(None)).astype(BF16)
    rows, columns = both_iotas()
    found = dot(high, x_picks(rows, columns, 0, E - MARGIN))
    faces = []
    for face in range(2):
        value = found[0:192, 128 * face : 128 * (face + 1)]
        for group in range(1, 4):
            part = found[192 * group : 192 * (group + 1), 128 * face : 128 * (face + 1)]
            value = value + pltpu.roll(part, 32 * group, 1)
        faces.append(value.astype(BF16))
    x0, x1 = faces
    low_rows, high_rows = [], []
    for slot in range(SLOTS):
        low_rows.append(both_halves(rows_ref, slice(E * slot, E * slot + MARGIN)))
        high_rows.append(both_halves(rows_ref, slice(E * slot + E - MARGIN, E * (slot + 1))))
    y0, y1 = jnp.concatenate(low_rows, axis=0), jnp.concatenate(high_rows, axis=0)
    y0, y1 = [jnp.concatenate([v[:, 0:128], v[:, 128:256]], axis=0).astype(BF16) for v in (y0, y1)]
    lane = lane_iota((192, 128))
    first = rows_ref[0, 0:192, :]
    second = pltpu.roll(rows_ref[0, 192:384, :], 64, 1)
    z0 = jnp.where(lane < 64, first, second).astype(BF16)
    first = rows_ref[1, 384:576, :]
    second = pltpu.roll(rows_ref[1, 576:768, :], 64, 1)
    z1 = jnp.where(lane < 64, first, second).astype(BF16)
    return (z0, z1), (y0, y1), (x0, x1)


def sort_margins(present, odd, axis, pair):
    on = [present[0, 2 * axis + side] >= 0 for side in range(2)]
    pair = [value.astype(F32) for value in pair]
    low = jnp.where(odd, pair[0], pair[1])
    high = jnp.where(odd, pair[1], pair[0])
    zero = jnp.zeros_like(low)
    return jnp.where(on[0], low, zero), jnp.where(on[1], high, zero)


def assemble(present, odds, rows_ref, margins, high_ref, low_ref):
    (zm, zp), (ym, yp), (xm, xp) = [
        sort_margins(present, odds[axis], axis, margins[axis]) for axis in range(3)
    ]
    rows, columns = both_iotas()
    picks = x_picks(columns, rows, PAD - MARGIN, E)
    parts = []
    for group in range(4):
        pair = [pltpu.roll(v, 128 - 32 * group, 1) if group else v for v in (xm, xp)]
        parts.append(jnp.concatenate(pair, axis=1))
    side = dot(jnp.concatenate(parts, axis=0).astype(BF16), picks)
    ym_rows, yp_rows = [jnp.concatenate([v[0:128], v[128:256]], axis=1) for v in (ym, yp)]
    z_sides = []
    for value in (zp, zm):
        z_sides.append(pltpu.roll(value, 64, 1))
        z_sides.append(value)
    lane = lane_iota((E, 128))
    for slot in range(SLOTS):
        group, inner = slot // 4, slot % 4
        core = both_halves(rows_ref, slice(E * slot, E * (slot + 1)))
        high, low = split(core)
        added = side[E * slot : E * (slot + 1)]
        full = high.astype(F32) + added
        z_side = z_sides[group][E * inner : E * (inner + 1), :]
        right = jnp.where(lane < 64, full[:, 128:256], z_side)
        high_ref[PAD * slot : PAD * slot + E, 0:128] = full[:, 0:128].astype(BF16)
        high_ref[PAD * slot : PAD * slot + E, 128:256] = right.astype(BF16)
        rows = slice(MARGIN * slot, MARGIN * (slot + 1))
        outer = jnp.concatenate([yp_rows[rows], ym_rows[rows]], axis=0)
        high_ref[PAD * slot + E : PAD * (slot + 1), :] = outer.astype(BF16)
        low_ref[PAD * slot : PAD * slot + E, :] = low
        low_ref[PAD * slot + E : PAD * (slot + 1), :] = jnp.zeros((PAD - E, LANES), BF16)


def lines_stage(high, low, table, out_ref, rows, step):
    for start in range(0, rows, step):
        part = slice(start, start + step)
        wide = jnp.concatenate([high[part, :], low[part, :], high[part, :]], axis=1)
        out_ref[part, :] = dot(wide, table[...])


def y_stage(lines_ref, table, count, out_ref):
    for pair in range(SLOTS // 2):
        one = lines_ref[count * 2 * pair : count * (2 * pair + 1), :]
        two = lines_ref[count * (2 * pair + 1) : count * (2 * pair + 2), :]
        real = jnp.concatenate([one[:, 0:128], two[:, 0:128]], axis=1)
        imag = jnp.concatenate([one[:, 128:256], two[:, 128:256]], axis=1)
        high, low = split(jnp.concatenate([real, imag], axis=0))
        out = dot(table[...], jnp.concatenate([high, low, high], axis=0))
        out_ref[2 * pair] = out[:, 0:128]
        out_ref[2 * pair + 1] = out[:, 128:256]


def y_back_stage(planes_ref, table, out_ref):
    for pair in range(SLOTS // 2):
        both = jnp.concatenate([planes_ref[2 * pair], planes_ref[2 * pair + 1]], axis=1)
        high, low = split(both)
        out = dot(table[...], jnp.concatenate([high, low, high], axis=0))
        for which in range(2):
            rows = slice(E * (2 * pair + which), E * (2 * pair + which + 1))
            lanes = slice(128 * which, 128 * (which + 1))
            out_ref[rows, 0:128] = out[0:E, lanes]
            out_ref[rows, 128:256] = out[E : 2 * E, lanes]


def turn(value, cosine, sine):
    real, imag = value
    return real * cosine - imag * sine, real * sine + imag * cosine


def dft4(values, sign):
    (ar, ai), (br, bi), (cr, ci), (dr, di) = values
    sr, si, mr, mi = ar + cr, ai + ci, ar - cr, ai - ci
    pr, pi, qr, qi = br + dr, bi + di, br - dr, bi - di
    if sign > 0:
        first, third = (mr - qi, mi + qr), (mr + qi, mi - qr)
    else:
        first, third = (mr + qi, mi - qr), (mr - qi, mi + qr)
    return [(sr + pr, si + pi), first, (sr - pr, si - pi), third]


def dft16(values, sign):
    inner = []
    for low in range(4):
        line = dft4([values[4 * top + low] for top in range(4)], sign)
        moved = []
        for k in range(4):
            turns = low * k
            real, imag = line[k]
            if turns == 0:
                moved.append((real, imag))
            elif turns == 4:
                moved.append((-imag, real) if sign > 0 else (imag, -real))
            elif turns in (2, 6):
                root = float(np.sqrt(0.5))
                a, b = root * real, root * imag
                if turns == 2:
                    moved.append((a - b, a + b) if sign > 0 else (a + b, b - a))
                else:
                    moved.append((-a - b, a - b) if sign > 0 else (b - a, -a - b))
            else:
                angle = sign * 2.0 * np.pi * turns / SLOTS
                moved.append(turn((real, imag), float(np.cos(angle)), float(np.sin(angle))))
        inner.append(moved)
    out = [None] * SLOTS
    for k in range(4):
        line = dft4([inner[low][k] for low in range(4)], sign)
        for top in range(4):
            out[k + 4 * top] = line[top]
    return out


def z_forward(planes_ref, twiddle, rows, rows_imag):
    values = []
    for slot in range(SLOTS):
        value = (planes_ref[slot, rows, :], planes_ref[slot, rows_imag, :])
        if slot:
            value = turn(value, twiddle[0, slot], twiddle[1, slot])
        values.append(value)
    return dft16(values, -1)


def z_stage(planes_ref, out_ref):
    @pl.loop(0, PAD // 8, unroll=2)
    def _(step):
        rows = pl.ds(pl.multiple_of(8 * step, 8), 8)
        rows_imag = pl.ds(pl.multiple_of(8 * step + PAD, 8), 8)
        values = [(planes_ref[slot, rows, :], planes_ref[slot, rows_imag, :]) for slot in range(SLOTS)]
        values = dft16(values, -1)
        for slot in range(SLOTS):
            out_ref[slot, rows, :] = values[slot][0]
            out_ref[slot, rows_imag, :] = values[slot][1]


def filter_stage(planes_ref, kernel_ref, twiddle, conjugate, out_ref):
    @pl.loop(0, PAD // 8, unroll=2)
    def _(step):
        rows = pl.ds(pl.multiple_of(8 * step, 8), 8)
        rows_imag = pl.ds(pl.multiple_of(8 * step + PAD, 8), 8)
        values = z_forward(planes_ref, twiddle, rows, rows_imag)
        for slot in range(SLOTS):
            cosine, sine = kernel_ref[slot, rows, :], kernel_ref[slot, rows_imag, :]
            if conjugate:
                real, imag = values[slot]
                values[slot] = (real * cosine + imag * sine, imag * cosine - real * sine)
            else:
                values[slot] = turn(values[slot], cosine, sine)
        values = dft16(values, 1)
        for slot in range(SLOTS):
            real, imag = values[slot]
            if slot:
                cosine, sine = twiddle[0, slot], twiddle[1, slot]
                real, imag = real * cosine + imag * sine, imag * cosine - real * sine
            out_ref[slot, rows, :] = real
            out_ref[slot, rows_imag, :] = imag


def tap_stage(flat_ref, lines, spread, table, turns, table_y_ref, planes_ref):
    lane = lane_iota((3, 128))
    for tap in range(KS):
        row, start = KS2 * tap // 128, KS2 * tap % 128
        value = flat_ref[row : row + 3, :]
        if start:
            value = pltpu.roll(value, 128 - start, 1)
            after = pltpu.roll(flat_ref[row + 1 : row + 4, :], 128 - start, 1)
            value = jnp.where(lane < 128 - start, value, after)
        for part in range(3):
            lines[part, tap : tap + 1, :] = value[part : part + 1]
    lane = lane_iota((TAPS, 128))
    for line in range(KS):
        part, start = KS * line // 128, KS * line % 128
        value = lines[part]
        if start:
            value = pltpu.roll(value, 128 - start, 1)
            if start + KS > 128:
                after = pltpu.roll(lines[part + 1], 128 - start, 1)
                value = jnp.where(lane < 128 - start, value, after)
        spread[TAPS * line : TAPS * (line + 1), :] = jnp.where(lane < KS, value, 0.0)
    for line in range(KS, TAPS):
        spread[TAPS * line : TAPS * (line + 1), :] = jnp.zeros((TAPS, 128), F32)
    rows = jnp.concatenate([spread[pl.ds(tap, TAPS, stride=TAPS), :] for tap in range(KS)], axis=0)
    high = rows.astype(BF16).astype(F32)
    low = rows - high
    wide = high + pltpu.roll(low, 32, 1) + pltpu.roll(high, 64, 1)
    out = dot(wide.astype(BF16), table[...])
    slots = [None] * SLOTS
    for tap in range(KS):
        part = out[TAPS * tap : TAPS * (tap + 1)]
        value = part[:, 0:128], part[:, 128:256]
        if tap != MARGIN:
            cosine, sine = [jnp.concatenate([turns[i, tap]] * 3, axis=0) for i in range(2)]
            value = turn(value, cosine, sine)
        slot = (tap - MARGIN) % SLOTS
        if slots[slot] is not None:
            value = value[0] + slots[slot][0], value[1] + slots[slot][1]
        slots[slot] = value
    for pair in range(SLOTS // 2):
        one, two = slots[2 * pair], slots[2 * pair + 1]
        real = jnp.concatenate([one[0], two[0]], axis=1)
        imag = jnp.concatenate([one[1], two[1]], axis=1)
        high, low = split(jnp.concatenate([real, imag], axis=0))
        out = dot(table_y_ref[...], jnp.concatenate([high, low, high], axis=0))
        planes_ref[2 * pair] = out[:, 0:128]
        planes_ref[2 * pair + 1] = out[:, 128:256]


def gathered_place(count, distance):
    place, size = 0, 1
    for bits in gather_rounds(count):
        for bit in bits:
            place = place + size * ((distance >> bit) & 1)
            size *= 2
    return place


def spectrum_kernel(update, count, order, lists, blend, cell_row, near, far, table, turns, table_y_ref, out_ref, flat, lines, spread, planes):
    view = order[update]
    own = lax.axis_index("blk")
    half = count // 2
    total = blend[0, 0, view] + blend[0, 1, view]
    value = None
    rows = slice(CELLROWS * update, CELLROWS * (update + 1))
    for k in range(2):
        place = gathered_place(count, cell_row[lists[0, k, view]] ^ own)
        inner = lax.rem(place, half)
        line = jnp.where(place < half, near[inner].astype(F32), far[inner].astype(F32))[rows]
        weight = blend[0, k, view] / total * (2.0 / float(PAD**3))
        part = line * (weight / jnp.sum(line))
        value = part if value is None else value + part
    flat[...] = value
    tap_stage(flat, lines, spread, table, turns, table_y_ref, planes)
    z_stage(planes, out_ref)


def grid_bits(count):
    low_count = count.bit_length() - 2
    bits = [[bit for bit in range(low_count) if bit % 3 == axis] for axis in range(3)]
    bits[2] = [low_count] + bits[2]
    return bits


def gather_rounds(count):
    bits = list(range(count.bit_length() - 1))
    rounds = [bits[:1]]
    bits = bits[1:]
    while bits:
        rounds.append(bits[:2])
        bits = bits[2:]
    return rounds[::-1]


def odd_places(count):
    own = lax.axis_index("blk")
    return [((own >> bits[0]) & 1) == 1 if bits else own < 0 for bits in grid_bits(count)]


def slab_kinds(count):
    return [
        (axis, far)
        for far in (0, 1)
        for axis in (2, 1, 0)
        if len(grid_bits(count)[axis]) > far
    ]


def store_slabs(count, slabs, outs):
    odds = odd_places(count)
    for (axis, far), out in zip(slab_kinds(count), outs):
        low, high = slabs[axis]
        out[...] = jnp.where(odds[axis], high, low) if far else jnp.where(odds[axis], low, high)


def cells_kernel(order, cells, out, got, pad, sems):
    copies = []
    for update in range(UPDATES):
        copies.append(pltpu.make_async_copy(cells.at[order[update]], got.at[update], sems.at[update]))
        copies[-1].start()
    pad[...] = jnp.zeros((1, CELLROWS * 128), F32)
    for update in range(UPDATES):
        copies[update].wait()
        pad[:, 0:KS3] = got[update]
        wide = pad[...]
        rows = [wide[:, 128 * row : 128 * (row + 1)] for row in range(CELLROWS)]
        here = slice(CELLROWS * update, CELLROWS * (update + 1))
        out[here, :] = jnp.concatenate(rows, axis=0).astype(BF16)


def start_kernel(count, est, u_out, *refs):
    outs, (flat, sem) = refs[:-2], refs[-2:]
    copy = pltpu.make_async_copy(est, flat, sem)
    copy.start()
    copy.wait()
    unflatten(lambda row: flat[pl.ds(row, 8, stride=3), :], u_out)
    store_slabs(count, pack_slabs(u_out), outs)


VIEW_PARTS = 3


def views_kernel(order, observed, o0, o1, near, wide, sems):
    part_lanes = FLAT * 128 // VIEW_PARTS
    copies = []
    for part in range(VIEW_PARTS):
        here = pl.ds(part_lanes * part, part_lanes)
        copies.append(pltpu.make_async_copy(observed.at[:, :, here], near.at[:, :, here], sems.at[part]))
        copies[-1].start()
    step_rows = 32
    for part in range(VIEW_PARTS):
        copies[part].wait()

        @pl.loop(0, FLAT // VIEW_PARTS // step_rows)
        def _(step):
            for row in range(step_rows):
                at = part * (FLAT // VIEW_PARTS) + step * step_rows + row
                lanes = pl.ds(pl.multiple_of(at * 128, 128), 128)
                wide[pl.ds(pl.multiple_of(at * 8, 8), VIEWS), :] = near[0, :, lanes].astype(F32)

    for update, out in enumerate((o0, o1)):
        view = order[update]
        unflatten(lambda row: wide[pl.ds(8 * row + view, 8, stride=24), :], out)


def field_stage(count, present, u, slabs, ea, gy, out, high, low, lines):
    found = {kind: slab[...] for kind, slab in zip(slab_kinds(count), slabs)}
    margins = []
    for axis in range(3):
        blank = jnp.zeros(SLABS[axis].shape, BF16)
        margins.append((found.get((axis, 0), blank), found.get((axis, 1), blank)))
    assemble(present, odd_places(count), u, margins, high, low)
    lines_stage(high, low, ea, lines, SLOTS * PAD, 256)
    y_stage(lines, gy, PAD, out)


def divide(value, by):
    guess = pl.reciprocal(by, approx=True)
    guess = guess * (2.0 - by * guess)
    ratio = value * guess
    return ratio + guess * (value - ratio * by)


def wide_terms(value):
    high, low = split(value)
    return jnp.concatenate([high, low, high], axis=1)


STEP = 192


def update_body(tissue, kernel, u, o, tables, planes, lines, new_ref):
    ea, ei, gh, gb, twiddle = tables
    filter_stage(planes, kernel, twiddle, False, planes)
    y_back_stage(planes, gb, lines)
    lane = lane_iota((STEP, LANES))
    valid = (lane % PAD < E) & (lane < 3 * PAD)
    for start in range(0, SLOTS * E, STEP):
        rows = slice(start, start + STEP)
        blurred = dot(wide_terms(lines[rows, :]), ei[...])
        quotient = jnp.where(valid, divide(both_halves(o, rows), blurred), 0.0)
        lines[rows, :] = dot(wide_terms(quotient), ea[...])
    y_stage(lines, gh, E, planes)
    filter_stage(planes, kernel, twiddle, True, planes)
    y_back_stage(planes, gb, lines)
    alive = tissue[0] > 0
    for start in range(0, SLOTS * E, STEP):
        rows = slice(start, start + STEP)
        correction = dot(wide_terms(lines[rows, :]), ei[...])
        for half in range(2):
            core = u[half, rows, :]
            new_ref[half, rows, :] = jnp.where(alive, core * correction[:, 128 * half : 128 * (half + 1)], core)


def first_kernel(count, tissue, present, u, *refs):
    kinds = len(slab_kinds(count))
    slabs, (kernel, o, ea, gy, ei, gh, gb, twiddle, u_out), outs = refs[:kinds], refs[kinds : kinds + 9], refs[kinds + 9 : -4]
    planes, high, low, lines = refs[-4:]
    field_stage(count, present, u, slabs, ea, gy, planes, high, low, lines)
    update_body(tissue, kernel, u, o, (ea, ei, gh, gb, twiddle), planes, lines, u_out)
    store_slabs(count, pack_slabs(u_out), outs)


def last_kernel(count, tissue, present, u, *refs):
    kinds = len(slab_kinds(count))
    slabs, (kernel, o, ea, gy, ei, gh, gb, twiddle, out) = refs[:kinds], refs[kinds : kinds + 9]
    planes, high, low, lines, fresh = refs[-5:]
    field_stage(count, present, u, slabs, ea, gy, planes, high, low, lines)
    update_body(tissue, kernel, u, o, (ea, ei, gh, gb, twiddle), planes, lines, fresh)
    flatten(fresh, out)


VM = pl.BlockSpec(memory_space=pltpu.VMEM)
SM = pl.BlockSpec(memory_space=pltpu.SMEM)
ANY = pl.BlockSpec(memory_space=pl.ANY)
HBM = pl.BlockSpec(memory_space=pltpu.HBM)
PARAMS = pltpu.CompilerParams(vmem_limit_bytes=48 * 1024 * 1024)


def shape(dims, kind=F32):
    return jax.ShapeDtypeStruct(dims, kind)


SLAB = shape((192, 128), BF16)
WIDE_SLAB = shape((256, 128), BF16)
SLABS = [SLAB, WIDE_SLAB, SLAB]
CELLS = shape((UPDATES * CELLROWS, 128), BF16)
ROWS = shape((2, SLOTS * E, 128))
ROWS_V = pltpu.VMEM((2, SLOTS * E, 128), F32)
PLANES = shape((SLOTS, 128, 128))
PLANES_V = pltpu.VMEM((SLOTS, 128, 128), F32)
LINES_V = pltpu.VMEM((SLOTS * PAD, LANES), F32)
TERMS_V = pltpu.VMEM((SLOTS * PAD, LANES), BF16)


def call(body, ins, outs, args, scratch=(), name=None):
    many = isinstance(outs, list)
    return pl.pallas_call(
        body,
        in_specs=ins,
        out_specs=[VM] * len(outs) if many else VM,
        out_shape=outs,
        scratch_shapes=list(scratch),
        compiler_params=PARAMS,
        name=name,
    )(*args)


def far_pairs(count, axis):
    bits = grid_bits(count)[axis]
    extent = 2 ** len(bits)
    pairs = []
    for number in range(count):
        at = sum(((number >> bit) & 1) << level for level, bit in enumerate(bits))
        moved = at + 1 if at % 2 else at - 1
        if 0 <= moved < extent:
            other = number
            for level, bit in enumerate(bits):
                other = other & ~(1 << bit) | ((moved >> level) & 1) << bit
            pairs.append((number, other))
    return pairs


def swap(value, distance, count):
    return lax.ppermute(value, "blk", [(number, number ^ distance) for number in range(count)])


def swap_slabs(slabs, count):
    margins = []
    for (axis, far), slab in zip(slab_kinds(count), slabs):
        if far:
            margins.append(lax.ppermute(slab, "blk", far_pairs(count, axis)))
        else:
            margins.append(swap(slab, 1 << grid_bits(count)[axis][0], count))
    return margins


def local(estimate, observed, psf_cells, tissue, neighbours, psf_list, psf_blend, cell_row, view_order):
    count = lax.axis_size("blk")
    ea = jnp.asarray(stacked(table_space_to_lines(), 0))
    ei = jnp.asarray(stacked(table_lines_to_space(), 0))
    gy = jnp.asarray(stacked(table_y(PAD), 1))
    gh = jnp.asarray(stacked(table_y(E), 1))
    gb = jnp.asarray(stacked(table_y_back(), 1))
    gt = jnp.asarray(stacked(table_y_taps(), 1))
    taps = jnp.asarray(table_taps())
    turns = jnp.asarray(table_tap_turns())
    twiddle = jnp.asarray(table_twiddle())
    lists = jnp.swapaxes(psf_list, 1, 2)
    blend = jnp.swapaxes(psf_blend, 1, 2)

    cells = call(
        cells_kernel,
        [SM, HBM],
        CELLS,
        (view_order, jnp.swapaxes(psf_cells, 0, 1)),
        [
            pltpu.VMEM((UPDATES, 1, KS3), F32),
            pltpu.VMEM((1, CELLROWS * 128), F32),
            pltpu.SemaphoreType.DMA((UPDATES,)),
        ],
        name="cells",
    )
    slab_shapes = [SLABS[axis] for axis, far in slab_kinds(count)]
    rows, *slabs = call(
        functools.partial(start_kernel, count),
        [HBM],
        [ROWS] + slab_shapes,
        (estimate.reshape(FLAT, 128),),
        [pltpu.VMEM((FLAT, 128), F32), pltpu.SemaphoreType.DMA],
        name="start",
    )
    targets = call(
        views_kernel,
        [SM, HBM],
        [ROWS, ROWS],
        (view_order, observed),
        [
            pltpu.VMEM((1, VIEWS, FLAT * 128), BF16),
            pltpu.VMEM((8 * FLAT, 128), F32),
            pltpu.SemaphoreType.DMA((VIEW_PARTS,)),
        ],
        name="views",
    )
    held = cells
    for number, bits in enumerate(gather_rounds(count)[:-1]):
        arrived = [held]
        for part in range(1, 2 ** len(bits)):
            distance = sum(((part >> level) & 1) << bit for level, bit in enumerate(bits))
            arrived.append(swap(held, distance, count))
        if number == 0:
            arrived, rows, slabs = lax.optimization_barrier((arrived, rows, slabs))
        if number == 1:
            arrived, targets, slabs = lax.optimization_barrier((arrived, targets, slabs))
        held = jnp.concatenate(arrived, axis=0)
    margins = swap_slabs(slabs, count)
    other = swap(held, 1, count)
    near_cells, far_cells = [v.reshape(count // 2, UPDATES * CELLROWS, 128) for v in (held, other)]

    def spectrum(update):
        return call(
            functools.partial(spectrum_kernel, update, count),
            [SM] * 4 + [VM] * 5,
            PLANES,
            (view_order, lists, blend, cell_row, near_cells, far_cells, taps, turns, gt),
            [
                pltpu.VMEM((CELLROWS, 128), F32),
                pltpu.VMEM((3, TAPS, 128), F32),
                pltpu.VMEM((TAPS * TAPS, 128), F32),
                PLANES_V,
            ],
            name="spectrum",
        )

    def update(body, outs, number, kernel, rows, margins, scratch, name):
        return call(
            functools.partial(body, count),
            [SM] * 2 + [VM] * (9 + len(slab_shapes)),
            outs,
            (tissue, neighbours, rows, *margins, kernel, targets[number], ea, gy, ei, gh, gb, twiddle),
            [PLANES_V, TERMS_V, TERMS_V, LINES_V] + scratch,
            name=name,
        )

    kernel = spectrum(0)
    kernel, margins = lax.optimization_barrier((kernel, margins))
    rows, *slabs = update(first_kernel, [ROWS] + slab_shapes, 0, kernel, rows, margins, [], "first")
    margins = swap_slabs(slabs, count)
    kernel = spectrum(1)
    kernel, margins = lax.optimization_barrier((kernel, margins))
    out = update(last_kernel, shape((FLAT, 128)), 1, kernel, rows, margins, [ROWS_V], "last")
    return out.reshape(1, FLAT * 128)


def solution(mesh):
    return jax.shard_map(
        local,
        mesh=mesh,
        in_specs=(
            P("blk", None),
            P("blk", None, None),
            P("blk", None, None),
            P("blk"),
            P("blk", None),
            P("blk", None, None),
            P("blk", None, None),
            P(),
            P(),
        ),
        out_specs=P("blk", None),
        check_vma=False,
    )
```

```python
import functools

import numpy as np

import jax
import jax.numpy as jnp
import ml_dtypes
from jax import lax
from jax.experimental import pallas as pl
from jax.experimental.pallas import tpu as pltpu
from jax.sharding import PartitionSpec as P

E = 48
MARGIN = 8
UPDATES = 2
VIEWS = 6
PAD = 64
KS = 17
KS2 = KS * KS
KS3 = 4913
SLOTS = 16
LANES = 256
TAPS = 24
CELLROWS = 40
FLAT = 864

F32 = jnp.float32
BF16 = jnp.bfloat16


def two_terms(table):
    high = table.astype(ml_dtypes.bfloat16)
    low = (table - high.astype(np.float64)).astype(ml_dtypes.bfloat16)
    return high, low


def stacked(table, axis):
    high, low = two_terms(table)
    return np.concatenate([high, high, low], axis=axis)


def x_positions():
    x = np.arange(PAD)
    return np.where(x < PAD - MARGIN, x, x - PAD)


def table_space_to_lines():
    z4, k4, kx = np.arange(4), np.arange(4), np.arange(32)
    angle = -2.0 * np.pi * (
        z4[:, None, None, None] * k4[None, None, :, None] / 4.0
        + (kx[None, None, None, :] + 0.5) * x_positions()[None, :, None, None] / PAD
    )
    angle = angle.reshape(LANES, 128)
    return np.concatenate([np.cos(angle), np.sin(angle)], axis=1)


def table_lines_to_space():
    back = table_space_to_lines().T.copy()
    back = back.reshape(LANES, 4, PAD)
    back[:, 3, :] = 0.0
    back[:, :, E:] = 0.0
    return back.reshape(LANES, LANES)


def complex_rows(angle):
    cosine, sine = np.cos(angle), np.sin(angle)
    return np.concatenate(
        [np.concatenate([cosine, -sine], axis=1), np.concatenate([sine, cosine], axis=1)], axis=0
    )


def table_y(count):
    ky, y = np.arange(PAD), np.arange(count)
    return complex_rows(-2.0 * np.pi * (ky[:, None] * y[None, :] % PAD) / PAD)


def table_y_back():
    ky, y = np.arange(PAD), np.arange(E)
    return complex_rows(2.0 * np.pi * (y[:, None] * ky[None, :] % PAD) / PAD)


def table_y_taps():
    ky, tap = np.arange(PAD), np.arange(TAPS) - MARGIN
    angle = -2.0 * np.pi * ky[:, None] * tap[None, :] / PAD
    return complex_rows(angle)


def table_taps():
    kx, tap = np.arange(32), np.arange(KS) - MARGIN
    angle = -2.0 * np.pi * (kx[None, :] + 0.5) * tap[:, None] / PAD
    full = np.concatenate([np.tile(np.cos(angle), (1, 4)), np.tile(np.sin(angle), (1, 4))], axis=1)
    high, low = two_terms(full)
    table = np.zeros((128, LANES), ml_dtypes.bfloat16)
    for start, term in ((0, high), (32, high), (64, low)):
        table[start : start + KS] = term
    return table


def table_tap_turns():
    k4 = np.repeat(np.arange(4), 32)
    tap = np.arange(KS) - MARGIN
    angle = -2.0 * np.pi * tap[:, None] * k4[None, :] / PAD
    both = np.stack([np.cos(angle), np.sin(angle)], axis=0)
    return np.broadcast_to(both[:, :, None, :], (2, KS, 8, 128)).astype(np.float32)


def table_twiddle():
    k4 = np.repeat(np.arange(4), 32)
    angle = -2.0 * np.pi * np.arange(SLOTS)[:, None] * k4[None, :] / PAD
    both = np.stack([np.cos(angle), np.sin(angle)], axis=0)
    return np.broadcast_to(both[:, :, None, :], (2, SLOTS, 8, 128)).astype(np.float32)


def split(value):
    high = value.astype(BF16)
    low = (value - high.astype(F32)).astype(BF16)
    return high, low


def dot(left, right):
    return jnp.dot(left, right, preferred_element_type=F32)


def both_halves(rows_ref, rows):
    return jnp.concatenate([rows_ref[0, rows, :], rows_ref[1, rows, :]], axis=1)


def lane_iota(shape):
    return lax.broadcasted_iota(jnp.int32, shape, 1)


def cut(pieces, piece, target):
    offset = E * piece
    first, start = offset // 128, offset % 128
    shift = (target - start) % 128
    one = pltpu.roll(pieces[first], shift, 1) if shift else pieces[first]
    if start + E <= 128:
        return one
    two = pltpu.roll(pieces[first + 1], shift, 1) if shift else pieces[first + 1]
    edge = target + 128 - start
    return jnp.where(lane_iota(one.shape) < edge, one, two)


def unflatten(load, out_ref):
    lane = lane_iota((8, 128))
    zero = jnp.zeros((8, 128), F32)
    for block in range(12):
        parts = []
        for z4 in range(3):
            first = 3 * (96 * z4 + 8 * block)
            parts.append([load(first + m) for m in range(3)])
        for piece in range(8):
            low = cut(parts[0], piece, 0)
            mid = cut(parts[1], piece, 64)
            top = cut(parts[2], piece, 0)
            left = jnp.where(lane < E, low, jnp.where(lane < 64, zero, mid))
            left = jnp.where(lane < 64 + E, left, zero)
            rows = pl.ds(64 * block + piece, 8, stride=8)
            out_ref[0, rows, :] = left
            out_ref[1, rows, :] = jnp.where(lane < E, top, zero)


def flatten(rows_ref, flat_ref):
    lane = lane_iota((8, 128))
    for block in range(12):
        found = []
        for piece in range(8):
            rows = pl.ds(64 * block + piece, 8, stride=8)
            found.append((rows_ref[0, rows, :], rows_ref[1, rows, :]))
        for z4 in range(3):
            first = 3 * (96 * z4 + 8 * block)
            out = [None, None, None]
            for piece in range(8):
                value = found[piece][0] if z4 < 2 else found[piece][1]
                source = 64 if z4 == 1 else 0
                offset = E * piece
                spot, start = offset // 128, offset % 128
                shift = (start - source) % 128
                moved = pltpu.roll(value, shift, 1) if shift else value
                if out[spot] is None:
                    out[spot] = moved
                else:
                    out[spot] = jnp.where(lane < start, out[spot], moved)
                if start + E > 128:
                    out[spot + 1] = moved
            for m in range(3):
                flat_ref[pl.ds(first + m, 8, stride=3), :] = out[m]


def x_picks(wide, packed, low_start, high_start):
    place = packed % 128
    start = jnp.where(packed >= 128, high_start, low_start)
    here = (wide // PAD == place // MARGIN) & (wide % PAD == start + place % MARGIN) & (place < 3 * MARGIN)
    return jnp.where(here, 1.0, 0.0).astype(BF16)


def both_iotas():
    dims = (LANES, LANES)
    return lax.broadcasted_iota(jnp.int32, dims, 0), lax.broadcasted_iota(jnp.int32, dims, 1)


def pack_slabs(rows_ref):
    high = both_halves(rows_ref, slice(None)).astype(BF16)
    rows, columns = both_iotas()
    found = dot(high, x_picks(rows, columns, 0, E - MARGIN))
    faces = []
    for face in range(2):
        value = found[0:192, 128 * face : 128 * (face + 1)]
        for group in range(1, 4):
            part = found[192 * group : 192 * (group + 1), 128 * face : 128 * (face + 1)]
            value = value + pltpu.roll(part, 32 * group, 1)
        faces.append(value.astype(BF16))
    x0, x1 = faces
    low_rows, high_rows = [], []
    for slot in range(SLOTS):
        low_rows.append(both_halves(rows_ref, slice(E * slot, E * slot + MARGIN)))
        high_rows.append(both_halves(rows_ref, slice(E * slot + E - MARGIN, E * (slot + 1))))
    y0, y1 = jnp.concatenate(low_rows, axis=0), jnp.concatenate(high_rows, axis=0)
    y0, y1 = [jnp.concatenate([v[:, 0:128], v[:, 128:256]], axis=0).astype(BF16) for v in (y0, y1)]
    lane = lane_iota((192, 128))
    first = rows_ref[0, 0:192, :]
    second = pltpu.roll(rows_ref[0, 192:384, :], 64, 1)
    z0 = jnp.where(lane < 64, first, second).astype(BF16)
    first = rows_ref[1, 384:576, :]
    second = pltpu.roll(rows_ref[1, 576:768, :], 64, 1)
    z1 = jnp.where(lane < 64, first, second).astype(BF16)
    return (z0, z1), (y0, y1), (x0, x1)


def sort_margins(present, odd, axis, pair):
    on = [present[0, 2 * axis + side] >= 0 for side in range(2)]
    pair = [value.astype(F32) for value in pair]
    low = jnp.where(odd, pair[0], pair[1])
    high = jnp.where(odd, pair[1], pair[0])
    zero = jnp.zeros_like(low)
    return jnp.where(on[0], low, zero), jnp.where(on[1], high, zero)


def assemble(present, odds, rows_ref, margins, high_ref, low_ref):
    (zm, zp), (ym, yp), (xm, xp) = [
        sort_margins(present, odds[axis], axis, margins[axis]) for axis in range(3)
    ]
    rows, columns = both_iotas()
    picks = x_picks(columns, rows, PAD - MARGIN, E)
    parts = []
    for group in range(4):
        pair = [pltpu.roll(v, 128 - 32 * group, 1) if group else v for v in (xm, xp)]
        parts.append(jnp.concatenate(pair, axis=1))
    side = dot(jnp.concatenate(parts, axis=0).astype(BF16), picks)
    ym_rows, yp_rows = [jnp.concatenate([v[0:128], v[128:256]], axis=1) for v in (ym, yp)]
    z_sides = []
    for value in (zp, zm):
        z_sides.append(pltpu.roll(value, 64, 1))
        z_sides.append(value)
    lane = lane_iota((E, 128))
    for slot in range(SLOTS):
        group, inner = slot // 4, slot % 4
        core = both_halves(rows_ref, slice(E * slot, E * (slot + 1)))
        high, low = split(core)
        added = side[E * slot : E * (slot + 1)]
        full = high.astype(F32) + added
        z_side = z_sides[group][E * inner : E * (inner + 1), :]
        right = jnp.where(lane < 64, full[:, 128:256], z_side)
        high_ref[PAD * slot : PAD * slot + E, 0:128] = full[:, 0:128].astype(BF16)
        high_ref[PAD * slot : PAD * slot + E, 128:256] = right.astype(BF16)
        rows = slice(MARGIN * slot, MARGIN * (slot + 1))
        outer = jnp.concatenate([yp_rows[rows], ym_rows[rows]], axis=0)
        high_ref[PAD * slot + E : PAD * (slot + 1), :] = outer.astype(BF16)
        low_ref[PAD * slot : PAD * slot + E, :] = low
        low_ref[PAD * slot + E : PAD * (slot + 1), :] = jnp.zeros((PAD - E, LANES), BF16)


def lines_stage(high, low, table, out_ref, rows, step):
    for start in range(0, rows, step):
        part = slice(start, start + step)
        wide = jnp.concatenate([high[part, :], low[part, :], high[part, :]], axis=1)
        out_ref[part, :] = dot(wide, table[...])


def y_stage(lines_ref, table, count, out_ref):
    for pair in range(SLOTS // 2):
        one = lines_ref[count * 2 * pair : count * (2 * pair + 1), :]
        two = lines_ref[count * (2 * pair + 1) : count * (2 * pair + 2), :]
        real = jnp.concatenate([one[:, 0:128], two[:, 0:128]], axis=1)
        imag = jnp.concatenate([one[:, 128:256], two[:, 128:256]], axis=1)
        high, low = split(jnp.concatenate([real, imag], axis=0))
        out = dot(table[...], jnp.concatenate([high, low, high], axis=0))
        out_ref[2 * pair] = out[:, 0:128]
        out_ref[2 * pair + 1] = out[:, 128:256]


def y_back_stage(planes_ref, table, out_ref):
    for pair in range(SLOTS // 2):
        both = jnp.concatenate([planes_ref[2 * pair], planes_ref[2 * pair + 1]], axis=1)
        high, low = split(both)
        out = dot(table[...], jnp.concatenate([high, low, high], axis=0))
        for which in range(2):
            rows = slice(E * (2 * pair + which), E * (2 * pair + which + 1))
            lanes = slice(128 * which, 128 * (which + 1))
            out_ref[rows, 0:128] = out[0:E, lanes]
            out_ref[rows, 128:256] = out[E : 2 * E, lanes]


def turn(value, cosine, sine):
    real, imag = value
    return real * cosine - imag * sine, real * sine + imag * cosine


def dft4(values, sign):
    (ar, ai), (br, bi), (cr, ci), (dr, di) = values
    sr, si, mr, mi = ar + cr, ai + ci, ar - cr, ai - ci
    pr, pi, qr, qi = br + dr, bi + di, br - dr, bi - di
    if sign > 0:
        first, third = (mr - qi, mi + qr), (mr + qi, mi - qr)
    else:
        first, third = (mr + qi, mi - qr), (mr - qi, mi + qr)
    return [(sr + pr, si + pi), first, (sr - pr, si - pi), third]


def dft16(values, sign):
    inner = []
    for low in range(4):
        line = dft4([values[4 * top + low] for top in range(4)], sign)
        moved = []
        for k in range(4):
            turns = low * k
            real, imag = line[k]
            if turns == 0:
                moved.append((real, imag))
            elif turns == 4:
                moved.append((-imag, real) if sign > 0 else (imag, -real))
            elif turns in (2, 6):
                root = float(np.sqrt(0.5))
                a, b = root * real, root * imag
                if turns == 2:
                    moved.append((a - b, a + b) if sign > 0 else (a + b, b - a))
                else:
                    moved.append((-a - b, a - b) if sign > 0 else (b - a, -a - b))
            else:
                angle = sign * 2.0 * np.pi * turns / SLOTS
                moved.append(turn((real, imag), float(np.cos(angle)), float(np.sin(angle))))
        inner.append(moved)
    out = [None] * SLOTS
    for k in range(4):
        line = dft4([inner[low][k] for low in range(4)], sign)
        for top in range(4):
            out[k + 4 * top] = line[top]
    return out


def z_forward(planes_ref, twiddle, rows, rows_imag):
    values = []
    for slot in range(SLOTS):
        value = (planes_ref[slot, rows, :], planes_ref[slot, rows_imag, :])
        if slot:
            value = turn(value, twiddle[0, slot], twiddle[1, slot])
        values.append(value)
    return dft16(values, -1)


def z_stage(planes_ref, out_ref):
    @pl.loop(0, PAD // 8, unroll=2)
    def _(step):
        rows = pl.ds(pl.multiple_of(8 * step, 8), 8)
        rows_imag = pl.ds(pl.multiple_of(8 * step + PAD, 8), 8)
        values = [(planes_ref[slot, rows, :], planes_ref[slot, rows_imag, :]) for slot in range(SLOTS)]
        values = dft16(values, -1)
        for slot in range(SLOTS):
            out_ref[slot, rows, :] = values[slot][0]
            out_ref[slot, rows_imag, :] = values[slot][1]


def filter_stage(planes_ref, kernel_ref, twiddle, conjugate, out_ref):
    @pl.loop(0, PAD // 8, unroll=2)
    def _(step):
        rows = pl.ds(pl.multiple_of(8 * step, 8), 8)
        rows_imag = pl.ds(pl.multiple_of(8 * step + PAD, 8), 8)
        values = z_forward(planes_ref, twiddle, rows, rows_imag)
        for slot in range(SLOTS):
            cosine, sine = kernel_ref[slot, rows, :], kernel_ref[slot, rows_imag, :]
            if conjugate:
                real, imag = values[slot]
                values[slot] = (real * cosine + imag * sine, imag * cosine - real * sine)
            else:
                values[slot] = turn(values[slot], cosine, sine)
        values = dft16(values, 1)
        for slot in range(SLOTS):
            real, imag = values[slot]
            if slot:
                cosine, sine = twiddle[0, slot], twiddle[1, slot]
                real, imag = real * cosine + imag * sine, imag * cosine - real * sine
            out_ref[slot, rows, :] = real
            out_ref[slot, rows_imag, :] = imag


def tap_stage(flat_ref, lines, spread, table, turns, table_y_ref, planes_ref):
    lane = lane_iota((3, 128))
    for tap in range(KS):
        row, start = KS2 * tap // 128, KS2 * tap % 128
        value = flat_ref[row : row + 3, :]
        if start:
            value = pltpu.roll(value, 128 - start, 1)
            after = pltpu.roll(flat_ref[row + 1 : row + 4, :], 128 - start, 1)
            value = jnp.where(lane < 128 - start, value, after)
        for part in range(3):
            lines[part, tap : tap + 1, :] = value[part : part + 1]
    lane = lane_iota((TAPS, 128))
    for line in range(KS):
        part, start = KS * line // 128, KS * line % 128
        value = lines[part]
        if start:
            value = pltpu.roll(value, 128 - start, 1)
            if start + KS > 128:
                after = pltpu.roll(lines[part + 1], 128 - start, 1)
                value = jnp.where(lane < 128 - start, value, after)
        spread[TAPS * line : TAPS * (line + 1), :] = jnp.where(lane < KS, value, 0.0)
    for line in range(KS, TAPS):
        spread[TAPS * line : TAPS * (line + 1), :] = jnp.zeros((TAPS, 128), F32)
    rows = jnp.concatenate([spread[pl.ds(tap, TAPS, stride=TAPS), :] for tap in range(KS)], axis=0)
    high = rows.astype(BF16).astype(F32)
    low = rows - high
    wide = high + pltpu.roll(low, 32, 1) + pltpu.roll(high, 64, 1)
    out = dot(wide.astype(BF16), table[...])
    slots = [None] * SLOTS
    for tap in range(KS):
        part = out[TAPS * tap : TAPS * (tap + 1)]
        value = part[:, 0:128], part[:, 128:256]
        if tap != MARGIN:
            cosine, sine = [jnp.concatenate([turns[i, tap]] * 3, axis=0) for i in range(2)]
            value = turn(value, cosine, sine)
        slot = (tap - MARGIN) % SLOTS
        if slots[slot] is not None:
            value = value[0] + slots[slot][0], value[1] + slots[slot][1]
        slots[slot] = value
    for pair in range(SLOTS // 2):
        one, two = slots[2 * pair], slots[2 * pair + 1]
        real = jnp.concatenate([one[0], two[0]], axis=1)
        imag = jnp.concatenate([one[1], two[1]], axis=1)
        high, low = split(jnp.concatenate([real, imag], axis=0))
        out = dot(table_y_ref[...], jnp.concatenate([high, low, high], axis=0))
        planes_ref[2 * pair] = out[:, 0:128]
        planes_ref[2 * pair + 1] = out[:, 128:256]


def gathered_place(count, distance):
    place, size = 0, 1
    for bits in gather_rounds(count):
        for bit in bits:
            place = place + size * ((distance >> bit) & 1)
            size *= 2
    return place


def spectrum_kernel(update, count, order, lists, blend, cell_row, near, far, table, turns, table_y_ref, out_ref, flat, lines, spread, planes):
    view = order[update]
    own = lax.axis_index("blk")
    half = count // 2
    total = blend[0, 0, view] + blend[0, 1, view]
    value = None
    rows = slice(CELLROWS * update, CELLROWS * (update + 1))
    for k in range(2):
        place = gathered_place(count, cell_row[lists[0, k, view]] ^ own)
        inner = lax.rem(place, half)
        line = jnp.where(place < half, near[inner].astype(F32), far[inner].astype(F32))[rows]
        weight = blend[0, k, view] / total * (2.0 / float(PAD**3))
        part = line * (weight / jnp.sum(line))
        value = part if value is None else value + part
    flat[...] = value
    tap_stage(flat, lines, spread, table, turns, table_y_ref, planes)
    z_stage(planes, out_ref)


def grid_bits(count):
    low_count = count.bit_length() - 2
    bits = [[bit for bit in range(low_count) if bit % 3 == axis] for axis in range(3)]
    bits[2] = [low_count] + bits[2]
    return bits


def gather_rounds(count):
    bits = list(range(count.bit_length() - 1))
    rounds = [bits[:1]]
    bits = bits[1:]
    while bits:
        rounds.append(bits[:2])
        bits = bits[2:]
    return rounds[::-1]


def odd_places(count):
    own = lax.axis_index("blk")
    return [((own >> bits[0]) & 1) == 1 if bits else own < 0 for bits in grid_bits(count)]


def slab_kinds(count):
    return [
        (axis, far)
        for far in (0, 1)
        for axis in (2, 1, 0)
        if len(grid_bits(count)[axis]) > far
    ]


def store_slabs(count, slabs, outs):
    odds = odd_places(count)
    for (axis, far), out in zip(slab_kinds(count), outs):
        low, high = slabs[axis]
        out[...] = jnp.where(odds[axis], high, low) if far else jnp.where(odds[axis], low, high)


def cells_kernel(order, cells, out, got, pad, sems):
    copies = []
    for update in range(UPDATES):
        copies.append(pltpu.make_async_copy(cells.at[order[update]], got.at[update], sems.at[update]))
        copies[-1].start()
    pad[...] = jnp.zeros((1, CELLROWS * 128), F32)
    for update in range(UPDATES):
        copies[update].wait()
        pad[:, 0:KS3] = got[update]
        wide = pad[...]
        rows = [wide[:, 128 * row : 128 * (row + 1)] for row in range(CELLROWS)]
        here = slice(CELLROWS * update, CELLROWS * (update + 1))
        out[here, :] = jnp.concatenate(rows, axis=0).astype(BF16)


def start_kernel(count, est, u_out, *refs):
    outs, (flat, sem) = refs[:-2], refs[-2:]
    copy = pltpu.make_async_copy(est, flat, sem)
    copy.start()
    copy.wait()
    unflatten(lambda row: flat[pl.ds(row, 8, stride=3), :], u_out)
    store_slabs(count, pack_slabs(u_out), outs)


VIEW_PARTS = 9


def views_kernel(order, observed, o0, o1, near, wide, sems):
    part_rows = FLAT // VIEW_PARTS
    copies = []
    for part in range(VIEW_PARTS):
        here = pl.ds(part_rows * 128 * part, part_rows * 128)
        copies.append(pltpu.make_async_copy(observed.at[:, :, here], near.at[:, :, here], sems.at[part]))
        copies[-1].start()
    step_rows = 32
    for part in range(VIEW_PARTS):
        copies[part].wait()

        @pl.loop(0, part_rows // step_rows)
        def _(step):
            first = part * part_rows + step * step_rows
            lanes = pl.ds(pl.multiple_of(first * 128, 128), step_rows * 128)
            value = near[0, :, lanes].astype(F32)
            value = jnp.concatenate([value, value[0 : 8 - VIEWS]], axis=0)
            for row in range(step_rows):
                rows = pl.ds(pl.multiple_of((first + row) * 8, 8), 8)
                wide[rows, :] = value[:, 128 * row : 128 * (row + 1)]

    for update, out in enumerate((o0, o1)):
        view = order[update]
        unflatten(lambda row: wide[pl.ds(8 * row + view, 8, stride=24), :], out)


def field_stage(count, present, u, slabs, ea, gy, out, high, low, lines):
    found = {kind: slab[...] for kind, slab in zip(slab_kinds(count), slabs)}
    margins = []
    for axis in range(3):
        blank = jnp.zeros(SLABS[axis].shape, BF16)
        margins.append((found.get((axis, 0), blank), found.get((axis, 1), blank)))
    assemble(present, odd_places(count), u, margins, high, low)
    lines_stage(high, low, ea, lines, SLOTS * PAD, 256)
    y_stage(lines, gy, PAD, out)


def wide_terms(value):
    high, low = split(value)
    return jnp.concatenate([high, low, high], axis=1)


STEP = 192


def update_body(tissue, kernel, u, o, tables, planes, lines, new_ref):
    ea, ei, gh, gb, twiddle = tables
    filter_stage(planes, kernel, twiddle, False, planes)
    y_back_stage(planes, gb, lines)
    lane = lane_iota((STEP, LANES))
    valid = (lane % PAD < E) & (lane < 3 * PAD)
    for start in range(0, SLOTS * E, STEP):
        rows = slice(start, start + STEP)
        blurred = dot(wide_terms(lines[rows, :]), ei[...])
        quotient = jnp.where(valid, both_halves(o, rows) / blurred, 0.0)
        lines[rows, :] = dot(wide_terms(quotient), ea[...])
    y_stage(lines, gh, E, planes)
    filter_stage(planes, kernel, twiddle, True, planes)
    y_back_stage(planes, gb, lines)
    alive = tissue[0] > 0
    for start in range(0, SLOTS * E, STEP):
        rows = slice(start, start + STEP)
        correction = dot(wide_terms(lines[rows, :]), ei[...])
        for half in range(2):
            core = u[half, rows, :]
            new_ref[half, rows, :] = jnp.where(alive, core * correction[:, 128 * half : 128 * (half + 1)], core)


def first_kernel(count, tissue, present, u, *refs):
    kinds = len(slab_kinds(count))
    slabs, (kernel, o, ea, gy, ei, gh, gb, twiddle, u_out), outs = refs[:kinds], refs[kinds : kinds + 9], refs[kinds + 9 : -4]
    planes, high, low, lines = refs[-4:]
    field_stage(count, present, u, slabs, ea, gy, planes, high, low, lines)
    update_body(tissue, kernel, u, o, (ea, ei, gh, gb, twiddle), planes, lines, u_out)
    store_slabs(count, pack_slabs(u_out), outs)


def last_kernel(count, tissue, present, u, *refs):
    kinds = len(slab_kinds(count))
    slabs, (kernel, o, ea, gy, ei, gh, gb, twiddle, out) = refs[:kinds], refs[kinds : kinds + 9]
    planes, high, low, lines, fresh = refs[-5:]
    field_stage(count, present, u, slabs, ea, gy, planes, high, low, lines)
    update_body(tissue, kernel, u, o, (ea, ei, gh, gb, twiddle), planes, lines, fresh)
    flatten(fresh, out)


VM = pl.BlockSpec(memory_space=pltpu.VMEM)
SM = pl.BlockSpec(memory_space=pltpu.SMEM)
ANY = pl.BlockSpec(memory_space=pl.ANY)
HBM = pl.BlockSpec(memory_space=pltpu.HBM)
PARAMS = pltpu.CompilerParams(vmem_limit_bytes=48 * 1024 * 1024)


def shape(dims, kind=F32):
    return jax.ShapeDtypeStruct(dims, kind)


SLAB = shape((192, 128), BF16)
WIDE_SLAB = shape((256, 128), BF16)
SLABS = [SLAB, WIDE_SLAB, SLAB]
CELLS = shape((UPDATES * CELLROWS, 128), BF16)
ROWS = shape((2, SLOTS * E, 128))
ROWS_V = pltpu.VMEM((2, SLOTS * E, 128), F32)
PLANES = shape((SLOTS, 128, 128))
PLANES_V = pltpu.VMEM((SLOTS, 128, 128), F32)
LINES_V = pltpu.VMEM((SLOTS * PAD, LANES), F32)
TERMS_V = pltpu.VMEM((SLOTS * PAD, LANES), BF16)


def call(body, ins, outs, args, scratch=(), name=None):
    many = isinstance(outs, list)
    return pl.pallas_call(
        body,
        in_specs=ins,
        out_specs=[VM] * len(outs) if many else VM,
        out_shape=outs,
        scratch_shapes=list(scratch),
        compiler_params=PARAMS,
        name=name,
    )(*args)


def far_pairs(count, axis):
    bits = grid_bits(count)[axis]
    extent = 2 ** len(bits)
    pairs = []
    for number in range(count):
        at = sum(((number >> bit) & 1) << level for level, bit in enumerate(bits))
        moved = (at + 1 if at % 2 else at - 1) % extent
        other = number
        for level, bit in enumerate(bits):
            other = other & ~(1 << bit) | ((moved >> level) & 1) << bit
        pairs.append((number, other))
    return pairs


def swap(value, distance, count):
    return lax.ppermute(value, "blk", [(number, number ^ distance) for number in range(count)])


def swap_slab(kind, slab, count):
    axis, far = kind
    if far:
        return lax.ppermute(slab, "blk", far_pairs(count, axis))
    return swap(slab, 1 << grid_bits(count)[axis][0], count)


def swap_slabs(slabs, count):
    return [swap_slab(kind, slab, count) for kind, slab in zip(slab_kinds(count), slabs)]


def local(estimate, observed, psf_cells, tissue, neighbours, psf_list, psf_blend, cell_row, view_order):
    count = lax.axis_size("blk")
    ea = jnp.asarray(stacked(table_space_to_lines(), 0))
    ei = jnp.asarray(stacked(table_lines_to_space(), 0))
    gy = jnp.asarray(stacked(table_y(PAD), 1))
    gh = jnp.asarray(stacked(table_y(E), 1))
    gb = jnp.asarray(stacked(table_y_back(), 1))
    gt = jnp.asarray(stacked(table_y_taps(), 1))
    taps = jnp.asarray(table_taps())
    turns = jnp.asarray(table_tap_turns())
    twiddle = jnp.asarray(table_twiddle())
    lists = jnp.swapaxes(psf_list, 1, 2)
    blend = jnp.swapaxes(psf_blend, 1, 2)

    cells = call(
        cells_kernel,
        [SM, HBM],
        CELLS,
        (view_order, pltpu.with_memory_space_constraint(jnp.swapaxes(psf_cells, 0, 1), pltpu.HBM)),
        [
            pltpu.VMEM((UPDATES, 1, KS3), F32),
            pltpu.VMEM((1, CELLROWS * 128), F32),
            pltpu.SemaphoreType.DMA((UPDATES,)),
        ],
        name="cells",
    )
    slab_shapes = [SLABS[axis] for axis, far in slab_kinds(count)]
    rows, *slabs = call(
        functools.partial(start_kernel, count),
        [HBM],
        [ROWS] + slab_shapes,
        (pltpu.with_memory_space_constraint(estimate.reshape(FLAT, 128), pltpu.HBM),),
        [pltpu.VMEM((FLAT, 128), F32), pltpu.SemaphoreType.DMA],
        name="start",
    )
    targets = call(
        views_kernel,
        [SM, HBM],
        [ROWS, ROWS],
        (view_order, pltpu.with_memory_space_constraint(observed, pltpu.HBM)),
        [
            pltpu.VMEM((1, VIEWS, FLAT * 128), BF16),
            pltpu.VMEM((8 * FLAT, 128), F32),
            pltpu.SemaphoreType.DMA((VIEW_PARTS,)),
        ],
        name="views",
    )
    held = cells
    for number, bits in enumerate(gather_rounds(count)[:-1]):
        arrived = [held]
        for part in range(1, 2 ** len(bits)):
            distance = sum(((part >> level) & 1) << bit for level, bit in enumerate(bits))
            arrived.append(swap(held, distance, count))
        if number == 0:
            arrived, rows, slabs = lax.optimization_barrier((arrived, rows, slabs))
        if number == 1:
            kinds = slab_kinds(count)
            far = [swap_slab(kind, slab, count) if kind[1] else None for kind, slab in zip(kinds, slabs)]
            arrived, far, targets = lax.optimization_barrier((arrived, far, targets))
        held = jnp.concatenate(arrived, axis=0)
    margins = [swap_slab(kind, slab, count) if done is None else done for kind, slab, done in zip(kinds, slabs, far)]
    other = swap(held, 1, count)
    near_cells, far_cells = [v.reshape(count // 2, UPDATES * CELLROWS, 128) for v in (held, other)]

    def spectrum(update):
        return call(
            functools.partial(spectrum_kernel, update, count),
            [SM] * 4 + [VM] * 5,
            PLANES,
            (view_order, lists, blend, cell_row, near_cells, far_cells, taps, turns, gt),
            [
                pltpu.VMEM((CELLROWS, 128), F32),
                pltpu.VMEM((3, TAPS, 128), F32),
                pltpu.VMEM((TAPS * TAPS, 128), F32),
                PLANES_V,
            ],
            name="spectrum",
        )

    def update(body, outs, number, kernel, rows, margins, scratch, name):
        return call(
            functools.partial(body, count),
            [SM] * 2 + [VM] * (9 + len(slab_shapes)),
            outs,
            (tissue, neighbours, rows, *margins, kernel, targets[number], ea, gy, ei, gh, gb, twiddle),
            [PLANES_V, TERMS_V, TERMS_V, LINES_V] + scratch,
            name=name,
        )

    kernel = spectrum(0)
    kernel, margins = lax.optimization_barrier((kernel, margins))
    rows, *slabs = update(first_kernel, [ROWS] + slab_shapes, 0, kernel, rows, margins, [], "first")
    margins = swap_slabs(slabs, count)
    kernel = spectrum(1)
    kernel, margins = lax.optimization_barrier((kernel, margins))
    out = update(last_kernel, shape((FLAT, 128)), 1, kernel, rows, margins, [ROWS_V], "last")
    return out.reshape(1, FLAT * 128)


def solution(mesh):
    return jax.shard_map(
        local,
        mesh=mesh,
        in_specs=(
            P("blk", None),
            P("blk", None, None),
            P("blk", None, None),
            P("blk"),
            P("blk", None),
            P("blk", None, None),
            P("blk", None, None),
            P(),
            P(),
        ),
        out_specs=P("blk", None),
        check_vma=False,
    )
```

```python
import functools

import numpy as np

import jax
import jax.numpy as jnp
import ml_dtypes
from jax import lax
from jax.experimental import pallas as pl
from jax.experimental.pallas import tpu as pltpu
from jax.sharding import PartitionSpec as P

E = 48
MARGIN = 8
UPDATES = 2
VIEWS = 6
PAD = 64
KS = 17
KS2 = KS * KS
KS3 = 4913
SLOTS = 16
LANES = 256
TAPS = 24
CELLROWS = 40
FLAT = 864

F32 = jnp.float32
BF16 = jnp.bfloat16


def two_terms(table):
    high = table.astype(ml_dtypes.bfloat16)
    low = (table - high.astype(np.float64)).astype(ml_dtypes.bfloat16)
    return high, low


def stacked(table, axis):
    high, low = two_terms(table)
    return np.concatenate([high, high, low], axis=axis)


def x_positions():
    x = np.arange(PAD)
    return np.where(x < PAD - MARGIN, x, x - PAD)


def table_space_to_lines():
    z4, k4, kx = np.arange(4), np.arange(4), np.arange(32)
    angle = -2.0 * np.pi * (
        z4[:, None, None, None] * k4[None, None, :, None] / 4.0
        + (kx[None, None, None, :] + 0.5) * x_positions()[None, :, None, None] / PAD
    )
    angle = angle.reshape(LANES, 128)
    return np.concatenate([np.cos(angle), np.sin(angle)], axis=1)


def table_lines_to_space():
    back = table_space_to_lines().T.copy()
    back = back.reshape(LANES, 4, PAD)
    back[:, 3, :] = 0.0
    back[:, :, E:] = 0.0
    return back.reshape(LANES, LANES)


def complex_rows(angle):
    cosine, sine = np.cos(angle), np.sin(angle)
    return np.concatenate(
        [np.concatenate([cosine, -sine], axis=1), np.concatenate([sine, cosine], axis=1)], axis=0
    )


def table_y(count):
    ky, y = np.arange(PAD), np.arange(count)
    return complex_rows(-2.0 * np.pi * (ky[:, None] * y[None, :] % PAD) / PAD)


def table_y_back():
    ky, y = np.arange(PAD), np.arange(E)
    return complex_rows(2.0 * np.pi * (y[:, None] * ky[None, :] % PAD) / PAD)


def table_y_taps():
    ky, tap = np.arange(PAD), np.arange(TAPS) - MARGIN
    angle = -2.0 * np.pi * ky[:, None] * tap[None, :] / PAD
    return complex_rows(angle)


def table_taps():
    kx, tap = np.arange(32), np.arange(KS) - MARGIN
    angle = -2.0 * np.pi * (kx[None, :] + 0.5) * tap[:, None] / PAD
    full = np.concatenate([np.tile(np.cos(angle), (1, 4)), np.tile(np.sin(angle), (1, 4))], axis=1)
    high, low = two_terms(full)
    table = np.zeros((128, LANES), ml_dtypes.bfloat16)
    for start, term in ((0, high), (32, high), (64, low)):
        table[start : start + KS] = term
    return table


def table_tap_turns():
    k4 = np.repeat(np.arange(4), 32)
    tap = np.arange(KS) - MARGIN
    angle = -2.0 * np.pi * tap[:, None] * k4[None, :] / PAD
    both = np.stack([np.cos(angle), np.sin(angle)], axis=0)
    return np.broadcast_to(both[:, :, None, :], (2, KS, 8, 128)).astype(np.float32)


def table_twiddle():
    k4 = np.repeat(np.arange(4), 32)
    angle = -2.0 * np.pi * np.arange(SLOTS)[:, None] * k4[None, :] / PAD
    both = np.stack([np.cos(angle), np.sin(angle)], axis=0)
    return np.broadcast_to(both[:, :, None, :], (2, SLOTS, 8, 128)).astype(np.float32)


def split(value):
    high = value.astype(BF16)
    low = (value - high.astype(F32)).astype(BF16)
    return high, low


def dot(left, right):
    return jnp.dot(left, right, preferred_element_type=F32)


def both_halves(rows_ref, rows):
    return jnp.concatenate([rows_ref[0, rows, :], rows_ref[1, rows, :]], axis=1)


def lane_iota(shape):
    return lax.broadcasted_iota(jnp.int32, shape, 1)


def cut(pieces, piece, target):
    offset = E * piece
    first, start = offset // 128, offset % 128
    shift = (target - start) % 128
    one = pltpu.roll(pieces[first], shift, 1) if shift else pieces[first]
    if start + E <= 128:
        return one
    two = pltpu.roll(pieces[first + 1], shift, 1) if shift else pieces[first + 1]
    edge = target + 128 - start
    return jnp.where(lane_iota(one.shape) < edge, one, two)


def unflatten(load, out_ref):
    lane = lane_iota((8, 128))
    zero = jnp.zeros((8, 128), F32)
    for block in range(12):
        parts = []
        for z4 in range(3):
            first = 3 * (96 * z4 + 8 * block)
            parts.append([load(first + m) for m in range(3)])
        for piece in range(8):
            low = cut(parts[0], piece, 0)
            mid = cut(parts[1], piece, 64)
            top = cut(parts[2], piece, 0)
            left = jnp.where(lane < E, low, jnp.where(lane < 64, zero, mid))
            left = jnp.where(lane < 64 + E, left, zero)
            rows = pl.ds(64 * block + piece, 8, stride=8)
            out_ref[0, rows, :] = left
            out_ref[1, rows, :] = jnp.where(lane < E, top, zero)


def flatten(rows_ref, flat_ref):
    lane = lane_iota((8, 128))
    for block in range(12):
        found = []
        for piece in range(8):
            rows = pl.ds(64 * block + piece, 8, stride=8)
            found.append((rows_ref[0, rows, :], rows_ref[1, rows, :]))
        for z4 in range(3):
            first = 3 * (96 * z4 + 8 * block)
            out = [None, None, None]
            for piece in range(8):
                value = found[piece][0] if z4 < 2 else found[piece][1]
                source = 64 if z4 == 1 else 0
                offset = E * piece
                spot, start = offset // 128, offset % 128
                shift = (start - source) % 128
                moved = pltpu.roll(value, shift, 1) if shift else value
                if out[spot] is None:
                    out[spot] = moved
                else:
                    out[spot] = jnp.where(lane < start, out[spot], moved)
                if start + E > 128:
                    out[spot + 1] = moved
            for m in range(3):
                flat_ref[pl.ds(first + m, 8, stride=3), :] = out[m]


def squeeze(pieces):
    out = [None, None, None]
    for piece, value in enumerate(pieces):
        spot, start = E * piece // 128, E * piece % 128
        moved = pltpu.roll(value, start, 1) if start else value
        out[spot] = moved if out[spot] is None else jnp.where(lane_iota(moved.shape) < start, out[spot], moved)
        if start + E > 128:
            out[spot + 1] = moved
    return out


def stretch(full):
    return [cut(full, piece, 0) for piece in range(8)]


def pack_x_side(value):
    last = value[144:192]
    lane = lane_iota(last.shape)
    out = []
    for part in range(3):
        moved = pltpu.roll(last, (96 - 32 * part) % 128, 1)
        out.append(jnp.where(lane < 96, value[48 * part : 48 * (part + 1)], moved))
    return jnp.concatenate(out, axis=0)


def unpack_x_side(value):
    parts = [value[48 * part : 48 * (part + 1)] for part in range(3)]
    lane = lane_iota(parts[0].shape)
    last = pltpu.roll(parts[0], 32, 1)
    for part in range(1, 3):
        last = jnp.where(lane < 32 * part, last, pltpu.roll(parts[part], (32 + 32 * part) % 128, 1))
    return jnp.concatenate(parts + [last], axis=0)


def pack_z_side(blocks):
    return jnp.concatenate(squeeze(blocks), axis=0)


def unpack_z_side(value):
    return stretch([value[48 * part : 48 * (part + 1)] for part in range(3)])


def x_picks(wide, packed, low_start, high_start):
    place = packed % 128
    start = jnp.where(packed >= 128, high_start, low_start)
    here = (wide // PAD == place // MARGIN) & (wide % PAD == start + place % MARGIN) & (place < 3 * MARGIN)
    return jnp.where(here, 1.0, 0.0).astype(BF16)


def both_iotas():
    dims = (LANES, LANES)
    return lax.broadcasted_iota(jnp.int32, dims, 0), lax.broadcasted_iota(jnp.int32, dims, 1)


def pack_slabs(rows_ref):
    high = both_halves(rows_ref, slice(None)).astype(BF16)
    rows, columns = both_iotas()
    found = dot(high, x_picks(rows, columns, 0, E - MARGIN))
    faces = []
    for face in range(2):
        value = found[0:192, 128 * face : 128 * (face + 1)]
        for group in range(1, 4):
            part = found[192 * group : 192 * (group + 1), 128 * face : 128 * (face + 1)]
            value = value + pltpu.roll(part, 3 * MARGIN * group, 1)
        faces.append(pack_x_side(value).astype(BF16))
    x0, x1 = faces
    low_rows, high_rows = [], []
    for slot in range(SLOTS):
        low_rows.append(both_halves(rows_ref, slice(E * slot, E * slot + MARGIN)))
        high_rows.append(both_halves(rows_ref, slice(E * slot + E - MARGIN, E * (slot + 1))))
    y0, y1 = jnp.concatenate(low_rows, axis=0), jnp.concatenate(high_rows, axis=0)
    y0, y1 = [jnp.concatenate([v[:, 0:128], v[:, 128:256]], axis=0).astype(BF16) for v in (y0, y1)]
    z0 = pack_z_side([rows_ref[0, E * slot : E * (slot + 1), :] for slot in range(MARGIN)]).astype(BF16)
    z1 = pack_z_side([rows_ref[1, E * slot : E * (slot + 1), :] for slot in range(MARGIN, SLOTS)]).astype(BF16)
    return (z0, z1), (y0, y1), (x0, x1)


def sort_margins(present, odd, axis, pair):
    on = [present[0, 2 * axis + side] >= 0 for side in range(2)]
    pair = [value.astype(F32) for value in pair]
    low = jnp.where(odd, pair[0], pair[1])
    high = jnp.where(odd, pair[1], pair[0])
    zero = jnp.zeros_like(low)
    return jnp.where(on[0], low, zero), jnp.where(on[1], high, zero)


def assemble(present, odds, rows_ref, margins, high_ref, low_ref):
    (zm, zp), (ym, yp), (xm, xp) = [
        sort_margins(present, odds[axis], axis, margins[axis]) for axis in range(3)
    ]
    rows, columns = both_iotas()
    picks = x_picks(columns, rows, PAD - MARGIN, E)
    sides = [unpack_x_side(v) for v in (xm, xp)]
    parts = []
    for group in range(4):
        pair = [pltpu.roll(v, 128 - 3 * MARGIN * group, 1) if group else v for v in sides]
        parts.append(jnp.concatenate(pair, axis=1))
    side = dot(jnp.concatenate(parts, axis=0).astype(BF16), picks)
    ym_rows, yp_rows = [jnp.concatenate([v[0:128], v[128:256]], axis=1) for v in (ym, yp)]
    z_sides = [pltpu.roll(v, 64, 1) for value in (zp, zm) for v in unpack_z_side(value)]
    lane = lane_iota((E, 128))
    for slot in range(SLOTS):
        core = both_halves(rows_ref, slice(E * slot, E * (slot + 1)))
        high, low = split(core)
        added = side[E * slot : E * (slot + 1)]
        full = high.astype(F32) + added
        right = jnp.where(lane < 64, full[:, 128:256], jnp.where(lane < 64 + E, z_sides[slot], 0.0))
        high_ref[PAD * slot : PAD * slot + E, 0:128] = full[:, 0:128].astype(BF16)
        high_ref[PAD * slot : PAD * slot + E, 128:256] = right.astype(BF16)
        rows = slice(MARGIN * slot, MARGIN * (slot + 1))
        outer = jnp.concatenate([yp_rows[rows], ym_rows[rows]], axis=0)
        high_ref[PAD * slot + E : PAD * (slot + 1), :] = outer.astype(BF16)
        low_ref[PAD * slot : PAD * slot + E, :] = low
        low_ref[PAD * slot + E : PAD * (slot + 1), :] = jnp.zeros((PAD - E, LANES), BF16)


def lines_stage(high, low, table, out_ref, rows, step):
    for start in range(0, rows, step):
        part = slice(start, start + step)
        wide = jnp.concatenate([high[part, :], low[part, :], high[part, :]], axis=1)
        out_ref[part, :] = dot(wide, table[...])


def y_stage(lines_ref, table, count, out_ref):
    for pair in range(SLOTS // 2):
        one = lines_ref[count * 2 * pair : count * (2 * pair + 1), :]
        two = lines_ref[count * (2 * pair + 1) : count * (2 * pair + 2), :]
        real = jnp.concatenate([one[:, 0:128], two[:, 0:128]], axis=1)
        imag = jnp.concatenate([one[:, 128:256], two[:, 128:256]], axis=1)
        high, low = split(jnp.concatenate([real, imag], axis=0))
        out = dot(table[...], jnp.concatenate([high, low, high], axis=0))
        out_ref[2 * pair] = out[:, 0:128]
        out_ref[2 * pair + 1] = out[:, 128:256]


def y_back_stage(planes_ref, table, out_ref):
    for pair in range(SLOTS // 2):
        both = jnp.concatenate([planes_ref[2 * pair], planes_ref[2 * pair + 1]], axis=1)
        high, low = split(both)
        out = dot(table[...], jnp.concatenate([high, low, high], axis=0))
        for which in range(2):
            rows = slice(E * (2 * pair + which), E * (2 * pair + which + 1))
            lanes = slice(128 * which, 128 * (which + 1))
            out_ref[rows, 0:128] = out[0:E, lanes]
            out_ref[rows, 128:256] = out[E : 2 * E, lanes]


def turn(value, cosine, sine):
    real, imag = value
    return real * cosine - imag * sine, real * sine + imag * cosine


def dft4(values, sign):
    (ar, ai), (br, bi), (cr, ci), (dr, di) = values
    sr, si, mr, mi = ar + cr, ai + ci, ar - cr, ai - ci
    pr, pi, qr, qi = br + dr, bi + di, br - dr, bi - di
    if sign > 0:
        first, third = (mr - qi, mi + qr), (mr + qi, mi - qr)
    else:
        first, third = (mr + qi, mi - qr), (mr - qi, mi + qr)
    return [(sr + pr, si + pi), first, (sr - pr, si - pi), third]


def dft16(values, sign):
    inner = []
    for low in range(4):
        line = dft4([values[4 * top + low] for top in range(4)], sign)
        moved = []
        for k in range(4):
            turns = low * k
            real, imag = line[k]
            if turns == 0:
                moved.append((real, imag))
            elif turns == 4:
                moved.append((-imag, real) if sign > 0 else (imag, -real))
            elif turns in (2, 6):
                root = float(np.sqrt(0.5))
                a, b = root * real, root * imag
                if turns == 2:
                    moved.append((a - b, a + b) if sign > 0 else (a + b, b - a))
                else:
                    moved.append((-a - b, a - b) if sign > 0 else (b - a, -a - b))
            else:
                angle = sign * 2.0 * np.pi * turns / SLOTS
                moved.append(turn((real, imag), float(np.cos(angle)), float(np.sin(angle))))
        inner.append(moved)
    out = [None] * SLOTS
    for k in range(4):
        line = dft4([inner[low][k] for low in range(4)], sign)
        for top in range(4):
            out[k + 4 * top] = line[top]
    return out


def z_forward(planes_ref, twiddle, rows, rows_imag):
    values = []
    for slot in range(SLOTS):
        value = (planes_ref[slot, rows, :], planes_ref[slot, rows_imag, :])
        if slot:
            value = turn(value, twiddle[0, slot], twiddle[1, slot])
        values.append(value)
    return dft16(values, -1)


def z_stage(planes_ref, out_ref):
    @pl.loop(0, PAD // 8, unroll=2)
    def _(step):
        rows = pl.ds(pl.multiple_of(8 * step, 8), 8)
        rows_imag = pl.ds(pl.multiple_of(8 * step + PAD, 8), 8)
        values = [(planes_ref[slot, rows, :], planes_ref[slot, rows_imag, :]) for slot in range(SLOTS)]
        values = dft16(values, -1)
        for slot in range(SLOTS):
            out_ref[slot, rows, :] = values[slot][0]
            out_ref[slot, rows_imag, :] = values[slot][1]


def filter_stage(planes_ref, kernel_ref, twiddle, conjugate, out_ref):
    @pl.loop(0, PAD // 8, unroll=2)
    def _(step):
        rows = pl.ds(pl.multiple_of(8 * step, 8), 8)
        rows_imag = pl.ds(pl.multiple_of(8 * step + PAD, 8), 8)
        values = z_forward(planes_ref, twiddle, rows, rows_imag)
        for slot in range(SLOTS):
            cosine, sine = kernel_ref[slot, rows, :], kernel_ref[slot, rows_imag, :]
            if conjugate:
                real, imag = values[slot]
                values[slot] = (real * cosine + imag * sine, imag * cosine - real * sine)
            else:
                values[slot] = turn(values[slot], cosine, sine)
        values = dft16(values, 1)
        for slot in range(SLOTS):
            real, imag = values[slot]
            if slot:
                cosine, sine = twiddle[0, slot], twiddle[1, slot]
                real, imag = real * cosine + imag * sine, imag * cosine - real * sine
            out_ref[slot, rows, :] = real
            out_ref[slot, rows_imag, :] = imag


def tap_stage(flat_ref, lines, spread, table, turns, table_y_ref, planes_ref):
    lane = lane_iota((3, 128))
    for tap in range(KS):
        row, start = KS2 * tap // 128, KS2 * tap % 128
        value = flat_ref[row : row + 3, :]
        if start:
            value = pltpu.roll(value, 128 - start, 1)
            after = pltpu.roll(flat_ref[row + 1 : row + 4, :], 128 - start, 1)
            value = jnp.where(lane < 128 - start, value, after)
        for part in range(3):
            lines[part, tap : tap + 1, :] = value[part : part + 1]
    lane = lane_iota((TAPS, 128))
    for line in range(KS):
        part, start = KS * line // 128, KS * line % 128
        value = lines[part]
        if start:
            value = pltpu.roll(value, 128 - start, 1)
            if start + KS > 128:
                after = pltpu.roll(lines[part + 1], 128 - start, 1)
                value = jnp.where(lane < 128 - start, value, after)
        spread[TAPS * line : TAPS * (line + 1), :] = jnp.where(lane < KS, value, 0.0)
    for line in range(KS, TAPS):
        spread[TAPS * line : TAPS * (line + 1), :] = jnp.zeros((TAPS, 128), F32)
    rows = jnp.concatenate([spread[pl.ds(tap, TAPS, stride=TAPS), :] for tap in range(KS)], axis=0)
    high = rows.astype(BF16).astype(F32)
    low = rows - high
    wide = high + pltpu.roll(low, 32, 1) + pltpu.roll(high, 64, 1)
    out = dot(wide.astype(BF16), table[...])
    slots = [None] * SLOTS
    for tap in range(KS):
        part = out[TAPS * tap : TAPS * (tap + 1)]
        value = part[:, 0:128], part[:, 128:256]
        if tap != MARGIN:
            cosine, sine = [jnp.concatenate([turns[i, tap]] * 3, axis=0) for i in range(2)]
            value = turn(value, cosine, sine)
        slot = (tap - MARGIN) % SLOTS
        if slots[slot] is not None:
            value = value[0] + slots[slot][0], value[1] + slots[slot][1]
        slots[slot] = value
    for pair in range(SLOTS // 2):
        one, two = slots[2 * pair], slots[2 * pair + 1]
        real = jnp.concatenate([one[0], two[0]], axis=1)
        imag = jnp.concatenate([one[1], two[1]], axis=1)
        high, low = split(jnp.concatenate([real, imag], axis=0))
        out = dot(table_y_ref[...], jnp.concatenate([high, low, high], axis=0))
        planes_ref[2 * pair] = out[:, 0:128]
        planes_ref[2 * pair + 1] = out[:, 128:256]


def gathered_place(count, distance):
    place, size = 0, 1
    for bits in gather_rounds(count):
        for bit in bits:
            place = place + size * ((distance >> bit) & 1)
            size *= 2
    return place


def spectrum_kernel(update, count, order, lists, blend, cell_row, near, far, table, turns, table_y_ref, out_ref, flat, lines, spread, planes):
    view = order[update]
    own = lax.axis_index("blk")
    half = count // 2
    total = blend[0, 0, view] + blend[0, 1, view]
    value = None
    rows = slice(CELLROWS * update, CELLROWS * (update + 1))
    for k in range(2):
        place = gathered_place(count, cell_row[lists[0, k, view]] ^ own)
        inner = lax.rem(place, half)
        line = jnp.where(place < half, near[inner].astype(F32), far[inner].astype(F32))[rows]
        weight = blend[0, k, view] / total * (2.0 / float(PAD**3))
        part = line * (weight / jnp.sum(line))
        value = part if value is None else value + part
    flat[...] = value
    tap_stage(flat, lines, spread, table, turns, table_y_ref, planes)
    z_stage(planes, out_ref)


def grid_bits(count):
    low_count = count.bit_length() - 2
    bits = [[bit for bit in range(low_count) if bit % 3 == axis] for axis in range(3)]
    bits[2] = [low_count] + bits[2]
    return bits


def gather_rounds(count):
    axes = grid_bits(count)
    bits = axes[2][:2] + axes[1][:1] + axes[0][1:2]
    bits += [bit for bit in range(1, count.bit_length() - 1) if bit not in bits]
    rounds = []
    while bits:
        rounds.append(bits[:2])
        bits = bits[2:]
    return rounds + [[0]]


def riders(count):
    axes = grid_bits(count)
    found = {1: (0, 0)}
    if axes[1]:
        found[1 << axes[1][0]] = (1, 0)
    found[1 << axes[2][0]] = (2, 0)
    for axis in (1, 2):
        if len(axes[axis]) == 2:
            found[1 << axes[axis][0] | 1 << axes[axis][1]] = (axis, 1)
    if len(axes[0]) == 2:
        found[1 << axes[0][1]] = (0, 1)
    return found


def odd_places(count):
    own = lax.axis_index("blk")
    return [((own >> bits[0]) & 1) == 1 if bits else own < 0 for bits in grid_bits(count)]


def slab_kinds(count):
    kinds = [(1, 0), (2, 0), (2, 1), (0, 1), (0, 0), (1, 1)]
    return [kind for kind in kinds if len(grid_bits(count)[kind[0]]) > kind[1]]


def store_slabs(count, slabs, outs):
    odds = odd_places(count)
    for (axis, far), out in zip(slab_kinds(count), outs):
        low, high = slabs[axis]
        out[...] = jnp.where(odds[axis], high, low) if far else jnp.where(odds[axis], low, high)


def start_kernel(count, order, cells, est, u_out, cells_out, *refs):
    outs, (got, pad, flat, sems) = refs[:-4], refs[-4:]
    loading = pltpu.make_async_copy(est, flat, sems.at[UPDATES])
    loading.start()
    copies = []
    for update in range(UPDATES):
        copies.append(pltpu.make_async_copy(cells.at[order[update]], got.at[update], sems.at[update]))
        copies[-1].start()
    pad[...] = jnp.zeros((1, CELLROWS * 128), F32)
    for update in range(UPDATES):
        copies[update].wait()
        pad[:, 0:KS3] = got[update]
        wide = pad[...]
        rows = [wide[:, 128 * row : 128 * (row + 1)] for row in range(CELLROWS)]
        here = slice(CELLROWS * update, CELLROWS * (update + 1))
        cells_out[here, :] = jnp.concatenate(rows, axis=0).astype(BF16)
    loading.wait()
    unflatten(lambda row: flat[pl.ds(row, 8, stride=3), :], u_out)
    store_slabs(count, pack_slabs(u_out), outs)


VIEW_PARTS = 9


def views_kernel(order, observed, o0, o1, near, wide, sems):
    part_rows = FLAT // VIEW_PARTS
    copies = []
    for part in range(VIEW_PARTS):
        here = pl.ds(part_rows * 128 * part, part_rows * 128)
        copies.append(pltpu.make_async_copy(observed.at[:, :, here], near.at[:, :, here], sems.at[part]))
        copies[-1].start()
    step_rows = 32
    for part in range(VIEW_PARTS):
        copies[part].wait()

        @pl.loop(0, part_rows // step_rows)
        def _(step):
            first = part * part_rows + step * step_rows
            lanes = pl.ds(pl.multiple_of(first * 128, 128), step_rows * 128)
            value = near[0, :, lanes].astype(F32)
            value = jnp.concatenate([value, value[0 : 8 - VIEWS]], axis=0)
            for row in range(step_rows):
                rows = pl.ds(pl.multiple_of((first + row) * 8, 8), 8)
                wide[rows, :] = value[:, 128 * row : 128 * (row + 1)]

    for update, out in enumerate((o0, o1)):
        view = order[update]
        unflatten(lambda row: wide[pl.ds(8 * row + view, 8, stride=24), :], out)


def field_stage(count, present, u, slabs, ea, gy, out, high, low, lines):
    found = {kind: slab[...] for kind, slab in zip(slab_kinds(count), slabs)}
    margins = []
    for axis in range(3):
        blank = jnp.zeros(SLABS[axis].shape, BF16)
        margins.append((found.get((axis, 0), blank), found.get((axis, 1), blank)))
    assemble(present, odd_places(count), u, margins, high, low)
    lines_stage(high, low, ea, lines, SLOTS * PAD, 256)
    y_stage(lines, gy, PAD, out)


def wide_terms(value):
    high, low = split(value)
    return jnp.concatenate([high, low, high], axis=1)


STEP = 192


def update_body(tissue, kernel, u, o, tables, planes, lines, new_ref):
    ea, ei, gh, gb, twiddle = tables
    filter_stage(planes, kernel, twiddle, False, planes)
    y_back_stage(planes, gb, lines)
    lane = lane_iota((STEP, LANES))
    valid = (lane % PAD < E) & (lane < 3 * PAD)
    for start in range(0, SLOTS * E, STEP):
        rows = slice(start, start + STEP)
        blurred = dot(wide_terms(lines[rows, :]), ei[...])
        quotient = jnp.where(valid, both_halves(o, rows) / blurred, 0.0)
        lines[rows, :] = dot(wide_terms(quotient), ea[...])
    y_stage(lines, gh, E, planes)
    filter_stage(planes, kernel, twiddle, True, planes)
    y_back_stage(planes, gb, lines)
    alive = tissue[0] > 0
    for start in range(0, SLOTS * E, STEP):
        rows = slice(start, start + STEP)
        correction = dot(wide_terms(lines[rows, :]), ei[...])
        for half in range(2):
            core = u[half, rows, :]
            new_ref[half, rows, :] = jnp.where(alive, core * correction[:, 128 * half : 128 * (half + 1)], core)


def first_kernel(count, tissue, present, u, *refs):
    kinds = len(slab_kinds(count))
    slabs, (kernel, o, ea, gy, ei, gh, gb, twiddle, u_out), outs = refs[:kinds], refs[kinds : kinds + 9], refs[kinds + 9 : -4]
    planes, high, low, lines = refs[-4:]
    field_stage(count, present, u, slabs, ea, gy, planes, high, low, lines)
    update_body(tissue, kernel, u, o, (ea, ei, gh, gb, twiddle), planes, lines, u_out)
    store_slabs(count, pack_slabs(u_out), outs)


def last_kernel(count, tissue, present, u, *refs):
    kinds = len(slab_kinds(count))
    slabs, (kernel, o, ea, gy, ei, gh, gb, twiddle, out) = refs[:kinds], refs[kinds : kinds + 9]
    planes, high, low, lines, fresh = refs[-5:]
    field_stage(count, present, u, slabs, ea, gy, planes, high, low, lines)
    update_body(tissue, kernel, u, o, (ea, ei, gh, gb, twiddle), planes, lines, fresh)
    flatten(fresh, out)


VM = pl.BlockSpec(memory_space=pltpu.VMEM)
SM = pl.BlockSpec(memory_space=pltpu.SMEM)
ANY = pl.BlockSpec(memory_space=pl.ANY)
HBM = pl.BlockSpec(memory_space=pltpu.HBM)
PARAMS = pltpu.CompilerParams(vmem_limit_bytes=48 * 1024 * 1024)


def shape(dims, kind=F32):
    return jax.ShapeDtypeStruct(dims, kind)


SLAB = shape((144, 128), BF16)
WIDE_SLAB = shape((256, 128), BF16)
SLABS = [SLAB, WIDE_SLAB, SLAB]
CELLS = shape((UPDATES * CELLROWS, 128), BF16)
ROWS = shape((2, SLOTS * E, 128))
ROWS_V = pltpu.VMEM((2, SLOTS * E, 128), F32)
PLANES = shape((SLOTS, 128, 128))
PLANES_V = pltpu.VMEM((SLOTS, 128, 128), F32)
LINES_V = pltpu.VMEM((SLOTS * PAD, LANES), F32)
TERMS_V = pltpu.VMEM((SLOTS * PAD, LANES), BF16)


def call(body, ins, outs, args, scratch=(), name=None):
    many = isinstance(outs, list)
    return pl.pallas_call(
        body,
        in_specs=ins,
        out_specs=[VM] * len(outs) if many else VM,
        out_shape=outs,
        scratch_shapes=list(scratch),
        compiler_params=PARAMS,
        name=name,
    )(*args)


def far_pairs(count, axis):
    bits = grid_bits(count)[axis]
    extent = 2 ** len(bits)
    pairs = []
    for number in range(count):
        at = sum(((number >> bit) & 1) << level for level, bit in enumerate(bits))
        moved = at + 1 if at % 2 else at - 1
        other = number
        if 0 <= moved < extent:
            for level, bit in enumerate(bits):
                other = other & ~(1 << bit) | ((moved >> level) & 1) << bit
        else:
            other = number ^ (1 if axis else 2)
        pairs.append((number, other))
    return pairs


def swap(value, distance, count):
    return lax.ppermute(value, "blk", [(number, number ^ distance) for number in range(count)])


def swap_slab(kind, slab, count):
    axis, far = kind
    if far:
        return lax.ppermute(slab, "blk", far_pairs(count, axis))
    return swap(slab, 1 << grid_bits(count)[axis][0], count)


def swap_slabs(slabs, count):
    return [swap_slab(kind, slab, count) for kind, slab in zip(slab_kinds(count), slabs)]


def local(estimate, observed, psf_cells, tissue, neighbours, psf_list, psf_blend, cell_row, view_order):
    count = lax.axis_size("blk")
    ea = jnp.asarray(stacked(table_space_to_lines(), 0))
    ei = jnp.asarray(stacked(table_lines_to_space(), 0))
    gy = jnp.asarray(stacked(table_y(PAD), 1))
    gh = jnp.asarray(stacked(table_y(E), 1))
    gb = jnp.asarray(stacked(table_y_back(), 1))
    gt = jnp.asarray(stacked(table_y_taps(), 1))
    taps = jnp.asarray(table_taps())
    turns = jnp.asarray(table_tap_turns())
    twiddle = jnp.asarray(table_twiddle())
    lists = jnp.swapaxes(psf_list, 1, 2)
    blend = jnp.swapaxes(psf_blend, 1, 2)

    slab_shapes = [SLABS[axis] for axis, far in slab_kinds(count)]
    rows, cells, *slabs = call(
        functools.partial(start_kernel, count),
        [SM, HBM, HBM],
        [ROWS, CELLS] + slab_shapes,
        (
            view_order,
            pltpu.with_memory_space_constraint(jnp.swapaxes(psf_cells, 0, 1), pltpu.HBM),
            pltpu.with_memory_space_constraint(estimate.reshape(FLAT, 128), pltpu.HBM),
        ),
        [
            pltpu.VMEM((UPDATES, 1, KS3), F32),
            pltpu.VMEM((1, CELLROWS * 128), F32),
            pltpu.VMEM((FLAT, 128), F32),
            pltpu.SemaphoreType.DMA((UPDATES + 1,)),
        ],
        name="start",
    )
    targets = call(
        views_kernel,
        [SM, HBM],
        [ROWS, ROWS],
        (view_order, pltpu.with_memory_space_constraint(observed, pltpu.HBM)),
        [
            pltpu.VMEM((1, VIEWS, FLAT * 128), BF16),
            pltpu.VMEM((8 * FLAT, 128), F32),
            pltpu.SemaphoreType.DMA((VIEW_PARTS,)),
        ],
        name="views",
    )
    slabs = dict(zip(slab_kinds(count), slabs))
    riding = riders(count)
    margins = {}
    held = cells
    for number, bits in enumerate(gather_rounds(count)):
        arrived = [held]
        size = held.shape[0]
        for part in range(1, 2 ** len(bits)):
            distance = sum(((part >> level) & 1) << bit for level, bit in enumerate(bits))
            load = [held]
            kind = riding.get(distance)
            if kind is not None:
                load.append(slabs[kind])
            if distance == 1 and (0, 1) in margins:
                load.append(margins[0, 1])
            got = swap(jnp.concatenate(load, axis=0) if len(load) > 1 else held, distance, count)
            arrived.append(got[:size])
            if kind is not None:
                margins[kind] = got[size : size + slabs[kind].shape[0]]
            if distance == 1 and (0, 1) in margins:
                margins[0, 1] = got[got.shape[0] - SLAB.shape[0] :]
        if number == 0:
            arrived, targets = lax.optimization_barrier((arrived, targets))
        if bits != [0]:
            held = jnp.concatenate(arrived, axis=0)
    other = arrived[1]
    for kind in slab_kinds(count):
        if kind not in margins:
            margins[kind] = swap_slab(kind, slabs[kind], count)
    margins = [margins[kind] for kind in slab_kinds(count)]
    near_cells, far_cells = [v.reshape(count // 2, UPDATES * CELLROWS, 128) for v in (held, other)]

    def spectrum(update):
        return call(
            functools.partial(spectrum_kernel, update, count),
            [SM] * 4 + [VM] * 5,
            PLANES,
            (view_order, lists, blend, cell_row, near_cells, far_cells, taps, turns, gt),
            [
                pltpu.VMEM((CELLROWS, 128), F32),
                pltpu.VMEM((3, TAPS, 128), F32),
                pltpu.VMEM((TAPS * TAPS, 128), F32),
                PLANES_V,
            ],
            name="spectrum",
        )

    def update(body, outs, number, kernel, rows, margins, scratch, name):
        return call(
            functools.partial(body, count),
            [SM] * 2 + [VM] * (9 + len(slab_shapes)),
            outs,
            (tissue, neighbours, rows, *margins, kernel, targets[number], ea, gy, ei, gh, gb, twiddle),
            [PLANES_V, TERMS_V, TERMS_V, LINES_V] + scratch,
            name=name,
        )

    kernel = spectrum(0)
    kernel, margins = lax.optimization_barrier((kernel, margins))
    rows, *slabs = update(first_kernel, [ROWS] + slab_shapes, 0, kernel, rows, margins, [], "first")
    margins = swap_slabs(slabs, count)
    kernel = spectrum(1)
    kernel, margins = lax.optimization_barrier((kernel, margins))
    out = update(last_kernel, shape((FLAT, 128)), 1, kernel, rows, margins, [ROWS_V], "last")
    return out.reshape(1, FLAT * 128)


def solution(mesh):
    return jax.shard_map(
        local,
        mesh=mesh,
        in_specs=(
            P("blk", None),
            P("blk", None, None),
            P("blk", None, None),
            P("blk"),
            P("blk", None),
            P("blk", None, None),
            P("blk", None, None),
            P(),
            P(),
        ),
        out_specs=P("blk", None),
        check_vma=False,
    )
```

```python
import functools

import numpy as np

import jax
import jax.numpy as jnp
import ml_dtypes
from jax import lax
from jax.experimental import pallas as pl
from jax.experimental.pallas import tpu as pltpu
from jax.sharding import PartitionSpec as P

E = 48
MARGIN = 8
UPDATES = 2
VIEWS = 6
PAD = 64
KS = 17
KS2 = KS * KS
KS3 = 4913
SLOTS = 16
LANES = 256
TAPS = 24
CELLROWS = 40
FLAT = 864

F32 = jnp.float32
BF16 = jnp.bfloat16


def two_terms(table):
    high = table.astype(ml_dtypes.bfloat16)
    low = (table - high.astype(np.float64)).astype(ml_dtypes.bfloat16)
    return high, low


def stacked(table, axis):
    high, low = two_terms(table)
    return np.concatenate([high, high, low], axis=axis)


def x_positions():
    x = np.arange(PAD)
    return np.where(x < PAD - MARGIN, x, x - PAD)


def table_space_to_lines():
    z4, k4, kx = np.arange(4), np.arange(4), np.arange(32)
    angle = -2.0 * np.pi * (
        z4[:, None, None, None] * k4[None, None, :, None] / 4.0
        + (kx[None, None, None, :] + 0.5) * x_positions()[None, :, None, None] / PAD
    )
    angle = angle.reshape(LANES, 128)
    return np.concatenate([np.cos(angle), np.sin(angle)], axis=1)


def table_lines_to_space():
    back = table_space_to_lines().T.copy()
    back = back.reshape(LANES, 4, PAD)
    back[:, 3, :] = 0.0
    back[:, :, E:] = 0.0
    return back.reshape(LANES, LANES)


def complex_rows(angle):
    cosine, sine = np.cos(angle), np.sin(angle)
    return np.concatenate(
        [np.concatenate([cosine, -sine], axis=1), np.concatenate([sine, cosine], axis=1)], axis=0
    )


def table_y(count):
    ky, y = np.arange(PAD), np.arange(count)
    return complex_rows(-2.0 * np.pi * (ky[:, None] * y[None, :] % PAD) / PAD)


def table_y_back():
    ky, y = np.arange(PAD), np.arange(E)
    return complex_rows(2.0 * np.pi * (y[:, None] * ky[None, :] % PAD) / PAD)


def table_y_taps():
    ky, tap = np.arange(PAD), np.arange(TAPS) - MARGIN
    angle = -2.0 * np.pi * ky[:, None] * tap[None, :] / PAD
    return complex_rows(angle)


def table_taps():
    kx, tap = np.arange(32), np.arange(KS) - MARGIN
    angle = -2.0 * np.pi * (kx[None, :] + 0.5) * tap[:, None] / PAD
    full = np.concatenate([np.tile(np.cos(angle), (1, 4)), np.tile(np.sin(angle), (1, 4))], axis=1)
    high, low = two_terms(full)
    table = np.zeros((128, LANES), ml_dtypes.bfloat16)
    for start, term in ((0, high), (32, high), (64, low)):
        table[start : start + KS] = term
    return table


def table_tap_turns():
    k4 = np.repeat(np.arange(4), 32)
    tap = np.arange(KS) - MARGIN
    angle = -2.0 * np.pi * tap[:, None] * k4[None, :] / PAD
    both = np.stack([np.cos(angle), np.sin(angle)], axis=0)
    return np.broadcast_to(both[:, :, None, :], (2, KS, 8, 128)).astype(np.float32)


def table_twiddle():
    k4 = np.repeat(np.arange(4), 32)
    angle = -2.0 * np.pi * np.arange(SLOTS)[:, None] * k4[None, :] / PAD
    both = np.stack([np.cos(angle), np.sin(angle)], axis=0)
    return np.broadcast_to(both[:, :, None, :], (2, SLOTS, 8, 128)).astype(np.float32)


def split(value):
    high = value.astype(BF16)
    low = (value - high.astype(F32)).astype(BF16)
    return high, low


def dot(left, right):
    return jnp.dot(left, right, preferred_element_type=F32)


def both_halves(rows_ref, rows):
    return jnp.concatenate([rows_ref[0, rows, :], rows_ref[1, rows, :]], axis=1)


def lane_iota(shape):
    return lax.broadcasted_iota(jnp.int32, shape, 1)


def cut(pieces, piece, target):
    offset = E * piece
    first, start = offset // 128, offset % 128
    shift = (target - start) % 128
    one = pltpu.roll(pieces[first], shift, 1) if shift else pieces[first]
    if start + E <= 128:
        return one
    two = pltpu.roll(pieces[first + 1], shift, 1) if shift else pieces[first + 1]
    edge = target + 128 - start
    return jnp.where(lane_iota(one.shape) < edge, one, two)


def unflatten(load, out_ref):
    lane = lane_iota((8, 128))
    zero = jnp.zeros((8, 128), F32)
    for block in range(12):
        parts = []
        for z4 in range(3):
            first = 3 * (96 * z4 + 8 * block)
            parts.append([load(first + m) for m in range(3)])
        for piece in range(8):
            low = cut(parts[0], piece, 0)
            mid = cut(parts[1], piece, 64)
            top = cut(parts[2], piece, 0)
            left = jnp.where(lane < E, low, jnp.where(lane < 64, zero, mid))
            left = jnp.where(lane < 64 + E, left, zero)
            rows = pl.ds(64 * block + piece, 8, stride=8)
            out_ref[0, rows, :] = left
            out_ref[1, rows, :] = jnp.where(lane < E, top, zero)


def flatten(rows_ref, flat_ref):
    lane = lane_iota((8, 128))
    for block in range(12):
        found = []
        for piece in range(8):
            rows = pl.ds(64 * block + piece, 8, stride=8)
            found.append((rows_ref[0, rows, :], rows_ref[1, rows, :]))
        for z4 in range(3):
            first = 3 * (96 * z4 + 8 * block)
            out = [None, None, None]
            for piece in range(8):
                value = found[piece][0] if z4 < 2 else found[piece][1]
                source = 64 if z4 == 1 else 0
                offset = E * piece
                spot, start = offset // 128, offset % 128
                shift = (start - source) % 128
                moved = pltpu.roll(value, shift, 1) if shift else value
                if out[spot] is None:
                    out[spot] = moved
                else:
                    out[spot] = jnp.where(lane < start, out[spot], moved)
                if start + E > 128:
                    out[spot + 1] = moved
            for m in range(3):
                flat_ref[pl.ds(first + m, 8, stride=3), :] = out[m]


def squeeze(pieces):
    out = [None, None, None]
    for piece, value in enumerate(pieces):
        spot, start = E * piece // 128, E * piece % 128
        moved = pltpu.roll(value, start, 1) if start else value
        out[spot] = moved if out[spot] is None else jnp.where(lane_iota(moved.shape) < start, out[spot], moved)
        if start + E > 128:
            out[spot + 1] = moved
    return out


def stretch(full):
    return [cut(full, piece, 0) for piece in range(8)]


def pack_x_side(value):
    last = value[144:192]
    lane = lane_iota(last.shape)
    out = []
    for part in range(3):
        moved = pltpu.roll(last, (96 - 32 * part) % 128, 1)
        out.append(jnp.where(lane < 96, value[48 * part : 48 * (part + 1)], moved))
    return jnp.concatenate(out, axis=0)


def unpack_x_side(value):
    parts = [value[48 * part : 48 * (part + 1)] for part in range(3)]
    lane = lane_iota(parts[0].shape)
    last = pltpu.roll(parts[0], 32, 1)
    for part in range(1, 3):
        last = jnp.where(lane < 32 * part, last, pltpu.roll(parts[part], (32 + 32 * part) % 128, 1))
    return jnp.concatenate(parts + [last], axis=0)


def pack_z_side(blocks):
    return jnp.concatenate(squeeze(blocks), axis=0)


def unpack_z_side(value):
    return stretch([value[48 * part : 48 * (part + 1)] for part in range(3)])


def x_picks(wide, packed, low_start, high_start):
    place = packed % 128
    start = jnp.where(packed >= 128, high_start, low_start)
    here = (wide // PAD == place // MARGIN) & (wide % PAD == start + place % MARGIN) & (place < 3 * MARGIN)
    return jnp.where(here, 1.0, 0.0).astype(BF16)


def both_iotas():
    dims = (LANES, LANES)
    return lax.broadcasted_iota(jnp.int32, dims, 0), lax.broadcasted_iota(jnp.int32, dims, 1)


def pack_slabs(rows_ref):
    high = both_halves(rows_ref, slice(None)).astype(BF16)
    rows, columns = both_iotas()
    found = dot(high, x_picks(rows, columns, 0, E - MARGIN))
    faces = []
    for face in range(2):
        value = found[0:192, 128 * face : 128 * (face + 1)]
        for group in range(1, 4):
            part = found[192 * group : 192 * (group + 1), 128 * face : 128 * (face + 1)]
            value = value + pltpu.roll(part, 3 * MARGIN * group, 1)
        faces.append(pack_x_side(value).astype(BF16))
    x0, x1 = faces
    low_rows, high_rows = [], []
    for slot in range(SLOTS):
        low_rows.append(both_halves(rows_ref, slice(E * slot, E * slot + MARGIN)))
        high_rows.append(both_halves(rows_ref, slice(E * slot + E - MARGIN, E * (slot + 1))))
    y0, y1 = jnp.concatenate(low_rows, axis=0), jnp.concatenate(high_rows, axis=0)
    y0, y1 = [jnp.concatenate([v[:, 0:128], v[:, 128:256]], axis=0).astype(BF16) for v in (y0, y1)]
    z0 = pack_z_side([rows_ref[0, E * slot : E * (slot + 1), :] for slot in range(MARGIN)]).astype(BF16)
    z1 = pack_z_side([rows_ref[1, E * slot : E * (slot + 1), :] for slot in range(MARGIN, SLOTS)]).astype(BF16)
    return (z0, z1), (y0, y1), (x0, x1)


def sort_margins(present, odd, axis, pair):
    on = jnp.where(present[...] >= 0, 1.0, 0.0)
    pair = [value.astype(F32) for value in pair]
    low = jnp.where(odd, pair[0], pair[1])
    high = jnp.where(odd, pair[1], pair[0])
    return low * on[:, 2 * axis : 2 * axis + 1], high * on[:, 2 * axis + 1 : 2 * axis + 2]


def assemble(present, odds, rows_ref, margins, high_ref, low_ref):
    (zm, zp), (ym, yp), (xm, xp) = [
        sort_margins(present, odds[axis], axis, margins[axis]) for axis in range(3)
    ]
    rows, columns = both_iotas()
    picks = x_picks(columns, rows, PAD - MARGIN, E)
    sides = [unpack_x_side(v) for v in (xm, xp)]
    parts = []
    for group in range(4):
        pair = [pltpu.roll(v, 128 - 3 * MARGIN * group, 1) if group else v for v in sides]
        parts.append(jnp.concatenate(pair, axis=1))
    side = dot(jnp.concatenate(parts, axis=0).astype(BF16), picks)
    ym_rows, yp_rows = [jnp.concatenate([v[0:128], v[128:256]], axis=1) for v in (ym, yp)]
    z_sides = [pltpu.roll(v, 64, 1) for value in (zp, zm) for v in unpack_z_side(value)]
    lane = lane_iota((E, 128))
    for slot in range(SLOTS):
        core = both_halves(rows_ref, slice(E * slot, E * (slot + 1)))
        high, low = split(core)
        added = side[E * slot : E * (slot + 1)]
        full = high.astype(F32) + added
        right = jnp.where(lane < 64, full[:, 128:256], jnp.where(lane < 64 + E, z_sides[slot], 0.0))
        high_ref[PAD * slot : PAD * slot + E, 0:128] = full[:, 0:128].astype(BF16)
        high_ref[PAD * slot : PAD * slot + E, 128:256] = right.astype(BF16)
        rows = slice(MARGIN * slot, MARGIN * (slot + 1))
        outer = jnp.concatenate([yp_rows[rows], ym_rows[rows]], axis=0)
        high_ref[PAD * slot + E : PAD * (slot + 1), :] = outer.astype(BF16)
        low_ref[PAD * slot : PAD * slot + E, :] = low
        low_ref[PAD * slot + E : PAD * (slot + 1), :] = jnp.zeros((PAD - E, LANES), BF16)


def lines_stage(high, low, table, out_ref, rows, step):
    for start in range(0, rows, step):
        part = slice(start, start + step)
        wide = jnp.concatenate([high[part, :], low[part, :], high[part, :]], axis=1)
        out_ref[part, :] = dot(wide, table[...])


def y_stage(lines_ref, table, count, out_ref):
    for pair in range(SLOTS // 2):
        one = lines_ref[count * 2 * pair : count * (2 * pair + 1), :]
        two = lines_ref[count * (2 * pair + 1) : count * (2 * pair + 2), :]
        real = jnp.concatenate([one[:, 0:128], two[:, 0:128]], axis=1)
        imag = jnp.concatenate([one[:, 128:256], two[:, 128:256]], axis=1)
        high, low = split(jnp.concatenate([real, imag], axis=0))
        out = dot(table[...], jnp.concatenate([high, low, high], axis=0))
        out_ref[2 * pair] = out[:, 0:128]
        out_ref[2 * pair + 1] = out[:, 128:256]


def y_back_stage(planes_ref, table, out_ref):
    for pair in range(SLOTS // 2):
        both = jnp.concatenate([planes_ref[2 * pair], planes_ref[2 * pair + 1]], axis=1)
        high, low = split(both)
        out = dot(table[...], jnp.concatenate([high, low, high], axis=0))
        for which in range(2):
            rows = slice(E * (2 * pair + which), E * (2 * pair + which + 1))
            lanes = slice(128 * which, 128 * (which + 1))
            out_ref[rows, 0:128] = out[0:E, lanes]
            out_ref[rows, 128:256] = out[E : 2 * E, lanes]


def turn(value, cosine, sine):
    real, imag = value
    return real * cosine - imag * sine, real * sine + imag * cosine


def dft4(values, sign):
    (ar, ai), (br, bi), (cr, ci), (dr, di) = values
    sr, si, mr, mi = ar + cr, ai + ci, ar - cr, ai - ci
    pr, pi, qr, qi = br + dr, bi + di, br - dr, bi - di
    if sign > 0:
        first, third = (mr - qi, mi + qr), (mr + qi, mi - qr)
    else:
        first, third = (mr + qi, mi - qr), (mr - qi, mi + qr)
    return [(sr + pr, si + pi), first, (sr - pr, si - pi), third]


def dft16(values, sign):
    inner = []
    for low in range(4):
        line = dft4([values[4 * top + low] for top in range(4)], sign)
        moved = []
        for k in range(4):
            turns = low * k
            real, imag = line[k]
            if turns == 0:
                moved.append((real, imag))
            elif turns == 4:
                moved.append((-imag, real) if sign > 0 else (imag, -real))
            elif turns in (2, 6):
                root = float(np.sqrt(0.5))
                a, b = root * real, root * imag
                if turns == 2:
                    moved.append((a - b, a + b) if sign > 0 else (a + b, b - a))
                else:
                    moved.append((-a - b, a - b) if sign > 0 else (b - a, -a - b))
            else:
                angle = sign * 2.0 * np.pi * turns / SLOTS
                moved.append(turn((real, imag), float(np.cos(angle)), float(np.sin(angle))))
        inner.append(moved)
    out = [None] * SLOTS
    for k in range(4):
        line = dft4([inner[low][k] for low in range(4)], sign)
        for top in range(4):
            out[k + 4 * top] = line[top]
    return out


def z_forward(planes_ref, twiddle, rows, rows_imag):
    values = []
    for slot in range(SLOTS):
        value = (planes_ref[slot, rows, :], planes_ref[slot, rows_imag, :])
        if slot:
            value = turn(value, twiddle[0, slot], twiddle[1, slot])
        values.append(value)
    return dft16(values, -1)


def z_stage(planes_ref, out_ref):
    @pl.loop(0, PAD // 8, unroll=2)
    def _(step):
        rows = pl.ds(pl.multiple_of(8 * step, 8), 8)
        rows_imag = pl.ds(pl.multiple_of(8 * step + PAD, 8), 8)
        values = [(planes_ref[slot, rows, :], planes_ref[slot, rows_imag, :]) for slot in range(SLOTS)]
        values = dft16(values, -1)
        for slot in range(SLOTS):
            out_ref[slot, rows, :] = values[slot][0]
            out_ref[slot, rows_imag, :] = values[slot][1]


def filter_stage(planes_ref, kernel_ref, twiddle, conjugate, out_ref):
    @pl.loop(0, PAD // 8, unroll=2)
    def _(step):
        rows = pl.ds(pl.multiple_of(8 * step, 8), 8)
        rows_imag = pl.ds(pl.multiple_of(8 * step + PAD, 8), 8)
        values = z_forward(planes_ref, twiddle, rows, rows_imag)
        for slot in range(SLOTS):
            cosine, sine = kernel_ref[slot, rows, :], kernel_ref[slot, rows_imag, :]
            if conjugate:
                real, imag = values[slot]
                values[slot] = (real * cosine + imag * sine, imag * cosine - real * sine)
            else:
                values[slot] = turn(values[slot], cosine, sine)
        values = dft16(values, 1)
        for slot in range(SLOTS):
            real, imag = values[slot]
            if slot:
                cosine, sine = twiddle[0, slot], twiddle[1, slot]
                real, imag = real * cosine + imag * sine, imag * cosine - real * sine
            out_ref[slot, rows, :] = real
            out_ref[slot, rows_imag, :] = imag


def tap_stage(flat_ref, lines, spread, table, turns, table_y_ref, planes_ref):
    lane = lane_iota((3, 128))
    for tap in range(KS):
        row, start = KS2 * tap // 128, KS2 * tap % 128
        value = flat_ref[row : row + 3, :]
        if start:
            value = pltpu.roll(value, 128 - start, 1)
            after = pltpu.roll(flat_ref[row + 1 : row + 4, :], 128 - start, 1)
            value = jnp.where(lane < 128 - start, value, after)
        for part in range(3):
            lines[part, tap : tap + 1, :] = value[part : part + 1]
    lane = lane_iota((TAPS, 128))
    for line in range(KS):
        part, start = KS * line // 128, KS * line % 128
        value = lines[part]
        if start:
            value = pltpu.roll(value, 128 - start, 1)
            if start + KS > 128:
                after = pltpu.roll(lines[part + 1], 128 - start, 1)
                value = jnp.where(lane < 128 - start, value, after)
        spread[TAPS * line : TAPS * (line + 1), :] = jnp.where(lane < KS, value, 0.0)
    for line in range(KS, TAPS):
        spread[TAPS * line : TAPS * (line + 1), :] = jnp.zeros((TAPS, 128), F32)
    rows = jnp.concatenate([spread[pl.ds(tap, TAPS, stride=TAPS), :] for tap in range(KS)], axis=0)
    high = rows.astype(BF16).astype(F32)
    low = rows - high
    wide = high + pltpu.roll(low, 32, 1) + pltpu.roll(high, 64, 1)
    out = dot(wide.astype(BF16), table[...])
    slots = [None] * SLOTS
    for tap in range(KS):
        part = out[TAPS * tap : TAPS * (tap + 1)]
        value = part[:, 0:128], part[:, 128:256]
        if tap != MARGIN:
            cosine, sine = [jnp.concatenate([turns[i, tap]] * 3, axis=0) for i in range(2)]
            value = turn(value, cosine, sine)
        slot = (tap - MARGIN) % SLOTS
        if slots[slot] is not None:
            value = value[0] + slots[slot][0], value[1] + slots[slot][1]
        slots[slot] = value
    for pair in range(SLOTS // 2):
        one, two = slots[2 * pair], slots[2 * pair + 1]
        real = jnp.concatenate([one[0], two[0]], axis=1)
        imag = jnp.concatenate([one[1], two[1]], axis=1)
        high, low = split(jnp.concatenate([real, imag], axis=0))
        out = dot(table_y_ref[...], jnp.concatenate([high, low, high], axis=0))
        planes_ref[2 * pair] = out[:, 0:128]
        planes_ref[2 * pair + 1] = out[:, 128:256]


def gathered_place(count, distance):
    place, size = 0, 1
    for bits in gather_rounds(count):
        for bit in bits:
            place = place + size * ((distance >> bit) & 1)
            size *= 2
    return place


def spectrum_kernel(update, count, order, lists, blend, cell_row, near, far, table, turns, table_y_ref, out_ref, flat, tap_lines, spread, planes):
    own = lax.axis_index("blk")
    half = count // 2
    view = order[:, update : update + 1]
    chosen = jnp.where(lax.broadcasted_iota(jnp.int32, (1, VIEWS), 1) == view, 1.0, 0.0)
    numbers = lax.broadcasted_iota(jnp.int32, (1, count), 1)
    rows = slice(CELLROWS * update, CELLROWS * (update + 1))
    lines, weights = [], []
    for k in range(2):
        listed = jnp.sum(lists[0, k : k + 1, :].astype(F32) * chosen, axis=1, keepdims=True)
        owners = jnp.where(numbers == listed.astype(jnp.int32), cell_row[...].astype(F32), 0.0)
        place = gathered_place(count, jnp.sum(owners).astype(jnp.int32) ^ own)
        inner = lax.rem(place, half)
        line = jnp.where(place < half, near[inner].astype(F32), far[inner].astype(F32))[rows]
        lines.append(line)
        weights.append(jnp.sum(blend[0, k : k + 1, :] * chosen, axis=1, keepdims=True))
    total = (weights[0] + weights[1]) * (float(PAD**3) / 2.0)
    value = lines[0] * (weights[0] / (total * jnp.sum(lines[0], keepdims=True)))
    value = value + lines[1] * (weights[1] / (total * jnp.sum(lines[1], keepdims=True)))
    flat[...] = value
    tap_stage(flat, tap_lines, spread, table, turns, table_y_ref, planes)
    z_stage(planes, out_ref)


def grid_bits(count):
    low_count = count.bit_length() - 2
    bits = [[bit for bit in range(low_count) if bit % 3 == axis] for axis in range(3)]
    bits[2] = [low_count] + bits[2]
    return bits


def gather_rounds(count):
    axes = grid_bits(count)
    bits = axes[2][:2] + axes[1][:1] + axes[0][1:2]
    bits += [bit for bit in range(1, count.bit_length() - 1) if bit not in bits]
    rounds = []
    while bits:
        rounds.append(bits[:2])
        bits = bits[2:]
    return rounds + [[0]]


def riders(count):
    axes = grid_bits(count)
    found = {1: (0, 0)}
    if axes[1]:
        found[1 << axes[1][0]] = (1, 0)
    found[1 << axes[2][0]] = (2, 0)
    if len(axes[0]) == 2:
        found[1 << axes[0][1]] = (0, 1)
    return found


def odd_places(count):
    own = lax.axis_index("blk")
    return [((own >> bits[0]) & 1) == 1 if bits else own < 0 for bits in grid_bits(count)]


def slab_kinds(count):
    kinds = [(1, 0), (2, 0), (2, 1), (0, 1), (0, 0), (1, 1)]
    return [kind for kind in kinds if len(grid_bits(count)[kind[0]]) > kind[1]]


def store_slabs(count, slabs, outs):
    odds = odd_places(count)
    for (axis, far), out in zip(slab_kinds(count), outs):
        low, high = slabs[axis]
        out[...] = jnp.where(odds[axis], high, low) if far else jnp.where(odds[axis], low, high)


def start_kernel(count, order, cells, est, u_out, cells_out, *refs):
    outs, (view, got, pad, flat, sems) = refs[:-5], refs[-5:]
    copies = []
    for number, (source, target) in enumerate(((est, flat), (cells, got), (order, view))):
        copies.append(pltpu.make_async_copy(source, target, sems.at[number]))
        copies[-1].start()
    copies[0].wait()
    unflatten(lambda row: flat[pl.ds(row, 8, stride=3), :], u_out)
    store_slabs(count, pack_slabs(u_out), outs)
    copies[1].wait()
    copies[2].wait()
    pad[...] = jnp.zeros((1, CELLROWS * 128), F32)
    for update in range(UPDATES):
        now = view[:, update : update + 1]
        value = None
        for number in range(VIEWS):
            part = got[number] * jnp.where(now == number, 1.0, 0.0)
            value = part if value is None else value + part
        pad[:, 0:KS3] = value
        wide = pad[...]
        rows = [wide[:, 128 * row : 128 * (row + 1)] for row in range(CELLROWS)]
        here = slice(CELLROWS * update, CELLROWS * (update + 1))
        cells_out[here, :] = jnp.concatenate(rows, axis=0).astype(BF16)


VIEW_PARTS = 9


def views_kernel(order, observed, o0, o1, held, near, wide, sems):
    asked = pltpu.make_async_copy(order, held, sems.at[VIEW_PARTS])
    asked.start()
    part_rows = FLAT // VIEW_PARTS
    copies = []
    for part in range(VIEW_PARTS):
        here = pl.ds(part_rows * 128 * part, part_rows * 128)
        copies.append(pltpu.make_async_copy(observed.at[:, :, here], near.at[:, :, here], sems.at[part]))
        copies[-1].start()
    step_rows = 32
    for part in range(VIEW_PARTS):
        copies[part].wait()

        @pl.loop(0, part_rows // step_rows)
        def _(step):
            first = part * part_rows + step * step_rows
            lanes = pl.ds(pl.multiple_of(first * 128, 128), step_rows * 128)
            value = near[0, :, lanes].astype(F32)
            value = jnp.concatenate([value, value[0 : 8 - VIEWS]], axis=0)
            for row in range(step_rows):
                rows = pl.ds(pl.multiple_of((first + row) * 8, 8), 8)
                wide[rows, :] = value[:, 128 * row : 128 * (row + 1)]

    asked.wait()
    for update, out in enumerate((o0, o1)):
        view = jnp.sum(held[:, update : update + 1].astype(F32)).astype(jnp.int32)
        unflatten(lambda row: wide[pl.ds(8 * row + view, 8, stride=24), :], out)


def field_stage(count, present, u, slabs, ea, gy, out, high, low, lines):
    found = {kind: slab[...] for kind, slab in zip(slab_kinds(count), slabs)}
    margins = []
    for axis in range(3):
        blank = jnp.zeros(SLABS[axis].shape, BF16)
        margins.append((found.get((axis, 0), blank), found.get((axis, 1), blank)))
    assemble(present, odd_places(count), u, margins, high, low)
    lines_stage(high, low, ea, lines, SLOTS * PAD, 256)
    y_stage(lines, gy, PAD, out)


def wide_terms(value):
    high, low = split(value)
    return jnp.concatenate([high, low, high], axis=1)


STEP = 192


def update_body(tissue, kernel, u, o, tables, planes, lines, new_ref):
    ea, ei, gh, gb, twiddle = tables
    filter_stage(planes, kernel, twiddle, False, planes)
    y_back_stage(planes, gb, lines)
    lane = lane_iota((STEP, LANES))
    valid = (lane % PAD < E) & (lane < 3 * PAD)
    for start in range(0, SLOTS * E, STEP):
        rows = slice(start, start + STEP)
        blurred = dot(wide_terms(lines[rows, :]), ei[...])
        quotient = jnp.where(valid, both_halves(o, rows) / blurred, 0.0)
        lines[rows, :] = dot(wide_terms(quotient), ea[...])
    y_stage(lines, gh, E, planes)
    filter_stage(planes, kernel, twiddle, True, planes)
    y_back_stage(planes, gb, lines)
    alive = jnp.broadcast_to(tissue[...], (STEP, 128)) > 0
    for start in range(0, SLOTS * E, STEP):
        rows = slice(start, start + STEP)
        correction = dot(wide_terms(lines[rows, :]), ei[...])
        for half in range(2):
            core = u[half, rows, :]
            new_ref[half, rows, :] = jnp.where(alive, core * correction[:, 128 * half : 128 * (half + 1)], core)


def first_kernel(count, tissue, present, u, *refs):
    kinds = len(slab_kinds(count))
    slabs, (kernel, o, ea, gy, ei, gh, gb, twiddle, u_out), outs = refs[:kinds], refs[kinds : kinds + 9], refs[kinds + 9 : -4]
    planes, high, low, lines = refs[-4:]
    field_stage(count, present, u, slabs, ea, gy, planes, high, low, lines)
    update_body(tissue, kernel, u, o, (ea, ei, gh, gb, twiddle), planes, lines, u_out)
    store_slabs(count, pack_slabs(u_out), outs)


def last_kernel(count, tissue, present, u, *refs):
    kinds = len(slab_kinds(count))
    slabs, (kernel, o, ea, gy, ei, gh, gb, twiddle, out) = refs[:kinds], refs[kinds : kinds + 9]
    planes, high, low, lines, fresh = refs[-5:]
    field_stage(count, present, u, slabs, ea, gy, planes, high, low, lines)
    update_body(tissue, kernel, u, o, (ea, ei, gh, gb, twiddle), planes, lines, fresh)
    flatten(fresh, out)


VM = pl.BlockSpec(memory_space=pltpu.VMEM)
SM = pl.BlockSpec(memory_space=pltpu.SMEM)
ANY = pl.BlockSpec(memory_space=pl.ANY)
HBM = pl.BlockSpec(memory_space=pltpu.HBM)
PARAMS = pltpu.CompilerParams(vmem_limit_bytes=48 * 1024 * 1024)


def shape(dims, kind=F32):
    return jax.ShapeDtypeStruct(dims, kind)


SLAB = shape((144, 128), BF16)
WIDE_SLAB = shape((256, 128), BF16)
SLABS = [SLAB, WIDE_SLAB, SLAB]
CELLS = shape((UPDATES * CELLROWS, 128), BF16)
ROWS = shape((2, SLOTS * E, 128))
ROWS_V = pltpu.VMEM((2, SLOTS * E, 128), F32)
PLANES = shape((SLOTS, 128, 128))
PLANES_V = pltpu.VMEM((SLOTS, 128, 128), F32)
LINES_V = pltpu.VMEM((SLOTS * PAD, LANES), F32)
TERMS_V = pltpu.VMEM((SLOTS * PAD, LANES), BF16)


def call(body, ins, outs, args, scratch=(), name=None):
    many = isinstance(outs, list)
    return pl.pallas_call(
        body,
        in_specs=ins,
        out_specs=[VM] * len(outs) if many else VM,
        out_shape=outs,
        scratch_shapes=list(scratch),
        compiler_params=PARAMS,
        name=name,
    )(*args)


def far_pairs(count, axis):
    bits = grid_bits(count)[axis]
    extent = 2 ** len(bits)
    pairs = []
    for number in range(count):
        at = sum(((number >> bit) & 1) << level for level, bit in enumerate(bits))
        moved = at + 1 if at % 2 else at - 1
        other = number
        if 0 <= moved < extent:
            for level, bit in enumerate(bits):
                other = other & ~(1 << bit) | ((moved >> level) & 1) << bit
        else:
            other = number ^ (1 if axis else 2)
        pairs.append((number, other))
    return pairs


def swap(value, distance, count):
    return lax.ppermute(value, "blk", [(number, number ^ distance) for number in range(count)])


def swap_slab(kind, slab, count):
    axis, far = kind
    if far:
        return lax.ppermute(slab, "blk", far_pairs(count, axis))
    return swap(slab, 1 << grid_bits(count)[axis][0], count)


def swap_slabs(slabs, count):
    return [swap_slab(kind, slab, count) for kind, slab in zip(slab_kinds(count), slabs)]


def local(estimate, observed, psf_cells, tissue, neighbours, psf_list, psf_blend, cell_row, view_order):
    count = lax.axis_size("blk")
    ea = jnp.asarray(stacked(table_space_to_lines(), 0))
    ei = jnp.asarray(stacked(table_lines_to_space(), 0))
    gy = jnp.asarray(stacked(table_y(PAD), 1))
    gh = jnp.asarray(stacked(table_y(E), 1))
    gb = jnp.asarray(stacked(table_y_back(), 1))
    gt = jnp.asarray(stacked(table_y_taps(), 1))
    taps = jnp.asarray(table_taps())
    turns = jnp.asarray(table_tap_turns())
    twiddle = jnp.asarray(table_twiddle())
    lists = jnp.swapaxes(psf_list, 1, 2)
    blend = jnp.swapaxes(psf_blend, 1, 2)

    slab_shapes = [SLABS[axis] for axis, far in slab_kinds(count)]
    rows, cells, *slabs = call(
        functools.partial(start_kernel, count),
        [HBM, HBM, HBM],
        [ROWS, CELLS] + slab_shapes,
        (
            pltpu.with_memory_space_constraint(view_order.reshape(1, VIEWS), pltpu.HBM),
            pltpu.with_memory_space_constraint(jnp.swapaxes(psf_cells, 0, 1), pltpu.HBM),
            pltpu.with_memory_space_constraint(estimate.reshape(FLAT, 128), pltpu.HBM),
        ),
        [
            pltpu.VMEM((1, VIEWS), jnp.int32),
            pltpu.VMEM((VIEWS, 1, KS3), F32),
            pltpu.VMEM((1, CELLROWS * 128), F32),
            pltpu.VMEM((FLAT, 128), F32),
            pltpu.SemaphoreType.DMA((3,)),
        ],
        name="start",
    )
    targets = call(
        views_kernel,
        [HBM, HBM],
        [ROWS, ROWS],
        (
            pltpu.with_memory_space_constraint(view_order.reshape(1, VIEWS), pltpu.HBM),
            pltpu.with_memory_space_constraint(observed, pltpu.HBM),
        ),
        [
            pltpu.VMEM((1, VIEWS), jnp.int32),
            pltpu.VMEM((1, VIEWS, FLAT * 128), BF16),
            pltpu.VMEM((8 * FLAT, 128), F32),
            pltpu.SemaphoreType.DMA((VIEW_PARTS + 1,)),
        ],
        name="views",
    )
    slabs = dict(zip(slab_kinds(count), slabs))
    riding = riders(count)
    margins = {}
    held = cells
    for number, bits in enumerate(gather_rounds(count)):
        arrived = [held]
        size = held.shape[0]
        for part in range(1, 2 ** len(bits)):
            distance = sum(((part >> level) & 1) << bit for level, bit in enumerate(bits))
            load = [held]
            kind = riding.get(distance)
            if kind is not None:
                load.append(slabs[kind])
            if distance == 1 and (0, 1) in margins:
                load.append(margins[0, 1])
            got = swap(jnp.concatenate(load, axis=0) if len(load) > 1 else held, distance, count)
            arrived.append(got[:size])
            if kind is not None:
                margins[kind] = got[size : size + slabs[kind].shape[0]]
            if distance == 1 and (0, 1) in margins:
                margins[0, 1] = got[got.shape[0] - SLAB.shape[0] :]
        if number == 0:
            sides = {kind: slab for kind, slab in slabs.items() if kind not in riding.values()}
            arrived, targets, sides = lax.optimization_barrier((arrived, targets, sides))
        if number == 1:
            sides = {kind: swap_slab(kind, slab, count) for kind, slab in sides.items()}
            arrived, sides = lax.optimization_barrier((arrived, sides))
            margins.update(sides)
        if bits != [0]:
            held = jnp.concatenate(arrived, axis=0)
    other = arrived[1]
    margins = [margins[kind] for kind in slab_kinds(count)]
    near_cells, far_cells = [v.reshape(count // 2, UPDATES * CELLROWS, 128) for v in (held, other)]

    def spectrum(update):
        return call(
            functools.partial(spectrum_kernel, update, count),
            [VM] * 9,
            PLANES,
            (view_order.reshape(1, VIEWS), lists, blend, cell_row.reshape(1, count), near_cells, far_cells, taps, turns, gt),
            [
                pltpu.VMEM((CELLROWS, 128), F32),
                pltpu.VMEM((3, TAPS, 128), F32),
                pltpu.VMEM((TAPS * TAPS, 128), F32),
                PLANES_V,
            ],
            name="spectrum",
        )

    def update(body, outs, number, kernel, rows, margins, scratch, name):
        return call(
            functools.partial(body, count),
            [VM] * (11 + len(slab_shapes)),
            outs,
            (tissue.reshape(1, 1), neighbours, rows, *margins, kernel, targets[number], ea, gy, ei, gh, gb, twiddle),
            [PLANES_V, TERMS_V, TERMS_V, LINES_V] + scratch,
            name=name,
        )

    kernel = spectrum(0)
    kernel, margins = lax.optimization_barrier((kernel, margins))
    rows, *slabs = update(first_kernel, [ROWS] + slab_shapes, 0, kernel, rows, margins, [], "first")
    margins = swap_slabs(slabs, count)
    kernel = spectrum(1)
    kernel, margins = lax.optimization_barrier((kernel, margins))
    out = update(last_kernel, shape((FLAT, 128)), 1, kernel, rows, margins, [ROWS_V], "last")
    return out.reshape(1, FLAT * 128)


def solution(mesh):
    return jax.shard_map(
        local,
        mesh=mesh,
        in_specs=(
            P("blk", None),
            P("blk", None, None),
            P("blk", None, None),
            P("blk"),
            P("blk", None),
            P("blk", None, None),
            P("blk", None, None),
            P(),
            P(),
        ),
        out_specs=P("blk", None),
        check_vma=False,
    )
```

```python
import functools

import numpy as np

import jax
import jax.numpy as jnp
import ml_dtypes
from jax import lax
from jax.experimental import pallas as pl
from jax.experimental.pallas import tpu as pltpu
from jax.sharding import PartitionSpec as P

E = 48
MARGIN = 8
UPDATES = 2
VIEWS = 6
PAD = 64
KS = 17
KS2 = KS * KS
KS3 = 4913
SLOTS = 16
LANES = 256
TAPS = 24
CELLROWS = 40
FLAT = 864

F32 = jnp.float32
BF16 = jnp.bfloat16


def two_terms(table):
    high = table.astype(ml_dtypes.bfloat16)
    low = (table - high.astype(np.float64)).astype(ml_dtypes.bfloat16)
    return high, low


def stacked(table, axis):
    high, low = two_terms(table)
    return np.concatenate([high, high, low], axis=axis)


def x_positions():
    x = np.arange(PAD)
    return np.where(x < PAD - MARGIN, x, x - PAD)


def table_space_to_lines():
    z4, k4, kx = np.arange(4), np.arange(4), np.arange(32)
    angle = -2.0 * np.pi * (
        z4[:, None, None, None] * k4[None, None, :, None] / 4.0
        + (kx[None, None, None, :] + 0.5) * x_positions()[None, :, None, None] / PAD
    )
    angle = angle.reshape(LANES, 128)
    return np.concatenate([np.cos(angle), np.sin(angle)], axis=1)


def table_lines_to_space():
    back = table_space_to_lines().T.copy()
    back = back.reshape(LANES, 4, PAD)
    back[:, 3, :] = 0.0
    back[:, :, E:] = 0.0
    return back.reshape(LANES, LANES)


def complex_rows(angle):
    cosine, sine = np.cos(angle), np.sin(angle)
    return np.concatenate(
        [np.concatenate([cosine, -sine], axis=1), np.concatenate([sine, cosine], axis=1)], axis=0
    )


def table_y(count):
    ky, y = np.arange(PAD), np.arange(count)
    return complex_rows(-2.0 * np.pi * (ky[:, None] * y[None, :] % PAD) / PAD)


def table_y_back():
    ky, y = np.arange(PAD), np.arange(E)
    return complex_rows(2.0 * np.pi * (y[:, None] * ky[None, :] % PAD) / PAD)


def table_y_taps():
    ky, tap = np.arange(PAD), np.arange(TAPS) - MARGIN
    angle = -2.0 * np.pi * ky[:, None] * tap[None, :] / PAD
    return complex_rows(angle)


def table_taps():
    kx, tap = np.arange(32), np.arange(KS) - MARGIN
    angle = -2.0 * np.pi * (kx[None, :] + 0.5) * tap[:, None] / PAD
    full = np.concatenate([np.tile(np.cos(angle), (1, 4)), np.tile(np.sin(angle), (1, 4))], axis=1)
    high, low = two_terms(full)
    table = np.zeros((128, LANES), ml_dtypes.bfloat16)
    for start, term in ((0, high), (32, high), (64, low)):
        table[start : start + KS] = term
    return table


def table_tap_turns():
    k4 = np.repeat(np.arange(4), 32)
    tap = np.arange(KS) - MARGIN
    angle = -2.0 * np.pi * tap[:, None] * k4[None, :] / PAD
    both = np.stack([np.cos(angle), np.sin(angle)], axis=0)
    return np.broadcast_to(both[:, :, None, :], (2, KS, 8, 128)).astype(np.float32)


def table_twiddle():
    k4 = np.repeat(np.arange(4), 32)
    angle = -2.0 * np.pi * np.arange(SLOTS)[:, None] * k4[None, :] / PAD
    both = np.stack([np.cos(angle), np.sin(angle)], axis=0)
    return np.broadcast_to(both[:, :, None, :], (2, SLOTS, 8, 128)).astype(np.float32)


def split(value):
    high = value.astype(BF16)
    low = (value - high.astype(F32)).astype(BF16)
    return high, low


def dot(left, right):
    return jnp.dot(left, right, preferred_element_type=F32)


def both_halves(rows_ref, rows):
    return jnp.concatenate([rows_ref[0, rows, :], rows_ref[1, rows, :]], axis=1)


def lane_iota(shape):
    return lax.broadcasted_iota(jnp.int32, shape, 1)


def cut(pieces, piece, target):
    offset = E * piece
    first, start = offset // 128, offset % 128
    shift = (target - start) % 128
    one = pltpu.roll(pieces[first], shift, 1) if shift else pieces[first]
    if start + E <= 128:
        return one
    two = pltpu.roll(pieces[first + 1], shift, 1) if shift else pieces[first + 1]
    edge = target + 128 - start
    return jnp.where(lane_iota(one.shape) < edge, one, two)


def unflatten(load, out_ref):
    lane = lane_iota((8, 128))
    zero = jnp.zeros((8, 128), F32)
    for block in range(12):
        parts = []
        for z4 in range(3):
            first = 3 * (96 * z4 + 8 * block)
            parts.append([load(first + m) for m in range(3)])
        for piece in range(8):
            low = cut(parts[0], piece, 0)
            mid = cut(parts[1], piece, 64)
            top = cut(parts[2], piece, 0)
            left = jnp.where(lane < E, low, jnp.where(lane < 64, zero, mid))
            left = jnp.where(lane < 64 + E, left, zero)
            rows = pl.ds(64 * block + piece, 8, stride=8)
            out_ref[0, rows, :] = left
            out_ref[1, rows, :] = jnp.where(lane < E, top, zero)


def flatten(rows_ref, flat_ref):
    lane = lane_iota((8, 128))
    for block in range(12):
        found = []
        for piece in range(8):
            rows = pl.ds(64 * block + piece, 8, stride=8)
            found.append((rows_ref[0, rows, :], rows_ref[1, rows, :]))
        for z4 in range(3):
            first = 3 * (96 * z4 + 8 * block)
            out = [None, None, None]
            for piece in range(8):
                value = found[piece][0] if z4 < 2 else found[piece][1]
                source = 64 if z4 == 1 else 0
                offset = E * piece
                spot, start = offset // 128, offset % 128
                shift = (start - source) % 128
                moved = pltpu.roll(value, shift, 1) if shift else value
                if out[spot] is None:
                    out[spot] = moved
                else:
                    out[spot] = jnp.where(lane < start, out[spot], moved)
                if start + E > 128:
                    out[spot + 1] = moved
            for m in range(3):
                flat_ref[pl.ds(first + m, 8, stride=3), :] = out[m]


def squeeze(pieces):
    out = [None, None, None]
    for piece, value in enumerate(pieces):
        spot, start = E * piece // 128, E * piece % 128
        moved = pltpu.roll(value, start, 1) if start else value
        out[spot] = moved if out[spot] is None else jnp.where(lane_iota(moved.shape) < start, out[spot], moved)
        if start + E > 128:
            out[spot + 1] = moved
    return out


def stretch(full):
    return [cut(full, piece, 0) for piece in range(8)]


def pack_x_side(value):
    last = value[144:192]
    lane = lane_iota(last.shape)
    out = []
    for part in range(3):
        moved = pltpu.roll(last, (96 - 32 * part) % 128, 1)
        out.append(jnp.where(lane < 96, value[48 * part : 48 * (part + 1)], moved))
    return jnp.concatenate(out, axis=0)


def unpack_x_side(value):
    parts = [value[48 * part : 48 * (part + 1)] for part in range(3)]
    lane = lane_iota(parts[0].shape)
    last = pltpu.roll(parts[0], 32, 1)
    for part in range(1, 3):
        last = jnp.where(lane < 32 * part, last, pltpu.roll(parts[part], (32 + 32 * part) % 128, 1))
    return jnp.concatenate(parts + [last], axis=0)


def pack_z_side(blocks):
    return jnp.concatenate(squeeze(blocks), axis=0)


def unpack_z_side(value):
    return stretch([value[48 * part : 48 * (part + 1)] for part in range(3)])


def x_picks(wide, packed, low_start, high_start):
    place = packed % 128
    start = jnp.where(packed >= 128, high_start, low_start)
    here = (wide // PAD == place // MARGIN) & (wide % PAD == start + place % MARGIN) & (place < 3 * MARGIN)
    return jnp.where(here, 1.0, 0.0).astype(BF16)


def both_iotas():
    dims = (LANES, LANES)
    return lax.broadcasted_iota(jnp.int32, dims, 0), lax.broadcasted_iota(jnp.int32, dims, 1)


def pack_slabs(rows_ref):
    high = both_halves(rows_ref, slice(None)).astype(BF16)
    rows, columns = both_iotas()
    found = dot(high, x_picks(rows, columns, 0, E - MARGIN))
    faces = []
    for face in range(2):
        value = found[0:192, 128 * face : 128 * (face + 1)]
        for group in range(1, 4):
            part = found[192 * group : 192 * (group + 1), 128 * face : 128 * (face + 1)]
            value = value + pltpu.roll(part, 3 * MARGIN * group, 1)
        faces.append(pack_x_side(value).astype(BF16))
    x0, x1 = faces
    low_rows, high_rows = [], []
    for slot in range(SLOTS):
        low_rows.append(both_halves(rows_ref, slice(E * slot, E * slot + MARGIN)))
        high_rows.append(both_halves(rows_ref, slice(E * slot + E - MARGIN, E * (slot + 1))))
    y0, y1 = jnp.concatenate(low_rows, axis=0), jnp.concatenate(high_rows, axis=0)
    y0, y1 = [jnp.concatenate([v[:, 0:128], v[:, 128:256]], axis=0).astype(BF16) for v in (y0, y1)]
    z0 = pack_z_side([rows_ref[0, E * slot : E * (slot + 1), :] for slot in range(MARGIN)]).astype(BF16)
    z1 = pack_z_side([rows_ref[1, E * slot : E * (slot + 1), :] for slot in range(MARGIN, SLOTS)]).astype(BF16)
    return (z0, z1), (y0, y1), (x0, x1)


def sort_margins(present, odd, axis, pair):
    on = jnp.where(present[...] >= 0, 1.0, 0.0)
    pair = [value.astype(F32) for value in pair]
    low = jnp.where(odd, pair[0], pair[1])
    high = jnp.where(odd, pair[1], pair[0])
    return low * on[:, 2 * axis : 2 * axis + 1], high * on[:, 2 * axis + 1 : 2 * axis + 2]


def assemble(present, odds, rows_ref, margins, high_ref, low_ref):
    (zm, zp), (ym, yp), (xm, xp) = [
        sort_margins(present, odds[axis], axis, margins[axis]) for axis in range(3)
    ]
    rows, columns = both_iotas()
    picks = x_picks(columns, rows, PAD - MARGIN, E)
    sides = [unpack_x_side(v) for v in (xm, xp)]
    parts = []
    for group in range(4):
        pair = [pltpu.roll(v, 128 - 3 * MARGIN * group, 1) if group else v for v in sides]
        parts.append(jnp.concatenate(pair, axis=1))
    side = dot(jnp.concatenate(parts, axis=0).astype(BF16), picks)
    ym_rows, yp_rows = [jnp.concatenate([v[0:128], v[128:256]], axis=1) for v in (ym, yp)]
    z_sides = [pltpu.roll(v, 64, 1) for value in (zp, zm) for v in unpack_z_side(value)]
    lane = lane_iota((E, 128))
    for slot in range(SLOTS):
        core = both_halves(rows_ref, slice(E * slot, E * (slot + 1)))
        high, low = split(core)
        added = side[E * slot : E * (slot + 1)]
        full = high.astype(F32) + added
        right = jnp.where(lane < 64, full[:, 128:256], jnp.where(lane < 64 + E, z_sides[slot], 0.0))
        high_ref[PAD * slot : PAD * slot + E, 0:128] = full[:, 0:128].astype(BF16)
        high_ref[PAD * slot : PAD * slot + E, 128:256] = right.astype(BF16)
        rows = slice(MARGIN * slot, MARGIN * (slot + 1))
        outer = jnp.concatenate([yp_rows[rows], ym_rows[rows]], axis=0)
        high_ref[PAD * slot + E : PAD * (slot + 1), :] = outer.astype(BF16)
        low_ref[PAD * slot : PAD * slot + E, :] = low
        low_ref[PAD * slot + E : PAD * (slot + 1), :] = jnp.zeros((PAD - E, LANES), BF16)


def lines_stage(high, low, table, out_ref, rows, step):
    for start in range(0, rows, step):
        part = slice(start, start + step)
        wide = jnp.concatenate([high[part, :], low[part, :], high[part, :]], axis=1)
        out_ref[part, :] = dot(wide, table[...])


def y_stage(lines_ref, table, count, out_ref):
    for pair in range(SLOTS // 2):
        one = lines_ref[count * 2 * pair : count * (2 * pair + 1), :]
        two = lines_ref[count * (2 * pair + 1) : count * (2 * pair + 2), :]
        real = jnp.concatenate([one[:, 0:128], two[:, 0:128]], axis=1)
        imag = jnp.concatenate([one[:, 128:256], two[:, 128:256]], axis=1)
        high, low = split(jnp.concatenate([real, imag], axis=0))
        out = dot(table[...], jnp.concatenate([high, low, high], axis=0))
        out_ref[2 * pair] = out[:, 0:128]
        out_ref[2 * pair + 1] = out[:, 128:256]


def y_back_stage(planes_ref, table, out_ref):
    for pair in range(SLOTS // 2):
        both = jnp.concatenate([planes_ref[2 * pair], planes_ref[2 * pair + 1]], axis=1)
        high, low = split(both)
        out = dot(table[...], jnp.concatenate([high, low, high], axis=0))
        for which in range(2):
            rows = slice(E * (2 * pair + which), E * (2 * pair + which + 1))
            lanes = slice(128 * which, 128 * (which + 1))
            out_ref[rows, 0:128] = out[0:E, lanes]
            out_ref[rows, 128:256] = out[E : 2 * E, lanes]


def turn(value, cosine, sine):
    real, imag = value
    return real * cosine - imag * sine, real * sine + imag * cosine


def dft4(values, sign):
    (ar, ai), (br, bi), (cr, ci), (dr, di) = values
    sr, si, mr, mi = ar + cr, ai + ci, ar - cr, ai - ci
    pr, pi, qr, qi = br + dr, bi + di, br - dr, bi - di
    if sign > 0:
        first, third = (mr - qi, mi + qr), (mr + qi, mi - qr)
    else:
        first, third = (mr + qi, mi - qr), (mr - qi, mi + qr)
    return [(sr + pr, si + pi), first, (sr - pr, si - pi), third]


def dft16(values, sign):
    inner = []
    for low in range(4):
        line = dft4([values[4 * top + low] for top in range(4)], sign)
        moved = []
        for k in range(4):
            turns = low * k
            real, imag = line[k]
            if turns == 0:
                moved.append((real, imag))
            elif turns == 4:
                moved.append((-imag, real) if sign > 0 else (imag, -real))
            elif turns in (2, 6):
                root = float(np.sqrt(0.5))
                a, b = root * real, root * imag
                if turns == 2:
                    moved.append((a - b, a + b) if sign > 0 else (a + b, b - a))
                else:
                    moved.append((-a - b, a - b) if sign > 0 else (b - a, -a - b))
            else:
                angle = sign * 2.0 * np.pi * turns / SLOTS
                moved.append(turn((real, imag), float(np.cos(angle)), float(np.sin(angle))))
        inner.append(moved)
    out = [None] * SLOTS
    for k in range(4):
        line = dft4([inner[low][k] for low in range(4)], sign)
        for top in range(4):
            out[k + 4 * top] = line[top]
    return out


def z_forward(planes_ref, twiddle, rows, rows_imag):
    values = []
    for slot in range(SLOTS):
        value = (planes_ref[slot, rows, :], planes_ref[slot, rows_imag, :])
        if slot:
            value = turn(value, twiddle[0, slot], twiddle[1, slot])
        values.append(value)
    return dft16(values, -1)


def z_stage(planes_ref, out_ref):
    @pl.loop(0, PAD // 8, unroll=2)
    def _(step):
        rows = pl.ds(pl.multiple_of(8 * step, 8), 8)
        rows_imag = pl.ds(pl.multiple_of(8 * step + PAD, 8), 8)
        values = [(planes_ref[slot, rows, :], planes_ref[slot, rows_imag, :]) for slot in range(SLOTS)]
        values = dft16(values, -1)
        for slot in range(SLOTS):
            out_ref[slot, rows, :] = values[slot][0]
            out_ref[slot, rows_imag, :] = values[slot][1]


def filter_stage(planes_ref, kernel_ref, twiddle, conjugate, out_ref):
    @pl.loop(0, PAD // 8, unroll=2)
    def _(step):
        rows = pl.ds(pl.multiple_of(8 * step, 8), 8)
        rows_imag = pl.ds(pl.multiple_of(8 * step + PAD, 8), 8)
        values = z_forward(planes_ref, twiddle, rows, rows_imag)
        for slot in range(SLOTS):
            cosine, sine = kernel_ref[slot, rows, :], kernel_ref[slot, rows_imag, :]
            if conjugate:
                real, imag = values[slot]
                values[slot] = (real * cosine + imag * sine, imag * cosine - real * sine)
            else:
                values[slot] = turn(values[slot], cosine, sine)
        values = dft16(values, 1)
        for slot in range(SLOTS):
            real, imag = values[slot]
            if slot:
                cosine, sine = twiddle[0, slot], twiddle[1, slot]
                real, imag = real * cosine + imag * sine, imag * cosine - real * sine
            out_ref[slot, rows, :] = real
            out_ref[slot, rows_imag, :] = imag


def tap_stage(flat_ref, lines, spread, table, turns, table_y_ref, planes_ref):
    lane = lane_iota((3, 128))
    for tap in range(KS):
        row, start = KS2 * tap // 128, KS2 * tap % 128
        value = flat_ref[row : row + 3, :]
        if start:
            value = pltpu.roll(value, 128 - start, 1)
            after = pltpu.roll(flat_ref[row + 1 : row + 4, :], 128 - start, 1)
            value = jnp.where(lane < 128 - start, value, after)
        for part in range(3):
            lines[part, tap : tap + 1, :] = value[part : part + 1]
    lane = lane_iota((TAPS, 128))
    for line in range(KS):
        part, start = KS * line // 128, KS * line % 128
        value = lines[part]
        if start:
            value = pltpu.roll(value, 128 - start, 1)
            if start + KS > 128:
                after = pltpu.roll(lines[part + 1], 128 - start, 1)
                value = jnp.where(lane < 128 - start, value, after)
        spread[TAPS * line : TAPS * (line + 1), :] = jnp.where(lane < KS, value, 0.0)
    for line in range(KS, TAPS):
        spread[TAPS * line : TAPS * (line + 1), :] = jnp.zeros((TAPS, 128), F32)
    rows = jnp.concatenate([spread[pl.ds(tap, TAPS, stride=TAPS), :] for tap in range(KS)], axis=0)
    high = rows.astype(BF16).astype(F32)
    low = rows - high
    wide = high + pltpu.roll(low, 32, 1) + pltpu.roll(high, 64, 1)
    out = dot(wide.astype(BF16), table[...])
    slots = [None] * SLOTS
    for tap in range(KS):
        part = out[TAPS * tap : TAPS * (tap + 1)]
        value = part[:, 0:128], part[:, 128:256]
        if tap != MARGIN:
            cosine, sine = [jnp.concatenate([turns[i, tap]] * 3, axis=0) for i in range(2)]
            value = turn(value, cosine, sine)
        slot = (tap - MARGIN) % SLOTS
        if slots[slot] is not None:
            value = value[0] + slots[slot][0], value[1] + slots[slot][1]
        slots[slot] = value
    for pair in range(SLOTS // 2):
        one, two = slots[2 * pair], slots[2 * pair + 1]
        real = jnp.concatenate([one[0], two[0]], axis=1)
        imag = jnp.concatenate([one[1], two[1]], axis=1)
        high, low = split(jnp.concatenate([real, imag], axis=0))
        out = dot(table_y_ref[...], jnp.concatenate([high, low, high], axis=0))
        planes_ref[2 * pair] = out[:, 0:128]
        planes_ref[2 * pair + 1] = out[:, 128:256]


def gathered_place(count, distance):
    place, size = 0, 1
    for bits in gather_rounds(count):
        for bit in bits:
            place = place + size * ((distance >> bit) & 1)
            size *= 2
    return place


def spectrum_kernel(update, count, order, lists, blend, cell_row, near, far, table, turns, table_y_ref, out_ref, flat, tap_lines, spread, planes):
    own = lax.axis_index("blk")
    half = count // 2
    view = order[:, update : update + 1]
    chosen = jnp.where(lax.broadcasted_iota(jnp.int32, (1, VIEWS), 1) == view, 1.0, 0.0)
    numbers = lax.broadcasted_iota(jnp.int32, (1, count), 1)
    rows = slice(CELLROWS * update, CELLROWS * (update + 1))
    lines, weights = [], []
    for k in range(2):
        listed = jnp.sum(lists[0, k : k + 1, :].astype(F32) * chosen, axis=1, keepdims=True)
        owners = jnp.where(numbers == listed.astype(jnp.int32), cell_row[...].astype(F32), 0.0)
        place = gathered_place(count, jnp.sum(owners).astype(jnp.int32) ^ own)
        inner = lax.rem(place, half)
        line = jnp.where(place < half, near[inner].astype(F32), far[inner].astype(F32))[rows]
        lines.append(line)
        weights.append(jnp.sum(blend[0, k : k + 1, :] * chosen, axis=1, keepdims=True))
    total = (weights[0] + weights[1]) * (float(PAD**3) / 2.0)
    value = lines[0] * (weights[0] / (total * jnp.sum(lines[0], keepdims=True)))
    value = value + lines[1] * (weights[1] / (total * jnp.sum(lines[1], keepdims=True)))
    flat[...] = value
    tap_stage(flat, tap_lines, spread, table, turns, table_y_ref, planes)
    z_stage(planes, out_ref)


def grid_bits(count):
    low_count = count.bit_length() - 2
    bits = [[bit for bit in range(low_count) if bit % 3 == axis] for axis in range(3)]
    bits[2] = [low_count] + bits[2]
    return bits


def gather_rounds(count):
    axes = grid_bits(count)
    bits = axes[2][:2] + axes[1][:1] + axes[0][1:2]
    bits += [bit for bit in range(1, count.bit_length() - 1) if bit not in bits]
    rounds = []
    while bits:
        rounds.append(bits[:2])
        bits = bits[2:]
    return rounds + [[0]]


def riders(count):
    axes = grid_bits(count)
    found = {1: (0, 0)}
    if axes[1]:
        found[1 << axes[1][0]] = (1, 0)
    found[1 << axes[2][0]] = (2, 0)
    if len(axes[0]) == 2:
        found[1 << axes[0][1]] = (0, 1)
    return found


def odd_places(count):
    own = lax.axis_index("blk")
    return [((own >> bits[0]) & 1) == 1 if bits else own < 0 for bits in grid_bits(count)]


def slab_kinds(count):
    kinds = [(1, 0), (2, 0), (2, 1), (0, 1), (0, 0), (1, 1)]
    return [kind for kind in kinds if len(grid_bits(count)[kind[0]]) > kind[1]]


def store_slabs(count, slabs, outs):
    odds = odd_places(count)
    for (axis, far), out in zip(slab_kinds(count), outs):
        low, high = slabs[axis]
        out[...] = jnp.where(odds[axis], high, low) if far else jnp.where(odds[axis], low, high)


def start_kernel(count, order, cells, est, u_out, cells_out, *refs):
    outs, (view, got, pad, flat, sems) = refs[:-5], refs[-5:]
    copies = []
    for number, (source, target) in enumerate(((est, flat), (cells, got), (order, view))):
        copies.append(pltpu.make_async_copy(source, target, sems.at[number]))
        copies[-1].start()
    copies[0].wait()
    unflatten(lambda row: flat[pl.ds(row, 8, stride=3), :], u_out)
    store_slabs(count, pack_slabs(u_out), outs)
    copies[1].wait()
    copies[2].wait()
    pad[...] = jnp.zeros((1, CELLROWS * 128), F32)
    rows = []
    for update in range(UPDATES):
        now = view[:, update : update + 1]
        value = None
        for number in range(VIEWS):
            part = got[number] * jnp.where(now == number, 1.0, 0.0)
            value = part if value is None else value + part
        pad[:, 0:KS3] = value
        wide = pad[...]
        rows += [wide[:, 128 * row : 128 * (row + 1)] for row in range(CELLROWS)]
    cells_out[...] = jnp.concatenate(rows, axis=0).astype(BF16)


VIEW_PARTS = 9


def views_kernel(order, observed, o0, o1, held, near, wide, sems):
    asked = pltpu.make_async_copy(order, held, sems.at[VIEW_PARTS])
    asked.start()
    part_rows = FLAT // VIEW_PARTS
    copies = []
    for part in range(VIEW_PARTS):
        here = pl.ds(part_rows * 128 * part, part_rows * 128)
        copies.append(pltpu.make_async_copy(observed.at[:, :, here], near.at[:, :, here], sems.at[part]))
        copies[-1].start()
    step_rows = 32
    for part in range(VIEW_PARTS):
        copies[part].wait()

        @pl.loop(0, part_rows // step_rows)
        def _(step):
            first = part * part_rows + step * step_rows
            lanes = pl.ds(pl.multiple_of(first * 128, 128), step_rows * 128)
            value = near[0, :, lanes].astype(F32)
            value = jnp.concatenate([value, value[0 : 8 - VIEWS]], axis=0)
            for row in range(step_rows):
                rows = pl.ds(pl.multiple_of((first + row) * 8, 8), 8)
                wide[rows, :] = value[:, 128 * row : 128 * (row + 1)]

    asked.wait()
    for update, out in enumerate((o0, o1)):
        view = jnp.sum(held[:, update : update + 1].astype(F32)).astype(jnp.int32)
        unflatten(lambda row: wide[pl.ds(8 * row + view, 8, stride=24), :], out)


def field_stage(count, present, u, slabs, ea, gy, out, high, low, lines):
    found = {kind: slab[...] for kind, slab in zip(slab_kinds(count), slabs)}
    margins = []
    for axis in range(3):
        blank = jnp.zeros(SLABS[axis].shape, BF16)
        margins.append((found.get((axis, 0), blank), found.get((axis, 1), blank)))
    assemble(present, odd_places(count), u, margins, high, low)
    lines_stage(high, low, ea, lines, SLOTS * PAD, 256)
    y_stage(lines, gy, PAD, out)


def wide_terms(value):
    high, low = split(value)
    return jnp.concatenate([high, low, high], axis=1)


STEP = 192


def update_body(tissue, kernel, u, o, tables, planes, lines, new_ref):
    ea, ei, gh, gb, twiddle = tables
    filter_stage(planes, kernel, twiddle, False, planes)
    y_back_stage(planes, gb, lines)
    lane = lane_iota((STEP, LANES))
    valid = (lane % PAD < E) & (lane < 3 * PAD)
    for start in range(0, SLOTS * E, STEP):
        rows = slice(start, start + STEP)
        blurred = dot(wide_terms(lines[rows, :]), ei[...])
        quotient = jnp.where(valid, both_halves(o, rows) / blurred, 0.0)
        lines[rows, :] = dot(wide_terms(quotient), ea[...])
    y_stage(lines, gh, E, planes)
    filter_stage(planes, kernel, twiddle, True, planes)
    y_back_stage(planes, gb, lines)
    alive = jnp.broadcast_to(tissue[...], (STEP, 128)) > 0
    for start in range(0, SLOTS * E, STEP):
        rows = slice(start, start + STEP)
        correction = dot(wide_terms(lines[rows, :]), ei[...])
        for half in range(2):
            core = u[half, rows, :]
            new_ref[half, rows, :] = jnp.where(alive, core * correction[:, 128 * half : 128 * (half + 1)], core)


def first_kernel(count, tissue, present, u, *refs):
    kinds = len(slab_kinds(count))
    slabs, (kernel, o, ea, gy, ei, gh, gb, twiddle, u_out), outs = refs[:kinds], refs[kinds : kinds + 9], refs[kinds + 9 : -4]
    planes, high, low, lines = refs[-4:]
    field_stage(count, present, u, slabs, ea, gy, planes, high, low, lines)
    update_body(tissue, kernel, u, o, (ea, ei, gh, gb, twiddle), planes, lines, u_out)
    store_slabs(count, pack_slabs(u_out), outs)


def last_kernel(count, tissue, present, u, *refs):
    kinds = len(slab_kinds(count))
    slabs, (kernel, o, ea, gy, ei, gh, gb, twiddle, out) = refs[:kinds], refs[kinds : kinds + 9]
    planes, high, low, lines, fresh = refs[-5:]
    field_stage(count, present, u, slabs, ea, gy, planes, high, low, lines)
    update_body(tissue, kernel, u, o, (ea, ei, gh, gb, twiddle), planes, lines, fresh)
    flatten(fresh, out)


VM = pl.BlockSpec(memory_space=pltpu.VMEM)
SM = pl.BlockSpec(memory_space=pltpu.SMEM)
ANY = pl.BlockSpec(memory_space=pl.ANY)
HBM = pl.BlockSpec(memory_space=pltpu.HBM)
PARAMS = pltpu.CompilerParams(vmem_limit_bytes=48 * 1024 * 1024)


def shape(dims, kind=F32):
    return jax.ShapeDtypeStruct(dims, kind)


SLAB = shape((144, 128), BF16)
WIDE_SLAB = shape((256, 128), BF16)
SLABS = [SLAB, WIDE_SLAB, SLAB]
CELLS = shape((UPDATES * CELLROWS, 128), BF16)
ROWS = shape((2, SLOTS * E, 128))
ROWS_V = pltpu.VMEM((2, SLOTS * E, 128), F32)
PLANES = shape((SLOTS, 128, 128))
PLANES_V = pltpu.VMEM((SLOTS, 128, 128), F32)
LINES_V = pltpu.VMEM((SLOTS * PAD, LANES), F32)
TERMS_V = pltpu.VMEM((SLOTS * PAD, LANES), BF16)


def call(body, ins, outs, args, scratch=(), name=None):
    many = isinstance(outs, list)
    return pl.pallas_call(
        body,
        in_specs=ins,
        out_specs=[VM] * len(outs) if many else VM,
        out_shape=outs,
        scratch_shapes=list(scratch),
        compiler_params=PARAMS,
        name=name,
    )(*args)


def far_pairs(count, axis):
    bits = grid_bits(count)[axis]
    extent = 2 ** len(bits)
    pairs = []
    for number in range(count):
        at = sum(((number >> bit) & 1) << level for level, bit in enumerate(bits))
        moved = at + 1 if at % 2 else at - 1
        other = number
        if 0 <= moved < extent:
            for level, bit in enumerate(bits):
                other = other & ~(1 << bit) | ((moved >> level) & 1) << bit
        else:
            other = number ^ (1 if axis else 2)
        pairs.append((number, other))
    return pairs


def swap(value, distance, count):
    return lax.ppermute(value, "blk", [(number, number ^ distance) for number in range(count)])


def swap_slab(kind, slab, count):
    axis, far = kind
    if far:
        return lax.ppermute(slab, "blk", far_pairs(count, axis))
    return swap(slab, 1 << grid_bits(count)[axis][0], count)


def swap_slabs(slabs, count):
    return [swap_slab(kind, slab, count) for kind, slab in zip(slab_kinds(count), slabs)]


def local(estimate, observed, psf_cells, tissue, neighbours, psf_list, psf_blend, cell_row, view_order):
    count = lax.axis_size("blk")
    ea = jnp.asarray(stacked(table_space_to_lines(), 0))
    ei = jnp.asarray(stacked(table_lines_to_space(), 0))
    gy = jnp.asarray(stacked(table_y(PAD), 1))
    gh = jnp.asarray(stacked(table_y(E), 1))
    gb = jnp.asarray(stacked(table_y_back(), 1))
    gt = jnp.asarray(stacked(table_y_taps(), 1))
    taps = jnp.asarray(table_taps())
    turns = jnp.asarray(table_tap_turns())
    twiddle = jnp.asarray(table_twiddle())
    lists = jnp.swapaxes(psf_list, 1, 2)
    blend = jnp.swapaxes(psf_blend, 1, 2)

    slab_shapes = [SLABS[axis] for axis, far in slab_kinds(count)]
    rows, cells, *slabs = call(
        functools.partial(start_kernel, count),
        [HBM, HBM, HBM],
        [ROWS, CELLS] + slab_shapes,
        (
            pltpu.with_memory_space_constraint(view_order.reshape(1, VIEWS), pltpu.HBM),
            pltpu.with_memory_space_constraint(jnp.swapaxes(psf_cells, 0, 1), pltpu.HBM),
            pltpu.with_memory_space_constraint(estimate.reshape(FLAT, 128), pltpu.HBM),
        ),
        [
            pltpu.VMEM((1, VIEWS), jnp.int32),
            pltpu.VMEM((VIEWS, 1, KS3), F32),
            pltpu.VMEM((1, CELLROWS * 128), F32),
            pltpu.VMEM((FLAT, 128), F32),
            pltpu.SemaphoreType.DMA((3,)),
        ],
        name="start",
    )
    targets = call(
        views_kernel,
        [HBM, HBM],
        [ROWS, ROWS],
        (
            pltpu.with_memory_space_constraint(view_order.reshape(1, VIEWS), pltpu.HBM),
            pltpu.with_memory_space_constraint(observed, pltpu.HBM),
        ),
        [
            pltpu.VMEM((1, VIEWS), jnp.int32),
            pltpu.VMEM((1, VIEWS, FLAT * 128), BF16),
            pltpu.VMEM((8 * FLAT, 128), F32),
            pltpu.SemaphoreType.DMA((VIEW_PARTS + 1,)),
        ],
        name="views",
    )
    slabs = dict(zip(slab_kinds(count), slabs))
    riding = riders(count)
    margins = {}
    held = cells
    for number, bits in enumerate(gather_rounds(count)):
        arrived = [held]
        size = held.shape[0]
        for part in range(1, 2 ** len(bits)):
            distance = sum(((part >> level) & 1) << bit for level, bit in enumerate(bits))
            load = [held]
            kind = riding.get(distance)
            if kind is not None:
                load.append(slabs[kind])
            if distance == 1 and (0, 1) in margins:
                load.append(margins[0, 1])
            got = swap(jnp.concatenate(load, axis=0) if len(load) > 1 else held, distance, count)
            arrived.append(got[:size])
            if kind is not None:
                margins[kind] = got[size : size + slabs[kind].shape[0]]
            if distance == 1 and (0, 1) in margins:
                margins[0, 1] = got[got.shape[0] - SLAB.shape[0] :]
        if number == 0:
            sides = {kind: slab for kind, slab in slabs.items() if kind not in riding.values()}
            arrived, targets, sides = lax.optimization_barrier((arrived, targets, sides))
        if number == 1:
            sides = {kind: swap_slab(kind, slab, count) for kind, slab in sides.items()}
            arrived, sides = lax.optimization_barrier((arrived, sides))
            margins.update(sides)
        if bits != [0]:
            held = jnp.concatenate(arrived, axis=0)
    other = arrived[1]
    margins = [margins[kind] for kind in slab_kinds(count)]
    near_cells, far_cells = [v.reshape(count // 2, UPDATES * CELLROWS, 128) for v in (held, other)]

    def spectrum(update):
        return call(
            functools.partial(spectrum_kernel, update, count),
            [VM] * 9,
            PLANES,
            (view_order.reshape(1, VIEWS), lists, blend, cell_row.reshape(1, count), near_cells, far_cells, taps, turns, gt),
            [
                pltpu.VMEM((CELLROWS, 128), F32),
                pltpu.VMEM((3, TAPS, 128), F32),
                pltpu.VMEM((TAPS * TAPS, 128), F32),
                PLANES_V,
            ],
            name="spectrum",
        )

    def update(body, outs, number, kernel, rows, margins, scratch, name):
        return call(
            functools.partial(body, count),
            [VM] * (11 + len(slab_shapes)),
            outs,
            (tissue.reshape(1, 1), neighbours, rows, *margins, kernel, targets[number], ea, gy, ei, gh, gb, twiddle),
            [PLANES_V, TERMS_V, TERMS_V, LINES_V] + scratch,
            name=name,
        )

    kernel = spectrum(0)
    kernel, margins = lax.optimization_barrier((kernel, margins))
    rows, *slabs = update(first_kernel, [ROWS] + slab_shapes, 0, kernel, rows, margins, [], "first")
    margins = swap_slabs(slabs, count)
    kernel = spectrum(1)
    kernel, margins = lax.optimization_barrier((kernel, margins))
    out = update(last_kernel, shape((FLAT, 128)), 1, kernel, rows, margins, [ROWS_V], "last")
    return out.reshape(1, FLAT * 128)


def solution(mesh):
    return jax.shard_map(
        local,
        mesh=mesh,
        in_specs=(
            P("blk", None),
            P("blk", None, None),
            P("blk", None, None),
            P("blk"),
            P("blk", None),
            P("blk", None, None),
            P("blk", None, None),
            P(),
            P(),
        ),
        out_specs=P("blk", None),
        check_vma=False,
    )
```
